32 devices in a mesh: fsdp: 8 (over y, x, core), rep: 4 (over z).
Axes of the slice: x: 2, y: 2, z: 4, core: 2. Of those that a mesh axis runs over, the one named last changes fastest.
Arguments:
- tokens: bfloat16 [64, 237, 768], P(('fsdp', 'rep')), may hold values from -6 to 6
- out_grad: bfloat16 [64, 237, 768], P(('fsdp', 'rep')), may hold values from -6 to 6
- masked: int32 [64, 40], P(('fsdp', 'rep')), may hold values from 0 to 1, as said below
- lengths: int32 [64], P(('fsdp', 'rep')), may hold values from 8 to 40, as said below
- mask_vec: bfloat16 [768], P('fsdp'), may hold values from -6 to 6
- norm1_gain: bfloat16 [768], P('fsdp'), may hold values from 0.099609375 to 1.8984375
- norm1_shift: bfloat16 [768], P('fsdp'), may hold values from -4 to 4
- w_qkv: bfloat16 [768, 2304], P('fsdp'), may hold values from -0.21875 to 0.21875
- query_bias: bfloat16 [768], P('fsdp'), may hold values from -4 to 4
- value_bias: bfloat16 [768], P('fsdp'), may hold values from -4 to 4
- w_out: bfloat16 [768, 768], P('fsdp'), may hold values from -0.875 to 0.875
- out_bias: bfloat16 [768], P('fsdp'), may hold values from -4 to 4
- norm2_gain: bfloat16 [768], P('fsdp'), may hold values from 0.099609375 to 1.8984375
- norm2_shift: bfloat16 [768], P('fsdp'), may hold values from -4 to 4
- vision_up: bfloat16 [768, 3072], P('fsdp'), may hold values from -0.21875 to 0.21875
- vision_up_bias: bfloat16 [3072], P('fsdp'), may hold values from -4 to 4
- vision_down: bfloat16 [3072, 768], P('fsdp'), may hold values from -0.21875 to 0.21875
- vision_down_bias: bfloat16 [768], P('fsdp'), may hold values from -4 to 4
- text_up: bfloat16 [768, 3072], P('fsdp'), may hold values from -0.21875 to 0.21875
- text_up_bias: bfloat16 [3072], P('fsdp'), may hold values from -4 to 4
- text_down: bfloat16 [3072, 768], P('fsdp'), may hold values from -0.21875 to 0.21875
- text_down_bias: bfloat16 [768], P('fsdp'), may hold values from -4 to 4
Outputs:
- mixed: bfloat16 [64, 237, 768], P(('fsdp', 'rep'))
- grad_tokens: float32 [64, 237, 768], P(('fsdp', 'rep'))
- grad_mask_vec: float32 [768], P('fsdp')
- grad_norm1_gain: float32 [768], P('fsdp')
- grad_norm1_shift: float32 [768], P('fsdp')
- grad_w_qkv: float32 [768, 2304], P('fsdp')
- grad_query_bias: float32 [768], P('fsdp')
- grad_value_bias: float32 [768], P('fsdp')
- grad_w_out: float32 [768, 768], P('fsdp')
- grad_out_bias: float32 [768], P('fsdp')
- grad_norm2_gain: float32 [768], P('fsdp')
- grad_norm2_shift: float32 [768], P('fsdp')
- grad_vision_up: float32 [768, 3072], P('fsdp')
- grad_vision_up_bias: float32 [3072], P('fsdp')
- grad_vision_down: float32 [3072, 768], P('fsdp')
- grad_vision_down_bias: float32 [768], P('fsdp')
- grad_text_up: float32 [768, 3072], P('fsdp')
- grad_text_up_bias: float32 [3072], P('fsdp')
- grad_text_down: float32 [3072, 768], P('fsdp')
- grad_text_down_bias: float32 [768], P('fsdp')
The draws below stay inside these ranges and needn't reach their ends.
Inputs may be any that keep to these rules, and one draw needn't show every extreme that they name: A caption fills the first lengths slots of its item; in every draw some item fills all 40 slots. Only slots below the item's length are masked; an item masks between 15 and 80 percent of its length, rounded down, and at least one slot.
All inputs are finite; a program needn't handle non-finite values.
Results may differ from the reference program's by a relative error of at most 0.017.
Values may be sent and summed in bfloat16 or wider, within the bound.
No kernel may reach another device: no remote copies, remote signals or barrier semaphores. Data moves between devices by JAX's collectives and lax.ppermute only.
A program may use at most 192 MiB of HBM per device.

```python
import jax
import jax.numpy as jnp
from jax import lax

D = 768
HEADS = 12
HEAD_DIM = 64
FF = 3072
PATCHES = 197
SLOTS = 40
ROWS = 237
ITEMS = 64


def caption_draw(key):
    key_len, key_long, key_share, key_order = jax.random.split(key, 4)
    drawn = jax.random.randint(key_len, (ITEMS,), SLOTS // 5, SLOTS + 1)
    longest = jax.random.randint(key_long, (), 0, ITEMS)
    item_index = jnp.arange(ITEMS)
    caption_len = jnp.where(item_index == longest, SLOTS, drawn).astype(jnp.int32)
    percent = jax.random.randint(key_share, (ITEMS,), 15, 81)
    counted = jnp.maximum(caption_len * percent // 100, 1)
    slot_index = jnp.arange(SLOTS)
    ranking = jax.random.randint(key_order, (ITEMS, SLOTS), 0, 1 << 20) * 64 + slot_index[None, :]
    inside = slot_index[None, :] < caption_len[:, None]
    ranking = jnp.where(inside, ranking, 1 << 28)
    order = jnp.argsort(ranking, axis=1, stable=True)
    place = jnp.argsort(order, axis=1, stable=True)
    chosen = (place < counted[:, None]).astype(jnp.int32)
    return (caption_len, chosen)


def draw_lengths(key, part):
    return caption_draw(key)[0]


def draw_masked(key, part):
    return caption_draw(key)[1]


def block_scale(rng, dims, cuts, low, top_value):
    factor_of, own = 1.0, jax.random.fold_in(rng, 6)
    for dim, parts in cuts:
        steps = jnp.exp(jax.random.uniform(jax.random.fold_in(own, dim), (parts,), jnp.float32, low / len(cuts), top_value / len(cuts)))
        factor_of = factor_of * jnp.repeat(steps, dims[dim] // parts).reshape([-1 if axis == dim else 1 for axis in range(len(dims))])
    return factor_of


def scatter_about(stream_key, extent, scale, most, pieces=(), kind=jnp.bfloat16):
    loudness = block_scale(stream_key, extent, pieces, -0.22, 0.18) if pieces else 1.0
    array = jax.random.normal(stream_key, extent, jnp.float32) * scale * loudness
    return jnp.minimum(jnp.maximum(array, -most), most).astype(kind)


def setup_inputs(seed: int = 0) -> dict:
    splits = jax.random.split(jax.random.key(seed), 23)
    return {
        "tokens": scatter_about(splits[0], (ITEMS, ROWS, D), 1.0, 6.0, ((0, 32),)),
        "out_grad": scatter_about(splits[1], (ITEMS, ROWS, D), 1.0, 6.0, ((0, 32),)),
        "masked": draw_masked(jax.random.fold_in(splits[22], 71), 0),
        "lengths": draw_lengths(jax.random.fold_in(splits[22], 71), 0),
        "mask_vec": scatter_about(splits[4], (D,), 1.0, 6.0, ((0, 8),)),
        "norm1_gain": jnp.clip(1.0 + 0.18 * jax.random.normal(splits[5], (D,), jnp.float32), 0.099609375, 1.8984375).astype(jnp.bfloat16),
        "norm1_shift": scatter_about(splits[6], (D,), 0.3, 4.0, ((0, 8),)),
        "w_qkv": scatter_about(splits[7], (D, 3 * D), D ** -0.5, 0.21875, ((0, 8),)),
        "query_bias": scatter_about(splits[8], (D,), 0.3, 4.0, ((0, 8),)),
        "value_bias": scatter_about(splits[9], (D,), 0.3, 4.0, ((0, 8),)),
        "w_out": scatter_about(splits[10], (D, D), (D // 16) ** -0.5, 0.875, ((0, 8),)),
        "out_bias": scatter_about(splits[11], (D,), 0.3, 4.0, ((0, 8),)),
        "norm2_gain": jnp.clip(1.0 + 0.18 * jax.random.normal(splits[12], (D,), jnp.float32), 0.099609375, 1.8984375).astype(jnp.bfloat16),
        "norm2_shift": scatter_about(splits[13], (D,), 0.3, 4.0, ((0, 8),)),
        "vision_up": scatter_about(splits[14], (D, FF), D ** -0.5, 0.21875, ((0, 8),)),
        "vision_up_bias": scatter_about(splits[15], (FF,), 0.3, 4.0, ((0, 8),)),
        "vision_down": scatter_about(splits[16], (FF, D), (FF // 4) ** -0.5, 0.21875, ((0, 8),)),
        "vision_down_bias": scatter_about(splits[17], (D,), 0.3, 4.0, ((0, 8),)),
        "text_up": scatter_about(splits[18], (D, FF), D ** -0.5, 0.21875, ((0, 8),)),
        "text_up_bias": scatter_about(splits[19], (FF,), 0.3, 4.0, ((0, 8),)),
        "text_down": scatter_about(splits[20], (FF, D), (FF // 4) ** -0.5, 0.21875, ((0, 8),)),
        "text_down_bias": scatter_about(splits[21], (D,), 0.3, 4.0, ((0, 8),)),
    }


@jax.custom_vjp
def low(v):
    return lax.optimization_barrier(v.astype(jnp.bfloat16)).astype(jnp.float32)

@jax.custom_vjp
def low_back(v):
    return v

def low_keep(v):
    return (low(v), None)

def low_pass(kept, grad):
    return (grad,)

def back_keep(v):
    return (v, None)

def back_low(kept, grad):
    return (low(grad),)
low.defvjp(low_keep, low_pass)
low_back.defvjp(back_keep, back_low)
epsilon = 1e-06
highest = lax.Precision.HIGHEST

def layer_norm(hidden, gain, shift):
    center = hidden - lax.optimization_barrier(jnp.mean(hidden, axis=-1, keepdims=True))
    spread = lax.optimization_barrier(jnp.mean(center * center, axis=-1, keepdims=True))
    return center * lax.rsqrt(spread + epsilon) * gain + shift

def matmul(left, right):
    return jnp.dot(left, right, precision=highest)

def expert(rows_in, up_matrix, up_shift, down_matrix, down_shift):
    upper = low_back(matmul(rows_in, up_matrix) + up_shift)
    active = low(jax.nn.gelu(upper, approximate=False))
    return low_back(matmul(active, down_matrix) + down_shift)

def forward(weights, inputs, mask_rows, valid_keys):
    mask_vector, gain_one, shift_one, qkv_matrix, query_shift, value_shift, out_matrix, out_shift, gain_two, shift_two, vision_upm, vision_upb, vision_downm, vision_downb, text_upm, text_upb, text_downm, text_downb = weights
    group, row_count, model_width = inputs.shape
    split_shape = (group, row_count, HEADS, HEAD_DIM)
    hidden0 = mask_rows * mask_vector + (1.0 - mask_rows) * inputs
    normed = low(layer_norm(hidden0, gain_one, shift_one)).reshape(group * row_count, model_width)
    projected = matmul(normed, qkv_matrix)
    query_part = low(low_back((projected[:, :model_width] + query_shift) * 0.125)).reshape(split_shape)
    key_part = low(low_back(projected[:, model_width:2 * model_width])).reshape(split_shape)
    value_part = low(low_back(projected[:, 2 * model_width:] + value_shift)).reshape(split_shape)
    scores = jnp.einsum('gqhd,gkhd->ghqk', query_part, key_part, precision=highest)
    scores = low_back(jnp.where(valid_keys[:, None, None, :], scores, -1000000000.0))
    probs = low(jax.nn.softmax(scores, axis=-1))
    context = jnp.einsum('ghqk,gkhd->gqhd', probs, value_part, precision=highest)
    context = low(low_back(context.reshape(group * row_count, model_width)))
    attended = low_back(matmul(context, out_matrix) + out_shift)
    hidden1 = hidden0 + attended.reshape(group, row_count, model_width)
    second = low(layer_norm(hidden1, gain_two, shift_two))
    vision = expert(second[:, :PATCHES].reshape(-1, model_width), vision_upm, vision_upb, vision_downm, vision_downb)
    text = expert(second[:, PATCHES:].reshape(-1, model_width), text_upm, text_upb, text_downm, text_downb)
    branch = jnp.concatenate([vision.reshape(group, PATCHES, model_width), text.reshape(group, SLOTS, model_width)], axis=1)
    return hidden1 + branch

def reference(tokens, out_grad, masked, lengths, mask_vec, norm1_gain, norm1_shift, w_qkv, query_bias, value_bias, w_out, out_bias, norm2_gain, norm2_shift, vision_up, vision_up_bias, vision_down, vision_down_bias, text_up, text_up_bias, text_down, text_down_bias):
    weights = tuple((member.astype(jnp.float32) for member in (mask_vec, norm1_gain, norm1_shift, w_qkv, query_bias, value_bias, w_out, out_bias, norm2_gain, norm2_shift, vision_up, vision_up_bias, vision_down, vision_down_bias, text_up, text_up_bias, text_down, text_down_bias)))
    mask_rows = jnp.concatenate([jnp.zeros((ITEMS, PATCHES), jnp.float32), masked.astype(jnp.float32)], axis=1)
    valid_keys = jnp.arange(ROWS, dtype=jnp.int32)[None, :] < (PATCHES + lengths)[:, None]
    group_items = 16
    blocks = ITEMS // group_items

    def reshaped(source):
        return source.reshape((blocks, group_items) + source.shape[1:])

    def advance(totals, block):
        inputs, cotangent, rows_mask, keys_valid = block
        rows_mask = rows_mask[..., None]

        def apply_layer(params, values):
            return forward(params, values, rows_mask, keys_valid)
        result, pullback = jax.vjp(apply_layer, weights, inputs)
        grad_params, grad_inputs = pullback(cotangent)
        totals = jax.tree.map(jnp.add, totals, grad_params)
        return (totals, (result.astype(jnp.bfloat16), grad_inputs))
    start = jax.tree.map(jnp.zeros_like, weights)
    totals, (mixed, grad_tokens) = lax.scan(advance, start, (reshaped(tokens.astype(jnp.float32)), reshaped(out_grad.astype(jnp.float32)), reshaped(mask_rows), reshaped(valid_keys)))
    return (mixed.reshape(ITEMS, ROWS, D), grad_tokens.reshape(ITEMS, ROWS, D), totals[0], totals[1], totals[2], totals[3], totals[4], totals[5], totals[6], totals[7], totals[8], totals[9], totals[10], totals[11], totals[12], totals[13], totals[14], totals[15], totals[16], totals[17])
```

```python
import functools
import math

import jax
import jax.numpy as jnp
from jax import lax
from jax.experimental import pallas as pl
from jax.experimental.pallas import tpu as pltpu
from jax.sharding import PartitionSpec as P

HEAD_DIM = 64
BF = jnp.bfloat16
F32 = jnp.float32
epsilon = 1e-06
VMEM_LIMIT = 58 * 1024 * 1024

ITEM = 256
TEXT_AT = 208


def cdiv(a, b):
    return -(-a // b)


def dot_nn(a, b):
    return lax.dot_general(a, b, (((1,), (0,)), ((), ())), preferred_element_type=F32)


def dot_nt(a, b):
    return lax.dot_general(a, b, (((1,), (1,)), ((), ())), preferred_element_type=F32)


def dot_tn(a, b):
    return lax.dot_general(a, b, (((0,), (0,)), ((), ())), preferred_element_type=F32)


def gelu_parts(upper):
    half = 0.5 * (1.0 + lax.erf(upper * math.sqrt(0.5)))
    slope = half + upper * (jnp.exp(-0.5 * upper * upper) * (1.0 / math.sqrt(2.0 * math.pi)))
    return upper * half, slope


def normalize(hidden):
    center = hidden - jnp.mean(hidden, axis=-1, keepdims=True)
    spread = jnp.mean(center * center, axis=-1, keepdims=True)
    scale = lax.rsqrt(spread + epsilon)
    return center * scale, scale


def start_rows(pieces, target, me, sems):
    block = target.shape[0] // 8
    copies = []
    for index, (slot, first, ref) in enumerate(pieces):
        row = pl.multiple_of((me ^ slot) * block + first, 16)
        copy = pltpu.make_async_copy(ref, target.at[pl.ds(row, ref.shape[0])], sems.at[index])
        copy.start()
        copies.append(copy)
    return copies


def mixed_in(tok, mask, vec, rows):
    keep = mask[rows, :]
    return keep * vec[0:1, :] + (1.0 - keep) * tok[rows, :].astype(F32)


def attn_fwd_kernel(slots, info, tok, mask, vec, bias, *refs):
    count = len(slots)
    pieces, (n1, qkv, probs, ctx, weight, sems) = refs[:count], refs[count:]
    me = info[0]
    width = tok.shape[1]
    copies = start_rows([(s, f, r) for (s, f), r in zip(slots, pieces)], weight, me, sems)

    @pl.loop(0, tok.shape[0] // 64)
    def _(step):
        rows = pl.ds(pl.multiple_of(step * 64, 64), 64)
        normal, _unused = normalize(mixed_in(tok, mask, vec, rows))
        n1[rows, :] = (normal * vec[1:2, :] + vec[2:3, :]).astype(BF)

    for copy in copies:
        copy.wait()

    @pl.loop(0, 3 * width // 256)
    def _(step):
        cols = pl.ds(pl.multiple_of(step * 256, 256), 256)
        factor = jnp.where(step < width // 256, 0.125, 1.0).astype(F32)
        out = dot_nn(n1[...], weight[:, cols])
        qkv[:, cols] = ((out + bias[0:1, cols]) * factor).astype(BF)

    pairs = width // 128
    patches = info[3]

    @pl.loop(0, (tok.shape[0] // ITEM) * pairs)
    def _(step):
        item, pair = step // pairs, step % pairs
        rows = pl.ds(pl.multiple_of(item * ITEM, ITEM), ITEM)
        lane = lambda part: pl.ds(pl.multiple_of(part * width + pair * 128, 128), 128)
        q2, k2, v2 = qkv[rows, lane(0)], qkv[rows, lane(1)], qkv[rows, lane(2)]
        low = lax.broadcasted_iota(jnp.int32, (ITEM, 128), 1) < HEAD_DIM
        zero = jnp.zeros_like(q2)
        both = jnp.concatenate([jnp.where(low, q2, zero), jnp.where(low, zero, q2)], axis=0)
        scores = dot_nt(both, k2)
        col = lax.broadcasted_iota(jnp.int32, (1, ITEM), 1)
        valid = (col < patches) | ((col >= TEXT_AT) & (col < TEXT_AT + info[1 + item]))
        scores = jnp.where(valid, scores, -1000000000.0)
        expo = jnp.exp(scores - jnp.max(scores, axis=-1, keepdims=True))
        prob = (expo * (1.0 / jnp.sum(expo, axis=-1, keepdims=True))).astype(BF)
        probs[step] = prob
        wide = jnp.concatenate([prob[:ITEM], prob[ITEM:]], axis=1)
        values = jnp.concatenate([jnp.where(low, v2, zero), jnp.where(low, zero, v2)], axis=0)
        ctx[rows, pl.ds(pl.multiple_of(pair * 128, 128), 128)] = dot_nn(wide, values).astype(BF)


def out_proj_kernel(slots, text_rows, info, tok, mask, vec, ctx, *refs):
    count = len(slots)
    pieces, (h1, n2, n2t, weight, sems) = refs[:count], refs[count:]
    copies = start_rows([(s, f, r) for (s, f), r in zip(slots, pieces)], weight, info[0], sems)
    for copy in copies:
        copy.wait()

    @pl.loop(0, tok.shape[0] // 128)
    def _(step):
        rows = pl.ds(pl.multiple_of(step * 128, 128), 128)
        attended = dot_nn(ctx[rows, :], weight[...]) + vec[5:6, :]
        hidden = mixed_in(tok, mask, vec, rows) + attended
        h1[rows, :] = hidden
        normal, _unused = normalize(hidden)
        n2[rows, :] = (normal * vec[6:7, :] + vec[7:8, :]).astype(BF)

    items = tok.shape[0] // ITEM
    text = [n2[i * ITEM + TEXT_AT : i * ITEM + ITEM, :].astype(F32)[:text_rows] for i in range(items)]
    n2t[...] = jnp.concatenate(text, axis=0).astype(BF)


def vision_kernel(info, n2, grad, h1, vec, up_bias, *refs):
    ups, downs = refs[:8], refs[8:16]
    mixed, gn2, up_keep, up_send, down_keep, down_send, bias_sums = refs[16:23]
    up_w, down_w, left, left_t, right, act, low, acc, sems = refs[23:]
    me = info[0]
    width = n2.shape[1]
    items = n2.shape[0] // ITEM
    chunk = 2 * downs[0].shape[0]
    copies = start_rows([(s, 0, r) for s, r in enumerate(ups)], up_w, me, sems)
    copies += start_rows([(s, 0, r) for s, r in enumerate(downs)], down_w, me, sems.at[pl.ds(8, 8)])
    for i in range(items):
        left[pl.ds(i * TEXT_AT, TEXT_AT), :] = n2[pl.ds(i * ITEM, TEXT_AT), :]
        right[pl.ds(i * TEXT_AT, TEXT_AT), :] = grad[pl.ds(i * ITEM, TEXT_AT), :]
    turned = left[...].T
    block = width // 8
    for b in range(8):
        place = pl.multiple_of((me ^ b) * block, 16)
        left_t[pl.ds(place, block), :] = turned[b * block : (b + 1) * block]
    acc[...] = jnp.zeros_like(acc)
    gn2[...] = jnp.zeros_like(gn2)
    for copy in copies:
        copy.wait()

    @pl.loop(0, 4)
    def _(step):
        chip = (me // 2) ^ step
        at = pl.multiple_of(chip * chunk, chunk)
        up_c = up_w[:, pl.ds(at, chunk)]
        down_c = down_w[pl.ds(at, chunk), :]
        upper = dot_nn(left[...], up_c) + up_bias[0:1, pl.ds(at, chunk)]
        active, slope = gelu_parts(upper)
        act[...] = active.astype(BF)
        grad_upper = dot_nt(right[...], down_c) * slope
        low[...] = grad_upper.astype(BF)
        bias_sums[0:1, pl.ds(at, chunk)] = jnp.sum(low[...].astype(F32), axis=0, keepdims=True)
        acc[...] += dot_nn(act[...], down_c)
        gn2[...] += dot_nt(low[...], up_c)
        grad_down = dot_tn(act[...], right[...]).astype(BF)
        half = chunk // 2

        @pl.when(me % 2 == 0)
        def _():
            down_keep[step] = grad_down[:half]
            down_send[step] = grad_down[half:]

        @pl.when(me % 2 == 1)
        def _():
            down_keep[step] = grad_down[half:]
            down_send[step] = grad_down[:half]

        grad_up = dot_nn(left_t[...], low[...]).astype(BF)
        for b in range(4):
            up_keep[b, :, pl.ds(at, chunk)] = grad_up[2 * b * block : (2 * b + 1) * block]
            up_send[b, :, pl.ds(at, chunk)] = grad_up[(2 * b + 1) * block : (2 * b + 2) * block]

    for i in range(items):
        rows = pl.ds(i * TEXT_AT, TEXT_AT)
        mixed[rows, :] = (h1[pl.ds(i * ITEM, TEXT_AT), :] + acc[rows, :] + vec[8:9, :]).astype(BF)


def text_kernel(info, up_mine, up_other, down, up_bias, *refs):
    ins, grads = refs[:8], refs[8:16]
    (branch_keep, branch_send, gn2_keep, gn2_send, up_keep, up_send, grad_down, bias_sums) = refs[16:24]
    up_w, left, right, left_t = refs[24:]
    me = info[0]
    block = up_mine.shape[1]
    rows = ins[0].shape[0]
    for s in range(4):
        up_w[pl.ds(pl.multiple_of((me ^ (2 * s)) * block, 16), block), :] = up_mine[s]
        up_w[pl.ds(pl.multiple_of((me ^ (2 * s + 1)) * block, 16), block), :] = up_other[s]
    for s in range(8):
        left[pl.ds(s * rows, rows), :] = ins[s][...]
        right[pl.ds(s * rows, rows), :] = grads[s][...]
    turned = left[...].T
    for b in range(8):
        place = pl.multiple_of((me ^ b) * block, 16)
        left_t[pl.ds(place, block), :] = turned[b * block : (b + 1) * block]
    upper = dot_nn(left[...], up_w[...]) + up_bias[...]
    active, slope = gelu_parts(upper)
    act = active.astype(BF)
    low = (dot_nt(right[...], down[...]) * slope).astype(BF)
    bias_sums[...] = jnp.sum(low.astype(F32), axis=0, keepdims=True)
    gn2 = dot_nt(low, up_w[...]).astype(BF)
    for s in range(4):
        gn2_keep[s] = gn2[2 * s * rows : (2 * s + 1) * rows]
        gn2_send[s] = gn2[(2 * s + 1) * rows : (2 * s + 2) * rows]
    branch = dot_nn(act, down[...]).astype(BF)
    for s in range(4):
        branch_keep[s] = branch[2 * s * rows : (2 * s + 1) * rows]
        branch_send[s] = branch[(2 * s + 1) * rows : (2 * s + 2) * rows]
    grad_down[...] = dot_tn(act, right[...]).astype(BF)
    grad_up = dot_nn(left_t[...], low).astype(BF)
    for b in range(4):
        up_keep[b] = grad_up[2 * b * block : (2 * b + 1) * block]
        up_send[b] = grad_up[(2 * b + 1) * block : (2 * b + 2) * block]


def attn_bwd_kernel(slots, text_rows, info, gn2v, t0, t1, t2, t3, grad, h1, vec, ctx, qkv, probs, n1, *refs):
    count = len(slots)
    pieces, refs = refs[:count], refs[count:]
    a_keep, a_send, b_keep, b_send, gh1, stacked, sums, bias_sums = refs[:8]
    weight, gn2, low, gctx, n1_t, ctx_t, sems = refs[8:]
    me = info[0]
    total, width = h1.shape
    items = total // ITEM
    copies = start_rows([(s, f, r) for (s, f), r in zip(slots, pieces)], weight, me, sems)
    text = (
        t0[...].astype(F32) + t1[...].astype(F32) + t2[...].astype(F32) + t3[...].astype(F32)
    )
    for i in range(items):
        gn2[pl.ds(i * ITEM, TEXT_AT), :] = gn2v[pl.ds(i * TEXT_AT, TEXT_AT), :]
        gn2[pl.ds(i * ITEM + TEXT_AT, text_rows), :] = text[i * text_rows : (i + 1) * text_rows]
        pad = ITEM - TEXT_AT - text_rows
        gn2[pl.ds(i * ITEM + TEXT_AT + text_rows, pad), :] = jnp.zeros((pad, width), F32)
    sums[...] = jnp.zeros_like(sums)

    @pl.loop(0, total // 64)
    def _(step):
        rows = pl.ds(pl.multiple_of(step * 64, 64), 64)
        normal, scale = normalize(h1[rows, :])
        above = gn2[rows, :]
        inner = above * vec[6:7, :]
        back = scale * (
            inner
            - jnp.mean(inner, axis=-1, keepdims=True)
            - normal * jnp.mean(inner * normal, axis=-1, keepdims=True)
        )
        out = grad[rows, :].astype(F32)
        hidden = out + back
        gh1[rows, :] = hidden
        low[rows, :] = hidden.astype(BF)
        sums[0:1, :] += jnp.sum(above * normal, axis=0, keepdims=True)
        sums[1:2, :] += jnp.sum(above, axis=0, keepdims=True)
        sums[2:3, :] += jnp.sum(hidden.astype(BF).astype(F32), axis=0, keepdims=True)

    block = width // 8
    for source, target in ((n1, n1_t), (ctx, ctx_t)):
        turned = source[...].T
        for b in range(8):
            place = pl.multiple_of((me ^ b) * block, 16)
            target[pl.ds(place, block), :] = turned[b * block : (b + 1) * block]

    for copy in copies:
        copy.wait()
    gctx[...] = dot_nt(low[...], weight[...]).astype(BF)
    pairs = width // 128

    @pl.loop(0, items * pairs)
    def _(step):
        item, pair = step // pairs, step % pairs
        rows = pl.ds(pl.multiple_of(item * ITEM, ITEM), ITEM)
        lane = lambda part: pl.ds(pl.multiple_of(part * width + pair * 128, 128), 128)
        q2, k2, v2 = qkv[rows, lane(0)], qkv[rows, lane(1)], qkv[rows, lane(2)]
        g2 = gctx[rows, pl.ds(pl.multiple_of(pair * 128, 128), 128)]
        lower = lax.broadcasted_iota(jnp.int32, (ITEM, 128), 1) < HEAD_DIM
        zero = jnp.zeros_like(q2)
        split = lambda a: jnp.concatenate([jnp.where(lower, a, zero), jnp.where(lower, zero, a)], axis=0)
        both_g = split(g2)
        prob_b = probs[step]
        prob = prob_b.astype(F32)
        gprob = dot_nt(both_g, v2)
        weighted = prob * gprob
        gscore = (weighted - prob * jnp.sum(weighted, axis=-1, keepdims=True)).astype(BF)
        stacked[rows, lane(2)] = dot_tn(prob_b, both_g).astype(BF)
        stacked[rows, lane(1)] = dot_tn(gscore, split(q2)).astype(BF)
        wide = jnp.concatenate([gscore[:ITEM], gscore[ITEM:]], axis=1)
        gquery = dot_nn(wide, split(k2)).astype(BF).astype(F32) * 0.125
        stacked[rows, lane(0)] = gquery.astype(BF)

    def put(keep, send, value, cols):
        for b in range(4):
            keep[b, :, cols] = value[2 * b * block : (2 * b + 1) * block]
            send[b, :, cols] = value[(2 * b + 1) * block : (2 * b + 2) * block]

    for part in range(2):
        cols = pl.ds(part * width, width)
        put(a_keep, a_send, dot_nn(n1_t[...], stacked[:, cols]).astype(BF), cols)
    first = pl.ds(0, width)
    put(b_keep, b_send, dot_nn(n1_t[...], stacked[:, 2 * width : 3 * width]).astype(BF), first)
    put(b_keep, b_send, dot_nn(ctx_t[...], low[...]).astype(BF), pl.ds(width, width))

    for part in range(3):
        cols = stacked[:, part * width : (part + 1) * width].astype(F32)
        bias_sums[0:1, part * width : (part + 1) * width] = jnp.sum(cols, axis=0, keepdims=True)


def last_kernel(slots, info, stacked, gh1, tok, mask, vec, *refs):
    count = len(slots)
    pieces, (gtok, sums, weight, sems) = refs[:count], refs[count:]
    copies = start_rows([(s, f, r) for (s, f), r in zip(slots, pieces)], weight, info[0], sems)
    sums[...] = jnp.zeros_like(sums)
    for copy in copies:
        copy.wait()

    @pl.loop(0, tok.shape[0] // 128)
    def _(step):
        rows = pl.ds(pl.multiple_of(step * 128, 128), 128)
        above = dot_nt(stacked[rows, :], weight[...])
        normal, scale = normalize(mixed_in(tok, mask, vec, rows))
        inner = above * vec[1:2, :]
        back = scale * (
            inner
            - jnp.mean(inner, axis=-1, keepdims=True)
            - normal * jnp.mean(inner * normal, axis=-1, keepdims=True)
        )
        hidden = gh1[rows, :] + back
        keep = mask[rows, :]
        gtok[rows, :] = hidden * (1.0 - keep)
        sums[0:1, :] += jnp.sum(hidden * keep, axis=0, keepdims=True)
        sums[1:2, :] += jnp.sum(above * normal, axis=0, keepdims=True)
        sums[2:3, :] += jnp.sum(above, axis=0, keepdims=True)


def call(kernel, outs, scratch, args, pieces=(), flops=0, moved=0):
    spec = lambda a: pl.BlockSpec(memory_space=pltpu.VMEM)
    in_specs = [pl.BlockSpec(memory_space=pltpu.SMEM)] + [spec(a) for a in args[1:]]
    in_specs += [pl.BlockSpec(memory_space=pl.ANY)] * len(pieces)
    return pl.pallas_call(
        kernel,
        out_shape=[jax.ShapeDtypeStruct(s, d) for s, d in outs],
        in_specs=in_specs,
        out_specs=[pl.BlockSpec(memory_space=pltpu.VMEM)] * len(outs),
        scratch_shapes=scratch,
        compiler_params=pltpu.CompilerParams(vmem_limit_bytes=VMEM_LIMIT),
        cost_estimate=pl.CostEstimate(flops=flops, bytes_accessed=moved, transcendentals=0),
    )(*args, *pieces)


def swap(array, mask, count=8):
    return lax.ppermute(array, "fsdp", [(i, i ^ mask) for i in range(count)])


def swap_rep(array, mask, count):
    return lax.ppermute(array, "rep", [(i, i ^ mask) for i in range(count)])


def gather(own, order):
    x, y = swap(own, 2), swap(own, 4)
    if order == "xy":
        far = [(6, 0, swap(x, 4))]
    elif order == "yx":
        far = [(6, 0, swap(y, 2))]
    else:
        half = own.shape[0] // 2
        far = [(6, 0, swap(x[:half], 4)), (6, half, swap(y[half:], 2))]
    here = [(0, 0, own), (2, 0, x), (4, 0, y)] + far
    return here + [(slot + 1, first, swap(a, 1)) for slot, first, a in here]


def add(*terms):
    out = terms[0].astype(F32)
    for term in terms[1:]:
        out = out + term.astype(F32)
    return out.astype(BF)


def scatter(keep, send, order):
    got = swap(send, 1)
    one, two = (2, 4) if order == "xy" else (4, 2)
    i, j = one // 2, two // 2
    there = swap(add(jnp.stack([keep[i], keep[3]]), jnp.stack([got[i], got[3]])), one)
    far = swap(add(keep[j], got[j], there[1]), two)
    return add(keep[0], got[0], there[0], far)


def planned(
    rep_count,
    tokens,
    out_grad,
    masked,
    lengths,
    mask_vec,
    norm1_gain,
    norm1_shift,
    w_qkv,
    query_bias,
    value_bias,
    w_out,
    out_bias,
    norm2_gain,
    norm2_shift,
    vision_up,
    vision_up_bias,
    vision_down,
    vision_down_bias,
    text_up,
    text_up_bias,
    text_down,
    text_down_bias,
):
    items, row_count, width = tokens.shape
    text_rows = masked.shape[1]
    patches = row_count - text_rows
    block = width // 8
    hidden_block = vision_down.shape[0]
    hidden = 8 * hidden_block
    total = items * ITEM
    me = lax.axis_index("fsdp").astype(jnp.int32)
    rep = lax.axis_index("rep").astype(jnp.int32)
    core = me % 2
    chip = me // 2

    def padded(array):
        z = lambda n: jnp.zeros((items, n, width), BF)
        parts = [array[:, :patches], z(TEXT_AT - patches), array[:, patches:], z(ITEM - TEXT_AT - text_rows)]
        return jnp.concatenate(parts, axis=1).reshape(total, width)

    tok = padded(tokens)
    grad = padded(out_grad)
    mask = jnp.concatenate(
        [
            jnp.zeros((items, TEXT_AT), F32),
            masked.astype(F32),
            jnp.zeros((items, ITEM - TEXT_AT - text_rows), F32),
        ],
        axis=1,
    ).reshape(total, 1)
    info = jnp.concatenate([me[None], lengths, jnp.full((1,), patches, jnp.int32)])

    names = (
        mask_vec,
        norm1_gain,
        norm1_shift,
        query_bias,
        value_bias,
        out_bias,
        norm2_gain,
        norm2_shift,
        vision_down_bias,
        text_down_bias,
    )
    own_vec = jnp.concatenate([jnp.stack(names), vision_up_bias.reshape(-1, block)], axis=0)
    own_vec = jnp.pad(own_vec, ((0, 16 - own_vec.shape[0]), (0, 128 - block)))
    vec_slots = jnp.stack([own_vec] + [swap(own_vec, m) for m in range(1, 8)])
    vec8 = jnp.take(vec_slots, me ^ jnp.arange(8, dtype=jnp.int32), axis=0)[:, :, :block]
    vec8 = vec8.astype(F32)
    vec = vec8.transpose(1, 0, 2).reshape(16, width)
    up_bias = vec8[:, 10 : 10 + hidden_block // block].reshape(1, hidden)
    qkv_bias = jnp.concatenate([vec[3:4], jnp.zeros((1, width), F32), vec[4:5]], axis=1)

    qkv_pieces = gather(w_qkv, "split")
    out_pieces = gather(w_out, "split")
    up_pieces = sorted(gather(vision_up, "xy"), key=lambda p: p[0])
    down_pieces = sorted(gather(vision_down, "yx"), key=lambda p: p[0])
    slots_of = lambda pieces: tuple((p[0], p[1]) for p in pieces)
    arrays_of = lambda pieces: [p[2] for p in pieces]

    pair = 2 * hidden_block
    column = lambda s: lax.dynamic_slice_in_dim(text_up, (chip ^ s) * pair, pair, axis=1)
    strips = jnp.stack([column(0)] + [swap(column(s), 2 * s) for s in (1, 2, 3)])
    strips = strips.reshape(4, block, 2, hidden_block)
    take = lambda k: lax.dynamic_index_in_dim(strips, k, axis=2, keepdims=False)
    text_up_mine, text_up_other = take(core), swap(take(1 - core), 1)
    grad_text = out_grad[:, patches:].reshape(-1, width)

    sem = lambda n: pltpu.SemaphoreType.DMA((n,))
    n1, qkv, probs, ctx = call(
        functools.partial(attn_fwd_kernel, slots_of(qkv_pieces)),
        [
            ((total, width), BF),
            ((total, 3 * width), BF),
            ((items * width // 128, 2 * ITEM, ITEM), BF),
            ((total, width), BF),
        ],
        [pltpu.VMEM((width, 3 * width), BF), sem(len(qkv_pieces))],
        [info, tok, mask, vec, qkv_bias],
        arrays_of(qkv_pieces),
        flops=2 * total * width * 3 * width * 2,
        moved=20_000_000,
    )
    h1, n2, n2t = call(
        functools.partial(out_proj_kernel, slots_of(out_pieces), text_rows),
        [((total, width), F32), ((total, width), BF), ((items * text_rows, width), BF)],
        [pltpu.VMEM((width, width), BF), sem(len(out_pieces))],
        [info, tok, mask, vec, ctx],
        arrays_of(out_pieces),
        flops=2 * total * width * width,
        moved=6_000_000,
    )

    text_in = [p[2] for p in sorted(gather_direct(n2t), key=lambda p: p[0])]
    text_grad = [p[2] for p in sorted(gather_direct(grad_text), key=lambda p: p[0])]
    slot_rows = items * text_rows
    quad = lambda r, c: ((4, r, c), BF)
    (branch_keep, branch_send, gn2_keep, gn2_send, tu_keep, tu_send, text_down_sum, text_bias_sum) = call(
        text_kernel,
        [
            quad(slot_rows, width),
            quad(slot_rows, width),
            quad(slot_rows, width),
            quad(slot_rows, width),
            quad(block, hidden_block),
            quad(block, hidden_block),
            ((hidden_block, width), BF),
            ((1, hidden_block), F32),
        ],
        [
            pltpu.VMEM((width, hidden_block), BF),
            pltpu.VMEM((8 * slot_rows, width), BF),
            pltpu.VMEM((8 * slot_rows, width), BF),
            pltpu.VMEM((width, 8 * slot_rows), BF),
        ],
        [
            info,
            text_up_mine,
            text_up_other,
            text_down,
            text_up_bias.astype(F32).reshape(1, hidden_block),
            *text_in,
            *text_grad,
        ],
        flops=12 * 8 * slot_rows * width * hidden_block,
        moved=8_000_000,
    )
    vision_rows = items * TEXT_AT
    mixed_v, gn2_v, vu_keep, vu_send, vd_keep, vd_send, vu_bias_sum = call(
        vision_kernel,
        [
            ((vision_rows, width), BF),
            ((vision_rows, width), F32),
            quad(block, hidden),
            quad(block, hidden),
            quad(hidden_block, width),
            quad(hidden_block, width),
            ((1, hidden), F32),
        ],
        [
            pltpu.VMEM((width, hidden), BF),
            pltpu.VMEM((hidden, width), BF),
            pltpu.VMEM((vision_rows, width), BF),
            pltpu.VMEM((width, vision_rows), BF),
            pltpu.VMEM((vision_rows, width), BF),
            pltpu.VMEM((vision_rows, pair), BF),
            pltpu.VMEM((vision_rows, pair), BF),
            pltpu.VMEM((vision_rows, width), F32),
            sem(16),
        ],
        [info, n2, grad, h1, vec, up_bias],
        [p[2] for p in up_pieces + down_pieces],
        flops=12 * vision_rows * width * hidden,
        moved=25_000_000,
    )

    def scatter_direct(keep, send):
        own = add(keep, swap(send, 1))
        return [own[0]] + [swap(own[s], 2 * s) for s in (1, 2, 3)]

    gn2_text = scatter_direct(gn2_keep, gn2_send)
    a_keep, a_send, b_keep, b_send, gh1, stacked, sums_two, qkv_sums = call(
        functools.partial(attn_bwd_kernel, slots_of(out_pieces), text_rows),
        [
            quad(block, 2 * width),
            quad(block, 2 * width),
            quad(block, 2 * width),
            quad(block, 2 * width),
            ((total, width), F32),
            ((total, 3 * width), BF),
            ((8, width), F32),
            ((1, 3 * width), F32),
        ],
        [
            pltpu.VMEM((width, width), BF),
            pltpu.VMEM((total, width), F32),
            pltpu.VMEM((total, width), BF),
            pltpu.VMEM((total, width), BF),
            pltpu.VMEM((width, total), BF),
            pltpu.VMEM((width, total), BF),
            sem(len(out_pieces)),
        ],
        [info, gn2_v, *gn2_text, grad, h1, vec, ctx, qkv, probs, n1],
        arrays_of(out_pieces),
        flops=2 * total * width * 5 * width + 40_000_000_00,
        moved=30_000_000,
    )
    gtok, sums_one = call(
        functools.partial(last_kernel, slots_of(qkv_pieces)),
        [((total, width), F32), ((8, width), F32)],
        [pltpu.VMEM((width, 3 * width), BF), sem(len(qkv_pieces))],
        [info, stacked, gh1, tok, mask, vec],
        arrays_of(qkv_pieces),
        flops=2 * total * width * 3 * width,
        moved=12_000_000,
    )

    flip = rep % 2

    def rep_sum(array):
        halves = array.reshape((2, array.shape[0] // 2) + array.shape[1:])
        pick = lambda k: lax.dynamic_index_in_dim(halves, k, axis=0, keepdims=False)
        part = add(pick(flip), swap_rep(pick(1 - flip), 1, rep_count))
        part = add(part, swap_rep(part, 2, rep_count))
        other = swap_rep(part, 1, rep_count)
        ordered = jnp.where(flip == 0, jnp.stack([part, other]), jnp.stack([other, part]))
        return ordered.reshape(array.shape)

    tu_keep, tu_send = (
        rep_sum(jnp.concatenate([tu_keep, tu_send], axis=0)).reshape(2, 4, block, hidden_block)
    )
    tu_got = swap(tu_send, 1)
    tu_wide = jnp.where(
        core == 0,
        jnp.concatenate([tu_keep, tu_got], axis=-1),
        jnp.concatenate([tu_got, tu_keep], axis=-1),
    )
    tu_all = jnp.stack([tu_wide[0]] + [swap(tu_wide[s], 2 * s) for s in (1, 2, 3)])
    tu_all = jnp.take(tu_all, chip ^ jnp.arange(4, dtype=jnp.int32), axis=0)
    grad_text_up = tu_all.transpose(1, 0, 2).reshape(block, hidden).astype(F32)
    grad_text_down = rep_sum(text_down_sum).astype(F32)
    grad_vision_up = rep_sum(scatter(vu_keep, vu_send, "xy")).astype(F32)
    grad_vision_down = rep_sum(scatter(vd_keep, vd_send, "yx")).astype(F32)
    grad_a = rep_sum(scatter(a_keep, a_send, "xy")).astype(F32)
    grad_b = rep_sum(scatter(b_keep, b_send, "yx")).astype(F32)
    grad_w_qkv = jnp.concatenate([grad_a, grad_b[:, :width]], axis=1)
    grad_w_out = grad_b[:, width:]

    grad_rows = out_grad.astype(F32)
    vd_bias_sum = jnp.sum(grad_rows[:, :patches], axis=(0, 1))[None]
    td_bias_sum = jnp.sum(grad_rows[:, patches:], axis=(0, 1))[None]
    qs = qkv_sums.reshape(3, width)
    flat = jnp.concatenate(
        [
            sums_one[0:3],
            qs[0:1],
            qs[2:3],
            sums_two[2:3],
            sums_two[0:2],
            vd_bias_sum,
            td_bias_sum,
            vu_bias_sum.reshape(8, hidden_block // block, block).transpose(1, 0, 2).reshape(-1, width),
        ],
        axis=0,
    )
    for m in (1, 2, 4):
        flat = flat + swap(flat, m)
    mine = lax.dynamic_slice_in_dim(flat, me * block, block, axis=1)
    mine = jnp.concatenate([mine, text_bias_sum.reshape(-1, block)], axis=0)
    for m in (1, 2):
        mine = mine + swap_rep(mine, m, rep_count)
    hid = hidden_block // block
    count = len(names)
    vec_grad = {i: mine[i] for i in range(count)}
    vu_bias_grad = mine[count : count + hid].reshape(-1)
    tu_bias_grad = mine[count + hid : count + 2 * hid].reshape(-1)

    mixed_v = mixed_v.reshape(items, TEXT_AT, width)[:, :patches]
    branch = scatter_direct(branch_keep, branch_send)
    branch = sum(b.astype(F32) for b in branch).reshape(items, text_rows, width)
    h1_text = h1.reshape(items, ITEM, width)[:, TEXT_AT : TEXT_AT + text_rows]
    mixed_t = (h1_text + branch + vec[9][None, None]).astype(BF)
    mixed = jnp.concatenate([mixed_v, mixed_t], axis=1)
    gtok = gtok.reshape(items, ITEM, width)
    grad_tokens = jnp.concatenate(
        [gtok[:, :patches], gtok[:, TEXT_AT : TEXT_AT + text_rows]], axis=1
    )
    return (
        mixed,
        grad_tokens,
        vec_grad[0],
        vec_grad[1],
        vec_grad[2],
        grad_w_qkv,
        vec_grad[3],
        vec_grad[4],
        grad_w_out,
        vec_grad[5],
        vec_grad[6],
        vec_grad[7],
        grad_vision_up,
        vu_bias_grad,
        grad_vision_down,
        vec_grad[8],
        grad_text_up,
        tu_bias_grad,
        grad_text_down,
        vec_grad[9],
    )


def gather_direct(own):
    here = [(0, 0, own)] + [(m, 0, swap(own, m)) for m in (2, 4, 6)]
    return here + [(slot + 1, first, swap(a, 1)) for slot, first, a in here]


def layer_norm(hidden, gain, shift):
    center = hidden - jnp.mean(hidden, axis=-1, keepdims=True)
    spread = jnp.mean(center * center, axis=-1, keepdims=True)
    return center * lax.rsqrt(spread + epsilon) * gain + shift


def exact_gelu(values):
    return jax.nn.gelu(values, approximate=False)


def expert_forward(rows_in, up_matrix, up_shift, down_matrix, down_shift):
    upper = jnp.dot(rows_in, up_matrix, preferred_element_type=jnp.float32) + up_shift.astype(
        jnp.float32
    )
    active, gelu_pull = jax.vjp(exact_gelu, upper)
    active_b = active.astype(jnp.bfloat16)
    result = jnp.dot(active_b, down_matrix, preferred_element_type=jnp.float32) + down_shift.astype(
        jnp.float32
    )
    return (result, active_b, gelu_pull)


def expert_backward(rows_in, active_b, gelu_pull, up_matrix, down_matrix, grad_b):
    grad_down = jnp.einsum("rf,rd->fd", active_b, grad_b, preferred_element_type=jnp.float32)
    grad_down_shift = jnp.sum(grad_b.astype(jnp.float32), axis=0)
    grad_active = jnp.einsum("rd,fd->rf", grad_b, down_matrix, preferred_element_type=jnp.float32)
    (grad_upper,) = gelu_pull(grad_active)
    upper_b = grad_upper.astype(jnp.bfloat16)
    grad_up = jnp.einsum("rd,rf->df", rows_in, upper_b, preferred_element_type=jnp.float32)
    grad_up_shift = jnp.sum(upper_b.astype(jnp.float32), axis=0)
    grad_rows = jnp.einsum("rf,df->rd", upper_b, up_matrix, preferred_element_type=jnp.float32)
    return (grad_up, grad_up_shift, grad_down, grad_down_shift, grad_rows)


def general(
    tokens,
    out_grad,
    masked,
    lengths,
    mask_vec,
    norm1_gain,
    norm1_shift,
    w_qkv,
    query_bias,
    value_bias,
    w_out,
    out_bias,
    norm2_gain,
    norm2_shift,
    vision_up,
    vision_up_bias,
    vision_down,
    vision_down_bias,
    text_up,
    text_up_bias,
    text_down,
    text_down_bias,
):
    item_count, row_count, model_width = tokens.shape
    slot_count = masked.shape[1]
    patches = row_count - slot_count
    head_count = model_width // HEAD_DIM
    split_shape = (item_count, row_count, head_count, HEAD_DIM)

    def fetch_attention():
        return (
            lax.all_gather(mask_vec, "fsdp", axis=0, tiled=True),
            lax.all_gather(norm1_gain, "fsdp", axis=0, tiled=True),
            lax.all_gather(norm1_shift, "fsdp", axis=0, tiled=True),
            lax.all_gather(w_qkv, "fsdp", axis=0, tiled=True),
            lax.all_gather(query_bias, "fsdp", axis=0, tiled=True),
            lax.all_gather(value_bias, "fsdp", axis=0, tiled=True),
            lax.all_gather(w_out, "fsdp", axis=0, tiled=True),
            lax.all_gather(out_bias, "fsdp", axis=0, tiled=True),
        )

    def fetch_feedforward():
        return (
            lax.all_gather(norm2_gain, "fsdp", axis=0, tiled=True),
            lax.all_gather(norm2_shift, "fsdp", axis=0, tiled=True),
            lax.all_gather(vision_up, "fsdp", axis=0, tiled=True),
            lax.all_gather(vision_up_bias, "fsdp", axis=0, tiled=True),
            lax.all_gather(vision_down, "fsdp", axis=0, tiled=True),
            lax.all_gather(vision_down_bias, "fsdp", axis=0, tiled=True),
            lax.all_gather(text_up, "fsdp", axis=0, tiled=True),
            lax.all_gather(text_up_bias, "fsdp", axis=0, tiled=True),
            lax.all_gather(text_down, "fsdp", axis=0, tiled=True),
            lax.all_gather(text_down_bias, "fsdp", axis=0, tiled=True),
        )

    attn_full = fetch_attention()
    full_mask, gain_one, shift_one, qkv_matrix, query_shift, value_shift, out_matrix, out_shift = (
        attn_full
    )
    mask_rows = jnp.concatenate(
        [jnp.zeros((item_count, patches), jnp.float32), masked.astype(jnp.float32)], axis=1
    )[:, :, None]
    hidden0 = mask_rows * full_mask.astype(jnp.float32) + (1.0 - mask_rows) * tokens.astype(
        jnp.float32
    )
    normed1, first_pull = jax.vjp(
        layer_norm, hidden0, gain_one.astype(jnp.float32), shift_one.astype(jnp.float32)
    )
    first_in = normed1.astype(jnp.bfloat16).reshape(item_count * row_count, model_width)
    projected = jnp.dot(first_in, qkv_matrix, preferred_element_type=jnp.float32)
    query_b = (
        ((projected[:, :model_width] + query_shift.astype(jnp.float32)) * 0.125)
        .astype(jnp.bfloat16)
        .reshape(split_shape)
    )
    key_b = projected[:, model_width : 2 * model_width].astype(jnp.bfloat16).reshape(split_shape)
    value_b = (
        (projected[:, 2 * model_width :] + value_shift.astype(jnp.float32))
        .astype(jnp.bfloat16)
        .reshape(split_shape)
    )
    key_index = jnp.arange(row_count, dtype=jnp.int32)
    valid_keys = (key_index[None, :] < patches + lengths[:, None])[:, None, None, :]

    def scores_of():
        raw_scores = jnp.einsum(
            "iqhd,ikhd->ihqk", query_b, key_b, preferred_element_type=jnp.float32
        )
        return jnp.where(valid_keys, raw_scores, -1000000000.0)

    scores = scores_of()
    top_score = jnp.max(scores, axis=-1, keepdims=True)
    expo = jnp.exp(scores - top_score)
    totals = jnp.sum(expo, axis=-1, keepdims=True)
    probs = expo / totals
    log_total = top_score + jnp.log(totals)
    context = jnp.einsum(
        "ihqk,ikhd->iqhd", probs.astype(jnp.bfloat16), value_b, preferred_element_type=jnp.float32
    )
    context_b = context.reshape(item_count * row_count, model_width).astype(jnp.bfloat16)
    attended = jnp.dot(
        context_b, out_matrix, preferred_element_type=jnp.float32
    ) + out_shift.astype(jnp.float32)
    hidden1 = hidden0 + attended.reshape(item_count, row_count, model_width)
    ffn_full = fetch_feedforward()
    (
        gain_two,
        shift_two,
        vision_upm,
        vision_upb,
        vision_downm,
        vision_downb,
        text_upm,
        text_upb,
        text_downm,
        text_downb,
    ) = ffn_full
    normed2, second_pull = jax.vjp(
        layer_norm, hidden1, gain_two.astype(jnp.float32), shift_two.astype(jnp.float32)
    )
    second_in = normed2.astype(jnp.bfloat16)
    patch_in = second_in[:, :patches].reshape(-1, model_width)
    text_in = second_in[:, patches:].reshape(-1, model_width)
    vision_out, vision_act, vision_pull = expert_forward(
        patch_in, vision_upm, vision_upb, vision_downm, vision_downb
    )
    text_out, text_act, text_pull = expert_forward(
        text_in, text_upm, text_upb, text_downm, text_downb
    )
    mixed = hidden1 + jnp.concatenate(
        [
            vision_out.reshape(item_count, patches, model_width),
            text_out.reshape(item_count, slot_count, model_width),
        ],
        axis=1,
    )
    cotangent = out_grad.astype(jnp.float32)
    branch_b = cotangent.astype(jnp.bfloat16)
    ffn_back = fetch_feedforward()
    vision_grads = expert_backward(
        patch_in,
        vision_act,
        vision_pull,
        ffn_back[2],
        ffn_back[4],
        branch_b[:, :patches].reshape(-1, model_width),
    )
    text_grads = expert_backward(
        text_in,
        text_act,
        text_pull,
        ffn_back[6],
        ffn_back[8],
        branch_b[:, patches:].reshape(-1, model_width),
    )
    grad_normed2 = jnp.concatenate(
        [
            vision_grads[4].reshape(item_count, patches, model_width),
            text_grads[4].reshape(item_count, slot_count, model_width),
        ],
        axis=1,
    )
    grad_hidden1_norm, grad_gain_two, grad_shift_two = second_pull(grad_normed2)
    grad_hidden1 = cotangent + grad_hidden1_norm
    attn_back = fetch_attention()
    grad_attn_b = grad_hidden1.reshape(-1, model_width).astype(jnp.bfloat16)
    grad_out_matrix = jnp.einsum(
        "rd,re->de", context_b, grad_attn_b, preferred_element_type=jnp.float32
    )
    grad_out_shift = jnp.sum(grad_attn_b.astype(jnp.float32), axis=0)
    grad_context = jnp.einsum(
        "re,de->rd", grad_attn_b, attn_back[6], preferred_element_type=jnp.float32
    )
    grad_context_b = grad_context.astype(jnp.bfloat16).reshape(split_shape)
    again_probs = jnp.exp(scores_of() - log_total)
    grad_probs = jnp.einsum(
        "iqhd,ikhd->ihqk", grad_context_b, value_b, preferred_element_type=jnp.float32
    )
    grad_value = jnp.einsum(
        "ihqk,iqhd->ikhd",
        again_probs.astype(jnp.bfloat16),
        grad_context_b,
        preferred_element_type=jnp.float32,
    )
    row_inner = jnp.sum(again_probs * grad_probs, axis=-1, keepdims=True)
    grad_scores_b = (again_probs * (grad_probs - row_inner)).astype(jnp.bfloat16)
    grad_query = jnp.einsum(
        "ihqk,ikhd->iqhd", grad_scores_b, key_b, preferred_element_type=jnp.float32
    )
    grad_key = jnp.einsum(
        "ihqk,iqhd->ikhd", grad_scores_b, query_b, preferred_element_type=jnp.float32
    )
    grad_query_b = grad_query.astype(jnp.bfloat16) * jnp.bfloat16(0.125)
    stacked = jnp.concatenate(
        [
            grad_query_b.reshape(-1, model_width),
            grad_key.astype(jnp.bfloat16).reshape(-1, model_width),
            grad_value.astype(jnp.bfloat16).reshape(-1, model_width),
        ],
        axis=1,
    )
    grad_qkv = jnp.einsum("rd,re->de", first_in, stacked, preferred_element_type=jnp.float32)
    grad_query_shift = jnp.sum(stacked[:, :model_width].astype(jnp.float32), axis=0)
    grad_value_shift = jnp.sum(stacked[:, 2 * model_width :].astype(jnp.float32), axis=0)
    grad_normed1 = jnp.einsum(
        "re,de->rd", stacked, attn_back[3], preferred_element_type=jnp.float32
    )
    grad_hidden0_norm, grad_gain_one, grad_shift_one = first_pull(
        grad_normed1.reshape(item_count, row_count, model_width)
    )
    grad_hidden0 = grad_hidden1 + grad_hidden0_norm
    grad_tokens = grad_hidden0 * (1.0 - mask_rows)
    grad_mask = jnp.sum(grad_hidden0 * mask_rows, axis=(0, 1))
    ffn_share = (
        lax.psum_scatter(grad_gain_two, "fsdp", scatter_dimension=0, tiled=True),
        lax.psum_scatter(grad_shift_two, "fsdp", scatter_dimension=0, tiled=True),
        lax.psum_scatter(vision_grads[0], "fsdp", scatter_dimension=0, tiled=True),
        lax.psum_scatter(vision_grads[1], "fsdp", scatter_dimension=0, tiled=True),
        lax.psum_scatter(vision_grads[2], "fsdp", scatter_dimension=0, tiled=True),
        lax.psum_scatter(vision_grads[3], "fsdp", scatter_dimension=0, tiled=True),
        lax.psum_scatter(text_grads[0], "fsdp", scatter_dimension=0, tiled=True),
        lax.psum_scatter(text_grads[1], "fsdp", scatter_dimension=0, tiled=True),
        lax.psum_scatter(text_grads[2], "fsdp", scatter_dimension=0, tiled=True),
        lax.psum_scatter(text_grads[3], "fsdp", scatter_dimension=0, tiled=True),
    )
    attn_share = (
        lax.psum_scatter(grad_mask, "fsdp", scatter_dimension=0, tiled=True),
        lax.psum_scatter(grad_gain_one, "fsdp", scatter_dimension=0, tiled=True),
        lax.psum_scatter(grad_shift_one, "fsdp", scatter_dimension=0, tiled=True),
        lax.psum_scatter(grad_qkv, "fsdp", scatter_dimension=0, tiled=True),
        lax.psum_scatter(grad_query_shift, "fsdp", scatter_dimension=0, tiled=True),
        lax.psum_scatter(grad_value_shift, "fsdp", scatter_dimension=0, tiled=True),
        lax.psum_scatter(grad_out_matrix, "fsdp", scatter_dimension=0, tiled=True),
        lax.psum_scatter(grad_out_shift, "fsdp", scatter_dimension=0, tiled=True),
    )
    quarter = (
        lax.psum_scatter(
            attn_share[0].astype(jnp.bfloat16), "rep", scatter_dimension=0, tiled=True
        ).astype(jnp.float32),
        lax.psum_scatter(
            attn_share[1].astype(jnp.bfloat16), "rep", scatter_dimension=0, tiled=True
        ).astype(jnp.float32),
        lax.psum_scatter(
            attn_share[2].astype(jnp.bfloat16), "rep", scatter_dimension=0, tiled=True
        ).astype(jnp.float32),
        lax.psum_scatter(
            attn_share[3].astype(jnp.bfloat16), "rep", scatter_dimension=0, tiled=True
        ).astype(jnp.float32),
        lax.psum_scatter(
            attn_share[4].astype(jnp.bfloat16), "rep", scatter_dimension=0, tiled=True
        ).astype(jnp.float32),
        lax.psum_scatter(
            attn_share[5].astype(jnp.bfloat16), "rep", scatter_dimension=0, tiled=True
        ).astype(jnp.float32),
        lax.psum_scatter(
            attn_share[6].astype(jnp.bfloat16), "rep", scatter_dimension=0, tiled=True
        ).astype(jnp.float32),
        lax.psum_scatter(
            attn_share[7].astype(jnp.bfloat16), "rep", scatter_dimension=0, tiled=True
        ).astype(jnp.float32),
        lax.psum_scatter(
            ffn_share[0].astype(jnp.bfloat16), "rep", scatter_dimension=0, tiled=True
        ).astype(jnp.float32),
        lax.psum_scatter(
            ffn_share[1].astype(jnp.bfloat16), "rep", scatter_dimension=0, tiled=True
        ).astype(jnp.float32),
        lax.psum_scatter(
            ffn_share[2].astype(jnp.bfloat16), "rep", scatter_dimension=0, tiled=True
        ).astype(jnp.float32),
        lax.psum_scatter(
            ffn_share[3].astype(jnp.bfloat16), "rep", scatter_dimension=0, tiled=True
        ).astype(jnp.float32),
        lax.psum_scatter(
            ffn_share[4].astype(jnp.bfloat16), "rep", scatter_dimension=0, tiled=True
        ).astype(jnp.float32),
        lax.psum_scatter(
            ffn_share[5].astype(jnp.bfloat16), "rep", scatter_dimension=0, tiled=True
        ).astype(jnp.float32),
        lax.psum_scatter(
            ffn_share[6].astype(jnp.bfloat16), "rep", scatter_dimension=0, tiled=True
        ).astype(jnp.float32),
        lax.psum_scatter(
            ffn_share[7].astype(jnp.bfloat16), "rep", scatter_dimension=0, tiled=True
        ).astype(jnp.float32),
        lax.psum_scatter(
            ffn_share[8].astype(jnp.bfloat16), "rep", scatter_dimension=0, tiled=True
        ).astype(jnp.float32),
        lax.psum_scatter(
            ffn_share[9].astype(jnp.bfloat16), "rep", scatter_dimension=0, tiled=True
        ).astype(jnp.float32),
    )
    summed = (
        lax.all_gather(quarter[0].astype(jnp.bfloat16), "rep", axis=0, tiled=True).astype(
            jnp.float32
        ),
        lax.all_gather(quarter[1].astype(jnp.bfloat16), "rep", axis=0, tiled=True).astype(
            jnp.float32
        ),
        lax.all_gather(quarter[2].astype(jnp.bfloat16), "rep", axis=0, tiled=True).astype(
            jnp.float32
        ),
        lax.all_gather(quarter[3].astype(jnp.bfloat16), "rep", axis=0, tiled=True).astype(
            jnp.float32
        ),
        lax.all_gather(quarter[4].astype(jnp.bfloat16), "rep", axis=0, tiled=True).astype(
            jnp.float32
        ),
        lax.all_gather(quarter[5].astype(jnp.bfloat16), "rep", axis=0, tiled=True).astype(
            jnp.float32
        ),
        lax.all_gather(quarter[6].astype(jnp.bfloat16), "rep", axis=0, tiled=True).astype(
            jnp.float32
        ),
        lax.all_gather(quarter[7].astype(jnp.bfloat16), "rep", axis=0, tiled=True).astype(
            jnp.float32
        ),
        lax.all_gather(quarter[8].astype(jnp.bfloat16), "rep", axis=0, tiled=True).astype(
            jnp.float32
        ),
        lax.all_gather(quarter[9].astype(jnp.bfloat16), "rep", axis=0, tiled=True).astype(
            jnp.float32
        ),
        lax.all_gather(quarter[10].astype(jnp.bfloat16), "rep", axis=0, tiled=True).astype(
            jnp.float32
        ),
        lax.all_gather(quarter[11].astype(jnp.bfloat16), "rep", axis=0, tiled=True).astype(
            jnp.float32
        ),
        lax.all_gather(quarter[12].astype(jnp.bfloat16), "rep", axis=0, tiled=True).astype(
            jnp.float32
        ),
        lax.all_gather(quarter[13].astype(jnp.bfloat16), "rep", axis=0, tiled=True).astype(
            jnp.float32
        ),
        lax.all_gather(quarter[14].astype(jnp.bfloat16), "rep", axis=0, tiled=True).astype(
            jnp.float32
        ),
        lax.all_gather(quarter[15].astype(jnp.bfloat16), "rep", axis=0, tiled=True).astype(
            jnp.float32
        ),
        lax.all_gather(quarter[16].astype(jnp.bfloat16), "rep", axis=0, tiled=True).astype(
            jnp.float32
        ),
        lax.all_gather(quarter[17].astype(jnp.bfloat16), "rep", axis=0, tiled=True).astype(
            jnp.float32
        ),
    )
    return (
        mixed.astype(jnp.bfloat16),
        grad_tokens,
        summed[0],
        summed[1],
        summed[2],
        summed[3],
        summed[4],
        summed[5],
        summed[6],
        summed[7],
        summed[8],
        summed[9],
        summed[10],
        summed[11],
        summed[12],
        summed[13],
        summed[14],
        summed[15],
        summed[16],
        summed[17],
    )


def solution(mesh):
    if mesh.shape["fsdp"] == 8 and mesh.shape["rep"] == 4:
        body = functools.partial(planned, mesh.shape["rep"])
    else:
        body = general
    return jax.shard_map(
        body,
        mesh=mesh,
        in_specs=(
            P(("fsdp", "rep"), None, None),
            P(("fsdp", "rep"), None, None),
            P(("fsdp", "rep"), None),
            P(("fsdp", "rep")),
            P("fsdp"),
            P("fsdp"),
            P("fsdp"),
            P("fsdp", None),
            P("fsdp"),
            P("fsdp"),
            P("fsdp", None),
            P("fsdp"),
            P("fsdp"),
            P("fsdp"),
            P("fsdp", None),
            P("fsdp"),
            P("fsdp", None),
            P("fsdp"),
            P("fsdp", None),
            P("fsdp"),
            P("fsdp", None),
            P("fsdp"),
        ),
        out_specs=(
            P(("fsdp", "rep"), None, None),
            P(("fsdp", "rep"), None, None),
            P("fsdp"),
            P("fsdp"),
            P("fsdp"),
            P("fsdp", None),
            P("fsdp"),
            P("fsdp"),
            P("fsdp", None),
            P("fsdp"),
            P("fsdp"),
            P("fsdp"),
            P("fsdp", None),
            P("fsdp"),
            P("fsdp", None),
            P("fsdp"),
            P("fsdp", None),
            P("fsdp"),
            P("fsdp", None),
            P("fsdp"),
        ),
        check_vma=False,
    )
```

```python
import functools
import math

import jax
import jax.numpy as jnp
from jax import lax
from jax.experimental import pallas as pl
from jax.experimental.pallas import tpu as pltpu
from jax.sharding import PartitionSpec as P

HEAD_DIM = 64
BF = jnp.bfloat16
F32 = jnp.float32
epsilon = 1e-06
VMEM_LIMIT = 58 * 1024 * 1024

ITEM = 256
SCALE = 0.2
TEXT_AT = 208


def cdiv(a, b):
    return -(-a // b)


def dot_nn(a, b):
    return lax.dot_general(a, b, (((1,), (0,)), ((), ())), preferred_element_type=F32)


def dot_nt(a, b):
    return lax.dot_general(a, b, (((1,), (1,)), ((), ())), preferred_element_type=F32)


def dot_tn(a, b):
    return lax.dot_general(a, b, (((0,), (0,)), ((), ())), preferred_element_type=F32)


def gelu_parts(upper):
    half = 0.5 * (1.0 + lax.erf(upper * math.sqrt(0.5)))
    slope = half + upper * (jnp.exp(-0.5 * upper * upper) * (1.0 / math.sqrt(2.0 * math.pi)))
    return upper * half, slope


def normalize(hidden):
    center = hidden - jnp.mean(hidden, axis=-1, keepdims=True)
    spread = jnp.mean(center * center, axis=-1, keepdims=True)
    scale = lax.rsqrt(spread + epsilon)
    return center * scale, scale


def start_rows(pieces, target, me, sems):
    block = target.shape[0] // 8
    copies = []
    for index, (slot, first, ref) in enumerate(pieces):
        row = pl.multiple_of((me ^ slot) * block + first, 16)
        copy = pltpu.make_async_copy(ref, target.at[pl.ds(row, ref.shape[0])], sems.at[index])
        copy.start()
        copies.append(copy)
    return copies


def mixed_in(tok, mask, vec, rows):
    keep = mask[rows, :]
    return keep * vec[0:1, :] + (1.0 - keep) * tok[rows, :].astype(F32)


def gate_kernel(count, *refs):
    del count, refs


def gate(arrays, after):
    count = len(arrays)
    return pl.pallas_call(
        functools.partial(gate_kernel, count),
        out_shape=[jax.ShapeDtypeStruct(a.shape, a.dtype) for a in arrays],
        in_specs=[pl.BlockSpec(memory_space=pl.ANY)] * (count + len(after)),
        out_specs=[pl.BlockSpec(memory_space=pl.ANY)] * count,
        input_output_aliases={i: i for i in range(count)},
        cost_estimate=pl.CostEstimate(flops=1000, bytes_accessed=1000, transcendentals=0),
    )(*arrays, *after)


def tick_kernel(*refs):
    refs[-1][...] = jnp.zeros(refs[-1].shape, F32)


def tick(after):
    return pl.pallas_call(
        tick_kernel,
        out_shape=jax.ShapeDtypeStruct((8, 128), F32),
        in_specs=[pl.BlockSpec(memory_space=pl.ANY)] * len(after),
        out_specs=pl.BlockSpec(memory_space=pltpu.VMEM),
        cost_estimate=pl.CostEstimate(flops=1000, bytes_accessed=1000, transcendentals=0),
    )(*after)


def prep_kernel(text_rows, info, tokens, out_grad, w_out, down, up, text_up, *outs):
    tok, grad, grad_v, grad_t, sums, out_copy, down_copy, up_mine, up_other, strip0, te1, te2, te3 = outs
    items, row_count, width = tokens.shape
    patches = row_count - text_rows
    tail = ITEM - TEXT_AT - text_rows
    zeros = lambda n: jnp.zeros((n, width), F32)
    totals = [zeros(1), zeros(1)]
    texts = []
    for i in range(items):
        for source, target in ((tokens, tok), (out_grad, grad)):
            whole = source[i].astype(F32)
            patch, text = whole[:patches], whole[patches:]
            full = jnp.concatenate([patch, zeros(TEXT_AT - patches), text, zeros(tail)], axis=0)
            target[pl.ds(i * ITEM, ITEM), :] = full.astype(BF)
            if target is grad:
                grad_v[pl.ds(i * TEXT_AT, TEXT_AT), :] = full[:TEXT_AT].astype(BF)
                texts.append(text)
                totals[0] = totals[0] + jnp.sum(patch, axis=0, keepdims=True)
                totals[1] = totals[1] + jnp.sum(text, axis=0, keepdims=True)
    slots = jnp.concatenate(texts, axis=0).astype(BF)
    grad_t[...] = slots
    sums[0:1, :] = totals[0]
    sums[1:2, :] = totals[1]
    out_copy[...] = w_out[...]
    down_copy[...] = down[...]
    chip = info[0] // 2
    side = chip % 2
    block = up.shape[0]
    pair = 2 * down.shape[0]
    strip = lambda ref, c: ref[:, pl.ds(pl.multiple_of(c * pair, 128), pair)]
    for k in range(2):
        up_mine[:, k * pair : (k + 1) * pair] = strip(up, side + 2 * k)
        up_other[:, k * pair : (k + 1) * pair] = strip(up, 1 - side + 2 * k)
    strip0[...] = strip(text_up, chip)
    for k, target in ((1, te1), (2, te2), (3, te3)):
        target[pl.ds(0, block), :] = strip(text_up, chip ^ k)
        target[pl.ds(block, slots.shape[0]), :] = slots


def norm_kernel(info, tok, mask, even, odd, *refs):
    n1, vec, up_bias, shards = refs[-4:]
    me = info[0]
    total, width = tok.shape
    block = width // 8
    for slot in range(8):
        shards[me ^ slot] = (even, odd)[slot % 2][slot // 2]
    wide = jnp.concatenate([shards[b] for b in range(8)], axis=1)
    lane = lax.broadcasted_iota(jnp.int32, (1024, width), 0)
    to = lax.broadcasted_iota(jnp.int32, (1024, width), 1)
    spread = ((lane // 128) * block + lane % 128 == to) & (lane % 128 < block)
    vec[...] = dot_nn(wide, jnp.where(spread, 1.0, 0.0).astype(BF))
    hid = up_bias.shape[1] // 4
    for q in range(4):
        b = (q // 2) * 4 + q % 2 + ((me // 2) % 2) * 2
        for r in range(hid // 128):
            at = q * hid + r * 128
            up_bias[0:1, at : at + 128] = shards[b, 10 + r : 11 + r, :].astype(F32)

    @pl.loop(0, total // 64)
    def _(step):
        rows = pl.ds(pl.multiple_of(step * 64, 64), 64)
        normal, _unused = normalize(mixed_in(tok, mask, vec, rows))
        n1[rows, :] = (normal * vec[1:2, :] + vec[2:3, :]).astype(BF)


def qkv_kernel(slots, info, n1, vec, *refs):
    count = len(slots)
    pieces = refs[:count]
    qkv, weight, bias, sems = refs[-4:]
    width = n1.shape[1]
    copies = start_rows([(s, f, r) for (s, f), r in zip(slots, pieces)], weight, info[0], sems)
    bias[0:1, 0:width] = vec[3:4, :]
    bias[0:1, width : 2 * width] = jnp.zeros((1, width), F32)
    bias[0:1, 2 * width : 3 * width] = vec[4:5, :]
    for copy in copies:
        copy.wait()

    @pl.loop(0, 3 * width // 256)
    def _(step):
        cols = pl.ds(pl.multiple_of(step * 256, 256), 256)
        factor = jnp.where(step < width // 256, 0.125, 1.0).astype(F32)
        out = dot_nn(n1[...], weight[:, cols])
        qkv[:, cols] = ((out + bias[0:1, cols]) * factor).astype(BF)


def attn_kernel(info, qkv, *refs):
    probs, ctx = refs[-2:]
    total, width = ctx.shape
    items = total // ITEM
    pairs = width // 128
    patches = info[3]

    @pl.loop(0, items * pairs)
    def _(step):
        item, pair = step // pairs, step % pairs
        rows = pl.ds(pl.multiple_of(item * ITEM, ITEM), ITEM)
        lane = lambda part: pl.ds(pl.multiple_of(part * width + pair * 128, 128), 128)
        q2, k2, v2 = qkv[rows, lane(0)], qkv[rows, lane(1)], qkv[rows, lane(2)]
        low = lax.broadcasted_iota(jnp.int32, (ITEM, 128), 1) < HEAD_DIM
        zero = jnp.zeros_like(q2)
        both = jnp.concatenate([jnp.where(low, q2, zero), jnp.where(low, zero, q2)], axis=0)
        scores = dot_nt(both, k2)
        col = lax.broadcasted_iota(jnp.int32, (1, ITEM), 1)
        valid = (col < patches) | ((col >= TEXT_AT) & (col < TEXT_AT + info[1 + item]))
        scores = jnp.where(valid, scores, -1000000000.0)
        expo = jnp.exp(scores - jnp.max(scores, axis=-1, keepdims=True))
        prob = (expo * (1.0 / jnp.sum(expo, axis=-1, keepdims=True))).astype(BF)
        probs[step] = prob
        wide = jnp.concatenate([prob[:ITEM], prob[ITEM:]], axis=1)
        values = jnp.concatenate([jnp.where(low, v2, zero), jnp.where(low, zero, v2)], axis=0)
        ctx[rows, pl.ds(pl.multiple_of(pair * 128, 128), 128)] = dot_nn(wide, values).astype(BF)


def out_kernel(text_rows, info, tok, mask, vec, ctx, out_w, *refs):
    h1, n2t, *n2v = refs[-2 - tok.shape[0] // ITEM :]
    items = tok.shape[0] // ITEM
    texts = []
    for i in range(items):
        for at, size in ((0, TEXT_AT), (TEXT_AT, ITEM - TEXT_AT)):
            rows = pl.ds(i * ITEM + at, size)
            attended = dot_nn(ctx[rows, :], out_w[...]) + vec[5:6, :]
            hidden = mixed_in(tok, mask, vec, rows) + attended
            h1[rows, :] = hidden
            normal, _unused = normalize(hidden)
            second = normal * vec[6:7, :] + vec[7:8, :]
            if at == 0:
                n2v[i][...] = second.astype(BF)
            else:
                texts.append(second[:text_rows])
    n2t[...] = jnp.concatenate(texts, axis=0).astype(BF)


def pack_kernel(info, strip0, te1, te2, te3, grad_t, pack):
    block, hid = strip0.shape[0], strip0.shape[1] // 2
    rows = grad_t.shape[0]
    other = pl.ds(pl.multiple_of((1 - info[0] % 2) * hid, 128), hid)
    for k, ref in enumerate((strip0, te1, te2, te3)):
        at = (k // 2) * block
        pack[at : at + block, (k % 2) * hid : (k % 2 + 1) * hid] = ref[pl.ds(0, block), other]
        there = pl.ds(2 * block + k * rows, rows)
        pack[there, :] = grad_t[...] if k == 0 else ref[pl.ds(block, rows), :]


def up_rows(me, pieces, target, sems):
    block = target.shape[0] // 8
    copies = []
    for index, (base, ref) in enumerate(pieces):
        for k in range(2):
            row = pl.multiple_of((me ^ (base + 2 * k)) * block, 16)
            sem = sems.at[2 * index + k]
            copies.append(pltpu.make_async_copy(ref.at[k], target.at[pl.ds(row, block)], sem))
    for copy in copies:
        copy.start()
    return copies


def place_of(me):
    return (me // 4) * 2 + me % 2


def vision_kernel(pair, items, info, grad, up_bias, *refs):
    parts, refs = refs[:items], refs[items:]
    ups, downs = refs[:4], refs[4:6]
    branch, gn2, act, low, up_w, down_w, rows_in, sems = refs[-8:]
    me = info[0]
    block = downs[0].shape[1]
    copies = up_rows(me, list(zip((0, 4, 1, 5), ups)), up_w, sems)
    place = place_of(me)
    for j in range(4):
        row = pl.multiple_of((place ^ j) * block, 16)
        copy = pltpu.make_async_copy(downs[j % 2].at[j // 2], down_w.at[pl.ds(row, block)], sems.at[8 + j])
        copy.start()
        copies.append(copy)
    for copy in copies:
        copy.wait()
    mine = grad.at[(me // 2) % 2 ^ 1] if pair else grad
    for i, part in enumerate(parts):
        rows_in[pl.ds(i * TEXT_AT, TEXT_AT), :] = part[...]
    chunk = 512
    for step in range(down_w.shape[0] // chunk):
        cols = slice(step * chunk, (step + 1) * chunk)
        upper = dot_nn(rows_in[...], up_w[:, cols]) + up_bias[0:1, cols]
        active, slope = gelu_parts(upper)
        active = active.astype(BF)
        act[:, cols] = active
        back = (dot_nt(mine[...], down_w[cols, :]) * slope).astype(BF)
        low[:, cols] = back
        if step == 0:
            sum_branch = dot_nn(active, down_w[cols, :])
            sum_gn2 = dot_nt(back, up_w[:, cols])
        else:
            sum_branch = sum_branch + dot_nn(active, down_w[cols, :])
            sum_gn2 = sum_gn2 + dot_nt(back, up_w[:, cols])
    branch[...] = sum_branch.astype(branch.dtype)
    gn2[...] = sum_gn2.astype(gn2.dtype)


def vision_grad_kernel(items, info, *refs):
    ins = refs[:items], refs[items : 2 * items]
    grads, refs = refs[2 * items], refs[2 * items + 1 :]
    acts, lows = refs[:2], refs[2:4]
    up_keep, up_send, down_keep, down_send, bias_sums = refs[-11:-6]
    left_t, act_t, right, low, turn0, turn1 = refs[-6:]
    me = info[0]
    rows, width = items * ins[0][0].shape[0], ins[0][0].shape[1]
    block = width // 8
    half = down_keep.shape[1]
    place, core = place_of(me), me % 2
    for k in range(2):
        at = pl.ds(k * rows, rows)
        right[at, :] = grads[(me // 2) % 2 ^ k]
        low[at, :] = lows[k][...]
        turned = jnp.concatenate([ref[...] for ref in ins[k]], axis=0).T
        turn = (turn0, turn1)[k]
        for b in range(8):
            spot = pl.multiple_of((me ^ b) * block, 16)
            turn[pl.ds(spot, block), :] = turned[b * block : (b + 1) * block]
        left_t[:, at] = turn[...]
        act_t[:, at] = acts[k][...].T
    chunk = 512
    for step in range(4 * half // chunk):
        cols = slice(step * chunk, (step + 1) * chunk)
        grad_up = dot_nn(left_t[...], low[:, cols])
        bias_sums[0:1, cols] = jnp.sum(low[:, cols].astype(F32), axis=0, keepdims=True)
        grad_up = grad_up.astype(BF)
        for b in range(4):
            up_keep[b, :, cols] = grad_up[2 * b * block : (2 * b + 1) * block]
            up_send[b, :, cols] = grad_up[(2 * b + 1) * block : (2 * b + 2) * block]
    for q in range(4):
        grad_down = dot_nn(act_t[q * half : (q + 1) * half, :], right[...]).astype(BF)
        side = (q // 2) ^ (place // 2)

        @pl.when(core == q % 2)
        def _():
            down_keep[side] = grad_down

        @pl.when(core != q % 2)
        def _():
            down_send[side] = grad_down


def text_kernel(info, down, up_bias, strip0, te1, te2, te3, far, even, odd, *refs):
    grad0, refs = refs[0], refs[1:]
    branch_keep, branch_send, gn2_keep, gn2_send, up_keep, up_send, grad_down, bias_sums = refs[-12:-4]
    up_w, left, right, left_t = refs[-4:]
    me = info[0]
    width = down.shape[1]
    hid = down.shape[0]
    block = width // 8
    rows = even.shape[1]
    mine = pl.ds(pl.multiple_of((me % 2) * hid, 128), hid)
    spot = lambda slot: pl.ds(pl.multiple_of((me ^ slot) * block, 16), block)
    up_w[spot(0), :] = strip0[:, mine]
    for s, te in ((2, te1), (4, te2), (6, te3)):
        up_w[spot(s), :] = te[pl.ds(0, block), mine]
        right[pl.ds(s * rows, rows), :] = te[pl.ds(block, rows), :]
    up_w[spot(1), :] = far[pl.ds(0, block), pl.ds(0, hid)]
    up_w[spot(3), :] = far[pl.ds(0, block), pl.ds(hid, hid)]
    up_w[spot(5), :] = far[pl.ds(block, block), pl.ds(0, hid)]
    up_w[spot(7), :] = far[pl.ds(block, block), pl.ds(hid, hid)]
    right[pl.ds(0, rows), :] = grad0[...]
    for k in range(4):
        right[pl.ds((2 * k + 1) * rows, rows), :] = far[pl.ds(2 * block + k * rows, rows), :]
    for slot in range(8):
        left[pl.ds(slot * rows, rows), :] = (even, odd)[slot % 2][slot // 2]
    turned = left[...].T
    for b in range(8):
        left_t[spot(b), :] = turned[b * block : (b + 1) * block]
    upper = dot_nn(left[...], up_w[...]) + up_bias[...]
    active, slope = gelu_parts(upper)
    act = active.astype(BF)
    low = (dot_nt(right[...], down[...]) * slope).astype(BF)
    bias_sums[...] = jnp.sum(low.astype(F32), axis=0, keepdims=True)
    gn2 = dot_nt(low, up_w[...]).astype(BF)
    branch = dot_nn(act, down[...]).astype(BF)
    for s in range(4):
        gn2_keep[s] = gn2[2 * s * rows : (2 * s + 1) * rows]
        gn2_send[s] = gn2[(2 * s + 1) * rows : (2 * s + 2) * rows]
        branch_keep[s] = branch[2 * s * rows : (2 * s + 1) * rows]
        branch_send[s] = branch[(2 * s + 1) * rows : (2 * s + 2) * rows]
    grad_down[...] = dot_tn(act, right[...]).astype(BF)
    grad_up = dot_nn(left_t[...], low).astype(BF)
    for b in range(4):
        up_keep[b] = grad_up[2 * b * block : (2 * b + 1) * block]
        up_send[b] = grad_up[(2 * b + 1) * block : (2 * b + 2) * block]


def attn_bwd_kernel(text_rows, info, gn2v, gn2x, t0, t1, t2, t3, grad, h1, vec, qkv, probs, weight, *refs):
    gh1, low, stacked, sums, gn2, gctx = refs[-6:]
    total, width = h1.shape
    items = total // ITEM
    text = (
        t0[0].astype(F32) + t1[...].astype(F32) + t2[...].astype(F32) + t3[...].astype(F32)
    )
    for i in range(items):
        part = pl.ds(i * TEXT_AT, TEXT_AT)
        gn2[pl.ds(i * ITEM, TEXT_AT), :] = gn2v[part, :] + gn2x[part, :].astype(F32)
        gn2[pl.ds(i * ITEM + TEXT_AT, text_rows), :] = text[i * text_rows : (i + 1) * text_rows]
        pad = ITEM - TEXT_AT - text_rows
        gn2[pl.ds(i * ITEM + TEXT_AT + text_rows, pad), :] = jnp.zeros((pad, width), F32)
    sums[...] = jnp.zeros_like(sums)

    @pl.loop(0, total // 64)
    def _(step):
        rows = pl.ds(pl.multiple_of(step * 64, 64), 64)
        normal, scale = normalize(h1[rows, :])
        above = gn2[rows, :]
        inner = above * vec[6:7, :]
        back = scale * (
            inner
            - jnp.mean(inner, axis=-1, keepdims=True)
            - normal * jnp.mean(inner * normal, axis=-1, keepdims=True)
        )
        out = grad[rows, :].astype(F32)
        hidden = out + back
        gh1[rows, :] = hidden
        low[rows, :] = hidden.astype(BF)
        sums[0:1, :] += jnp.sum(above * normal, axis=0, keepdims=True)
        sums[1:2, :] += jnp.sum(above, axis=0, keepdims=True)
        sums[2:3, :] += jnp.sum(hidden.astype(BF).astype(F32), axis=0, keepdims=True)

    gctx[...] = dot_nt(low[...], weight[...]).astype(BF)
    pairs = width // 128

    @pl.loop(0, items * pairs)
    def _(step):
        item, pair = step // pairs, step % pairs
        rows = pl.ds(pl.multiple_of(item * ITEM, ITEM), ITEM)
        lane = lambda part: pl.ds(pl.multiple_of(part * width + pair * 128, 128), 128)
        q2, k2, v2 = qkv[rows, lane(0)], qkv[rows, lane(1)], qkv[rows, lane(2)]
        g2 = gctx[rows, pl.ds(pl.multiple_of(pair * 128, 128), 128)]
        lower = lax.broadcasted_iota(jnp.int32, (ITEM, 128), 1) < HEAD_DIM
        zero = jnp.zeros_like(q2)
        split = lambda a: jnp.concatenate([jnp.where(lower, a, zero), jnp.where(lower, zero, a)], axis=0)
        both_g = split(g2)
        prob_b = probs[step]
        prob = prob_b.astype(F32)
        gprob = dot_nt(both_g, v2)
        weighted = prob * gprob
        gscore = (weighted - prob * jnp.sum(weighted, axis=-1, keepdims=True)).astype(BF)
        stacked[rows, lane(2)] = dot_tn(prob_b, both_g).astype(BF)
        stacked[rows, lane(1)] = dot_tn(gscore, split(q2)).astype(BF)
        wide = jnp.concatenate([gscore[:ITEM], gscore[ITEM:]], axis=1)
        gquery = dot_nn(wide, split(k2)).astype(BF).astype(F32) * 0.125
        stacked[rows, lane(0)] = gquery.astype(BF)

    for part in (0, 2):
        cols = stacked[:, part * width : (part + 1) * width].astype(F32)
        sums[3 + part // 2 : 4 + part // 2, :] = jnp.sum(cols, axis=0, keepdims=True)


def attn_grad_kernel(last, info, left, stacked, other_left, other, *refs):
    me = info[0]
    width = left.shape[1]
    block = width // 8
    keep, send, left_t, other_t = refs[-4:]
    first = 2 if last else 0
    for source, target in ((left, left_t), (other_left, other_t))[:2] if last else ((left, left_t),):
        turned = source[...].T
        for b in range(8):
            place = pl.multiple_of((me ^ b) * block, 16)
            target[pl.ds(place, block), :] = turned[b * block : (b + 1) * block]
    for part in range(2):
        cols = slice(part * width, (part + 1) * width)
        if last and part == 1:
            value = dot_nn(other_t[...], other[...]).astype(BF)
        else:
            right = stacked[:, (first + part) * width : (first + part + 1) * width]
            value = dot_nn(left_t[...], right).astype(BF)
        for b in range(4):
            keep[b, :, cols] = value[2 * b * block : (2 * b + 1) * block]
            send[b, :, cols] = value[(2 * b + 1) * block : (2 * b + 2) * block]


def last_kernel(slots, info, stacked, gh1, tok, mask, vec, *refs):
    count = len(slots)
    pieces = refs[:count]
    gtok, sums, weight, sems = refs[-4:]
    copies = start_rows([(s, f, r) for (s, f), r in zip(slots, pieces)], weight, info[0], sems)
    sums[...] = jnp.zeros_like(sums)
    for copy in copies:
        copy.wait()

    @pl.loop(0, tok.shape[0] // 128)
    def _(step):
        rows = pl.ds(pl.multiple_of(step * 128, 128), 128)
        above = dot_nt(stacked[rows, :], weight[...])
        normal, scale = normalize(mixed_in(tok, mask, vec, rows))
        inner = above * vec[1:2, :]
        back = scale * (
            inner
            - jnp.mean(inner, axis=-1, keepdims=True)
            - normal * jnp.mean(inner * normal, axis=-1, keepdims=True)
        )
        hidden = gh1[rows, :] + back
        keep = mask[rows, :]
        gtok[rows, :] = hidden * (1.0 - keep)
        sums[0:1, :] += jnp.sum(hidden * keep, axis=0, keepdims=True)
        sums[1:2, :] += jnp.sum(above * normal, axis=0, keepdims=True)
        sums[2:3, :] += jnp.sum(above, axis=0, keepdims=True)


def call(kernel, outs, scratch, args, pieces=(), us=1):
    in_specs = [pl.BlockSpec(memory_space=pltpu.SMEM)]
    in_specs += [pl.BlockSpec(memory_space=pltpu.VMEM)] * (len(args) - 1)
    in_specs += [pl.BlockSpec(memory_space=pl.ANY)] * len(pieces)
    return pl.pallas_call(
        kernel,
        out_shape=[jax.ShapeDtypeStruct(s, d) for s, d in outs],
        in_specs=in_specs,
        out_specs=[pl.BlockSpec(memory_space=pltpu.VMEM)] * len(outs),
        scratch_shapes=scratch,
        compiler_params=pltpu.CompilerParams(vmem_limit_bytes=VMEM_LIMIT),
        cost_estimate=pl.CostEstimate(flops=int(us * SCALE * 1.1e9), bytes_accessed=int(us * SCALE * 1e6), transcendentals=0),
    )(*args, *pieces)


def swap(array, mask):
    return lax.ppermute(array, "fsdp", [(i, i ^ mask) for i in range(8)])


def along_rep(array, pairs):
    return lax.ppermute(array, "rep", pairs)


def add(*terms):
    out = terms[0].astype(F32)
    for term in terms[1:]:
        out = out + term.astype(F32)
    return out.astype(BF)


def planned(
    tokens,
    out_grad,
    masked,
    lengths,
    mask_vec,
    norm1_gain,
    norm1_shift,
    w_qkv,
    query_bias,
    value_bias,
    w_out,
    out_bias,
    norm2_gain,
    norm2_shift,
    vision_up,
    vision_up_bias,
    vision_down,
    vision_down_bias,
    text_up,
    text_up_bias,
    text_down,
    text_down_bias,
):
    items, row_count, width = tokens.shape
    text_rows = masked.shape[1]
    patches = row_count - text_rows
    block = width // 8
    half = block // 2
    hid = vision_down.shape[0]
    pair = 2 * hid
    hidden = 8 * hid
    total = items * ITEM
    vision_rows = items * TEXT_AT
    slot_rows = items * text_rows
    te_rows = block + slot_rows
    me = lax.axis_index("fsdp").astype(jnp.int32)
    rep = lax.axis_index("rep").astype(jnp.int32)
    core, chip, side = me % 2, me // 2, (me // 2) % 2
    sem = lambda n: pltpu.SemaphoreType.DMA((n,))
    quad = lambda r, c: ((4, r, c), BF)

    names = (
        mask_vec,
        norm1_gain,
        norm1_shift,
        query_bias,
        value_bias,
        out_bias,
        norm2_gain,
        norm2_shift,
        vision_down_bias,
        text_down_bias,
    )
    own_vec = jnp.pad(jnp.stack(names), ((0, 0), (0, 128 - block)))
    own_vec = jnp.concatenate([own_vec, vision_up_bias.reshape(-1, 128)], axis=0)
    own_vec = jnp.pad(own_vec, ((0, 16 - own_vec.shape[0]), (0, 0)))[None]
    vx, vy, vxy = swap(own_vec, 2), swap(own_vec, 4), swap(own_vec, 6)
    qx, qy = swap(w_qkv, 2), swap(w_qkv, 4)
    mask = jnp.concatenate(
        [
            jnp.zeros((items, TEXT_AT), F32),
            masked.astype(F32),
            jnp.zeros((items, ITEM - TEXT_AT - text_rows), F32),
        ],
        axis=1,
    ).reshape(total, 1)
    info = jnp.concatenate([me[None], lengths, jnp.full((1,), patches, jnp.int32)])
    tok, grad, grad_v, grad_t, grad_sums, own_out, own_down, up_mine, up_other, strip0, te1, te2, te3 = call(
        functools.partial(prep_kernel, text_rows),
        [
            ((total, width), BF),
            ((total, width), BF),
            ((vision_rows, width), BF),
            ((slot_rows, width), BF),
            ((2, width), F32),
            ((block, width), BF),
            ((hid, width), BF),
            ((block, 2 * pair), BF),
            ((block, 2 * pair), BF),
            ((block, pair), BF),
            ((te_rows, width), BF),
            ((te_rows, width), BF),
            ((te_rows, width), BF),
        ],
        [],
        [info, tokens, out_grad, w_out, vision_down, vision_up, text_up],
        us=5,
    )
    vec_four = jnp.concatenate([own_vec, vx, vy, vxy], axis=0)
    vec_arrays = [vec_four, swap(vec_four, 1)]
    part1, part2 = gate([qx[:half], qy[half:]], [tok, vec_arrays[1]])

    far1, far2 = swap(part1, 4), swap(part2, 2)
    near = [swap(a, 1) for a in (w_qkv, qx, qy)]
    n1, vec, up_bias = call(
        norm_kernel,
        [((total, width), BF), ((16, width), F32), ((1, 4 * hid), F32)],
        [pltpu.VMEM((8, 16, 128), BF)],
        [info, tok, mask, *vec_arrays],
        [part1],
        us=5,
    )
    far1, far2, up_other, own_down, own_out, grad_v = gate(
        [far1, far2, up_other, own_down, own_out, grad_v], [n1, *near]
    )
    out_all = lax.all_gather(own_out, "fsdp", tiled=True)
    attn = [(0, 0, w_qkv), (2, 0, qx), (4, 0, qy), (6, 0, far1), (6, half, far2)]
    attn += [(1, 0, near[0]), (3, 0, near[1]), (5, 0, near[2]), (7, 0, swap(far1, 1)), (7, half, swap(far2, 1))]
    attn_slots = tuple((p[0], p[1]) for p in attn)
    attn_arrays = [p[2] for p in attn]

    up_x, down_y = swap(up_other, 2), swap(own_down, 4)
    (qkv,) = call(
        functools.partial(qkv_kernel, attn_slots),
        [((total, 3 * width), BF)],
        [pltpu.VMEM((width, 3 * width), BF), pltpu.VMEM((1, 3 * width), F32), sem(len(attn))],
        [info, n1, vec],
        attn_arrays,
        us=8,
    )
    t = tick([qkv, up_x, down_y])

    up_x, down_y, te1, te2, te3 = gate([up_x, down_y, te1, te2, te3], [t])
    up_two = jnp.stack([up_mine, up_x])
    up_y, up_c = swap(up_two, 4), swap(up_two, 1)
    te1, te3 = swap(te1, 2), swap(te3, 6)
    probs, ctx = call(
        attn_kernel,
        [((items * width // 128, 2 * ITEM, ITEM), BF), ((total, width), BF)],
        [],
        [info, qkv],
        [t],
        us=10,
    )
    t = tick([ctx, up_y, up_c, te1, te3])

    up_y, te1, te2, te3, down_y = gate([up_y, te1, te2, te3, down_y], [t])
    te2 = swap(te2, 4)
    down_two = jnp.stack([own_down, down_y])
    up_yc, down_c = swap(up_y, 1), swap(down_two, 1)
    h1, n2t, *n2v = call(
        functools.partial(out_kernel, text_rows),
        [((total, width), F32), ((slot_rows, width), BF)] + [((TEXT_AT, width), BF)] * items,
        [],
        [info, tok, mask, vec, ctx, out_all],
        [t],
        us=5,
    )
    t = tick([n2t, te2, up_yc, down_c])

    te1, te2, te3, n2t_sent, *n2v_sent = gate([te1, te2, te3, n2t, *n2v], [t])
    (pack,) = call(
        pack_kernel,
        [((2 * block + 4 * slot_rows, width), BF)],
        [],
        [info, strip0, te1, te2, te3, grad_t],
    )
    text_in = [swap(n2t_sent, 2), swap(n2t_sent, 4), swap(n2t_sent, 6)]
    n2x = [swap(n2v_sent[0], 2)]
    far = swap(pack, 1)
    weights = [up_two, up_y, up_c, up_yc, down_two, down_c]

    def vision(rows_in, grads, kind, after):
        return call(
            functools.partial(vision_kernel, kind == BF, items),
            [
                ((vision_rows, width), kind),
                ((vision_rows, width), kind),
                ((vision_rows, 4 * hid), BF),
                ((vision_rows, 4 * hid), BF),
            ],
            [
                pltpu.VMEM((width, 4 * hid), BF),
                pltpu.VMEM((4 * hid, width), BF),
                pltpu.VMEM((vision_rows, width), BF),
                sem(12),
            ],
            [info, grads, up_bias, *rows_in],
            [*weights, *after],
            us=9,
        )

    branch_own, gn2_own, act_own, low_own = vision(n2v, grad_v, F32, [pack])
    pairs = [[0, 2], [1, 3], [4, 6], [5, 7]]
    grad_pair = lax.all_gather(grad_v, "fsdp", axis_index_groups=pairs)
    t = tick([gn2_own, *text_in, n2x[0], far])

    far, *rest = gate([far, *text_in, *n2v_sent[1:]], [t])
    text_four = jnp.stack([n2t, *rest[:3]])
    text_odd = swap(text_four, 1)
    n2x += [swap(a, 2) for a in rest[3:]]
    branch_keep, branch_send, gn2_keep, gn2_send, tu_keep, tu_send, td, text_bias_sum = call(
        text_kernel,
        [
            quad(slot_rows, width),
            quad(slot_rows, width),
            quad(slot_rows, width),
            quad(slot_rows, width),
            quad(block, hid),
            quad(block, hid),
            ((hid, width), BF),
            ((1, hid), F32),
        ],
        [
            pltpu.VMEM((width, hid), BF),
            pltpu.VMEM((8 * slot_rows, width), BF),
            pltpu.VMEM((8 * slot_rows, width), BF),
            pltpu.VMEM((width, 8 * slot_rows), BF),
        ],
        [
            info,
            text_down,
            text_up_bias.astype(F32).reshape(1, hid),
            strip0,
            te1,
            te2,
            te3,
            far,
            text_four,
            text_odd,
            grad_t,
        ],
        us=6,
    )
    t = tick([gn2_keep, *n2x, grad_pair])

    gn2_send, *n2x = gate([gn2_send, *n2x], [t])
    gn2_sum = add(gn2_keep, swap(gn2_send, 1))
    gn2_text = [gn2_sum] + [swap(gn2_sum[s], 2 * s) for s in (1, 2, 3)]
    branch_x, gn2_x, act_x, low_x = vision(n2x, grad_pair, BF, [gn2_sum])
    t = tick([gn2_x, *gn2_text[1:]])

    (gn2_x,) = gate([gn2_x], [t])
    gn2_back = swap(gn2_x, 2)
    vu_keep, vu_send, vd_keep, vd_send, vu_bias_sum = call(
        functools.partial(vision_grad_kernel, items),
        [
            quad(block, 4 * hid),
            quad(block, 4 * hid),
            ((2, hid, width), BF),
            ((2, hid, width), BF),
            ((1, 4 * hid), F32),
        ],
        [
            pltpu.VMEM((width, 2 * vision_rows), BF),
            pltpu.VMEM((4 * hid, 2 * vision_rows), BF),
            pltpu.VMEM((2 * vision_rows, width), BF),
            pltpu.VMEM((2 * vision_rows, 4 * hid), BF),
            pltpu.VMEM((width, vision_rows), BF),
            pltpu.VMEM((width, vision_rows), BF),
        ],
        [info, *n2v, *n2x, grad_pair, act_own, act_x, low_own, low_x],
        [t],
        us=12,
    )
    t = tick([vu_bias_sum, gn2_back])

    vu_send, vd_send, branch_x, branch_send, gn2_back = gate([vu_send, vd_send, branch_x, branch_send, gn2_back], [t])
    vu_got, vd_got = swap(vu_send, 1), swap(vd_send, 1)
    vd_near, vd_far = add(vd_keep[0], vd_got[0]), add(vd_keep[1], vd_got[1])
    vu_far = [add(vu_keep[k], vu_got[k]) for k in (2, 3)]
    vd_y, vu_y1 = swap(vd_far, 4), swap(vu_far[1], 4)
    branch_back = swap(branch_x, 2)
    branch_got = swap(branch_send, 1)
    gh1, low_attn, stacked, sums_two = call(
        functools.partial(attn_bwd_kernel, text_rows),
        [((total, width), F32), ((total, width), BF), ((total, 3 * width), BF), ((8, width), F32)],
        [pltpu.VMEM((total, width), F32), pltpu.VMEM((total, width), BF)],
        [info, gn2_own, gn2_back, *gn2_text, grad, h1, vec, qkv, probs, out_all],
        [vd_far, *vu_far],
        us=18,
    )
    t = tick([stacked, vd_y, vu_y1, branch_back, branch_got])

    vd_y, vu_y1, vu_far0, branch_got = gate([vd_y, vu_y1, vu_far[0], branch_got], [t])
    vd = lax.psum(add(vd_near, vd_y), "rep", axis_index_groups=[[1, 0, 2, 3]])
    vu_x = swap(add(vu_keep[1], vu_got[1], vu_y1), 2)
    vu_y0 = swap(vu_far0, 4)

    def attn_grads(last, after):
        return call(
            functools.partial(attn_grad_kernel, last),
            [quad(block, 2 * width), quad(block, 2 * width)],
            [pltpu.VMEM((width, total), BF), pltpu.VMEM((width, total), BF)],
            [info, n1, stacked, ctx, low_attn],
            after,
            us=5,
        )

    a_keep, a_send = attn_grads(False, [t])
    t = tick([a_keep, vu_x, vu_y0])
    (a_send,) = gate([a_send], [t])
    a_got = swap(a_send, 1)
    branch_sum = add(branch_keep, branch_got)
    vu_both = jnp.stack([add(vu_keep[0], vu_got[0], vu_y0), vu_x])
    vu = lax.psum(vu_both, "rep", axis_index_groups=[[0, 1, 3, 2]])
    b_keep, b_send = attn_grads(True, [t])
    t = tick([b_keep, a_got])
    a_got, b_send, branch_sum = gate([a_got, b_send, branch_sum], [t])
    b_got = swap(b_send, 1)

    def begin(keep, got, one):
        i = one // 2
        return add(jnp.stack([keep[i], keep[3]]), jnp.stack([got[i], got[3]]))

    a_first, b_first = begin(a_keep, a_got, 2), begin(b_keep, b_got, 4)
    a_there, b_there = swap(a_first, 2), swap(b_first, 4)
    branch_t = [branch_sum] + [swap(branch_sum[s], 2 * s) for s in (1, 2, 3)]
    gtok, sums_one = call(
        functools.partial(last_kernel, attn_slots),
        [((total, width), F32), ((8, width), F32)],
        [pltpu.VMEM((width, 3 * width), BF), sem(len(attn))],
        [info, stacked, gh1, tok, mask, vec],
        attn_arrays + [a_first, b_first],
        us=12,
    )
    t = tick([sums_one, a_there, b_there, *branch_t[1:]])

    a_there, b_there, sums_one = gate([a_there, b_there, sums_one], [t])
    a_beyond = swap(add(a_keep[2], a_got[2], a_there[1]), 4)
    b_beyond = swap(add(b_keep[1], b_got[1], b_there[1]), 2)
    ga = add(a_keep[0], a_got[0], a_there[0], a_beyond)
    gb = add(b_keep[0], b_got[0], b_there[0], b_beyond)

    inner = (rep == 1) | (rep == 2)

    def rep_sum(array):
        part = add(array, along_rep(array, [(0, 1), (3, 2)]))
        whole = add(part, along_rep(part, [(1, 2), (2, 1)]))
        return jnp.where(inner, whole, along_rep(whole, [(1, 0), (2, 3)]))

    ga, gb = rep_sum(ga), rep_sum(gb)
    tu_keep, tu_send, td = lax.psum((tu_keep, tu_send, td), "rep")
    tu_keep, tu_send, td = gate([tu_keep, tu_send, td], [t])
    tu_got = swap(tu_send, 1)
    tu_wide = jnp.where(
        core == 0,
        jnp.concatenate([tu_keep, tu_got], axis=-1),
        jnp.concatenate([tu_got, tu_keep], axis=-1),
    )
    tu_all = [tu_wide[0]] + [swap(tu_wide[s], 2 * s) for s in (1, 2, 3)]
    tu_x = [jnp.where(side == 0, tu_all[k], tu_all[k ^ 1]) for k in range(4)]
    tu_y = [jnp.where(me // 4 == 0, tu_x[k], tu_x[k ^ 2]) for k in range(4)]
    grad_text_up = jnp.concatenate(tu_y, axis=1).astype(F32)
    grad_text_down = td.astype(F32)

    vu_sum = vu_bias_sum.reshape(2, 1, pair)
    vu_sum = jnp.where(
        side == 0,
        jnp.concatenate([vu_sum, jnp.zeros_like(vu_sum)], axis=1),
        jnp.concatenate([jnp.zeros_like(vu_sum), vu_sum], axis=1),
    )
    vu_sum = vu_sum.reshape(8, hid // block, block).transpose(1, 0, 2).reshape(-1, width)
    flat = jnp.concatenate(
        [sums_one[0:3], sums_two[3:5], sums_two[2:3], sums_two[0:2], grad_sums, vu_sum], axis=0
    )
    for m in (1, 2, 4):
        flat = flat + swap(flat, m)
    mine = lax.dynamic_slice_in_dim(flat, me * block, block, axis=1)
    mine = jnp.concatenate([mine, text_bias_sum.reshape(-1, block)], axis=0)
    for m in (1, 2):
        mine = mine + along_rep(mine, [(i, i ^ m) for i in range(4)])
    count = len(names)
    rows = hid // block
    vec_grad = [mine[i] for i in range(count)]
    vu_bias_grad = mine[count : count + rows].reshape(-1)
    tu_bias_grad = mine[count + rows : count + 2 * rows].reshape(-1)

    vu, vd = gate([vu, vd], [ga, gb])
    ga, gb = ga.astype(F32), gb.astype(F32)
    grad_w_qkv = jnp.concatenate([ga, gb[:, :width]], axis=1)
    grad_w_out = gb[:, width:]
    vu_s = [jnp.where(side == 0, vu[k], vu[1 - k]) for k in range(2)]
    grad_vision_up = jnp.concatenate(
        [vu_s[0][:, :pair], vu_s[1][:, :pair], vu_s[0][:, pair:], vu_s[1][:, pair:]], axis=1
    ).astype(F32)
    grad_vision_down = vd.astype(F32)
    h1 = h1.reshape(items, ITEM, width)
    branch_v = (branch_own + branch_back.astype(F32)).reshape(items, TEXT_AT, width)[:, :patches]
    mixed_v = h1[:, :patches] + branch_v + vec[8][None, None]
    branch_t = branch_t[0][0].astype(F32) + sum(b.astype(F32) for b in branch_t[1:])
    branch_t = branch_t.reshape(items, text_rows, width)
    mixed_t = h1[:, TEXT_AT : TEXT_AT + text_rows] + branch_t + vec[9][None, None]
    mixed = jnp.concatenate([mixed_v.astype(BF), mixed_t.astype(BF)], axis=1)
    gtok = gtok.reshape(items, ITEM, width)
    grad_tokens = jnp.concatenate(
        [gtok[:, :patches], gtok[:, TEXT_AT : TEXT_AT + text_rows]], axis=1
    )
    return (
        mixed,
        grad_tokens,
        vec_grad[0],
        vec_grad[1],
        vec_grad[2],
        grad_w_qkv,
        vec_grad[3],
        vec_grad[4],
        grad_w_out,
        vec_grad[5],
        vec_grad[6],
        vec_grad[7],
        grad_vision_up,
        vu_bias_grad,
        grad_vision_down,
        vec_grad[8],
        grad_text_up,
        tu_bias_grad,
        grad_text_down,
        vec_grad[9],
    )


def layer_norm(hidden, gain, shift):
    center = hidden - jnp.mean(hidden, axis=-1, keepdims=True)
    spread = jnp.mean(center * center, axis=-1, keepdims=True)
    return center * lax.rsqrt(spread + epsilon) * gain + shift


def exact_gelu(values):
    return jax.nn.gelu(values, approximate=False)


def expert_forward(rows_in, up_matrix, up_shift, down_matrix, down_shift):
    upper = jnp.dot(rows_in, up_matrix, preferred_element_type=jnp.float32) + up_shift.astype(
        jnp.float32
    )
    active, gelu_pull = jax.vjp(exact_gelu, upper)
    active_b = active.astype(jnp.bfloat16)
    result = jnp.dot(active_b, down_matrix, preferred_element_type=jnp.float32) + down_shift.astype(
        jnp.float32
    )
    return (result, active_b, gelu_pull)


def expert_backward(rows_in, active_b, gelu_pull, up_matrix, down_matrix, grad_b):
    grad_down = jnp.einsum("rf,rd->fd", active_b, grad_b, preferred_element_type=jnp.float32)
    grad_down_shift = jnp.sum(grad_b.astype(jnp.float32), axis=0)
    grad_active = jnp.einsum("rd,fd->rf", grad_b, down_matrix, preferred_element_type=jnp.float32)
    (grad_upper,) = gelu_pull(grad_active)
    upper_b = grad_upper.astype(jnp.bfloat16)
    grad_up = jnp.einsum("rd,rf->df", rows_in, upper_b, preferred_element_type=jnp.float32)
    grad_up_shift = jnp.sum(upper_b.astype(jnp.float32), axis=0)
    grad_rows = jnp.einsum("rf,df->rd", upper_b, up_matrix, preferred_element_type=jnp.float32)
    return (grad_up, grad_up_shift, grad_down, grad_down_shift, grad_rows)


def general(
    tokens,
    out_grad,
    masked,
    lengths,
    mask_vec,
    norm1_gain,
    norm1_shift,
    w_qkv,
    query_bias,
    value_bias,
    w_out,
    out_bias,
    norm2_gain,
    norm2_shift,
    vision_up,
    vision_up_bias,
    vision_down,
    vision_down_bias,
    text_up,
    text_up_bias,
    text_down,
    text_down_bias,
):
    item_count, row_count, model_width = tokens.shape
    slot_count = masked.shape[1]
    patches = row_count - slot_count
    head_count = model_width // HEAD_DIM
    split_shape = (item_count, row_count, head_count, HEAD_DIM)

    def fetch_attention():
        return (
            lax.all_gather(mask_vec, "fsdp", axis=0, tiled=True),
            lax.all_gather(norm1_gain, "fsdp", axis=0, tiled=True),
            lax.all_gather(norm1_shift, "fsdp", axis=0, tiled=True),
            lax.all_gather(w_qkv, "fsdp", axis=0, tiled=True),
            lax.all_gather(query_bias, "fsdp", axis=0, tiled=True),
            lax.all_gather(value_bias, "fsdp", axis=0, tiled=True),
            lax.all_gather(w_out, "fsdp", axis=0, tiled=True),
            lax.all_gather(out_bias, "fsdp", axis=0, tiled=True),
        )

    def fetch_feedforward():
        return (
            lax.all_gather(norm2_gain, "fsdp", axis=0, tiled=True),
            lax.all_gather(norm2_shift, "fsdp", axis=0, tiled=True),
            lax.all_gather(vision_up, "fsdp", axis=0, tiled=True),
            lax.all_gather(vision_up_bias, "fsdp", axis=0, tiled=True),
            lax.all_gather(vision_down, "fsdp", axis=0, tiled=True),
            lax.all_gather(vision_down_bias, "fsdp", axis=0, tiled=True),
            lax.all_gather(text_up, "fsdp", axis=0, tiled=True),
            lax.all_gather(text_up_bias, "fsdp", axis=0, tiled=True),
            lax.all_gather(text_down, "fsdp", axis=0, tiled=True),
            lax.all_gather(text_down_bias, "fsdp", axis=0, tiled=True),
        )

    attn_full = fetch_attention()
    full_mask, gain_one, shift_one, qkv_matrix, query_shift, value_shift, out_matrix, out_shift = (
        attn_full
    )
    mask_rows = jnp.concatenate(
        [jnp.zeros((item_count, patches), jnp.float32), masked.astype(jnp.float32)], axis=1
    )[:, :, None]
    hidden0 = mask_rows * full_mask.astype(jnp.float32) + (1.0 - mask_rows) * tokens.astype(
        jnp.float32
    )
    normed1, first_pull = jax.vjp(
        layer_norm, hidden0, gain_one.astype(jnp.float32), shift_one.astype(jnp.float32)
    )
    first_in = normed1.astype(jnp.bfloat16).reshape(item_count * row_count, model_width)
    projected = jnp.dot(first_in, qkv_matrix, preferred_element_type=jnp.float32)
    query_b = (
        ((projected[:, :model_width] + query_shift.astype(jnp.float32)) * 0.125)
        .astype(jnp.bfloat16)
        .reshape(split_shape)
    )
    key_b = projected[:, model_width : 2 * model_width].astype(jnp.bfloat16).reshape(split_shape)
    value_b = (
        (projected[:, 2 * model_width :] + value_shift.astype(jnp.float32))
        .astype(jnp.bfloat16)
        .reshape(split_shape)
    )
    key_index = jnp.arange(row_count, dtype=jnp.int32)
    valid_keys = (key_index[None, :] < patches + lengths[:, None])[:, None, None, :]

    def scores_of():
        raw_scores = jnp.einsum(
            "iqhd,ikhd->ihqk", query_b, key_b, preferred_element_type=jnp.float32
        )
        return jnp.where(valid_keys, raw_scores, -1000000000.0)

    scores = scores_of()
    top_score = jnp.max(scores, axis=-1, keepdims=True)
    expo = jnp.exp(scores - top_score)
    totals = jnp.sum(expo, axis=-1, keepdims=True)
    probs = expo / totals
    log_total = top_score + jnp.log(totals)
    context = jnp.einsum(
        "ihqk,ikhd->iqhd", probs.astype(jnp.bfloat16), value_b, preferred_element_type=jnp.float32
    )
    context_b = context.reshape(item_count * row_count, model_width).astype(jnp.bfloat16)
    attended = jnp.dot(
        context_b, out_matrix, preferred_element_type=jnp.float32
    ) + out_shift.astype(jnp.float32)
    hidden1 = hidden0 + attended.reshape(item_count, row_count, model_width)
    ffn_full = fetch_feedforward()
    (
        gain_two,
        shift_two,
        vision_upm,
        vision_upb,
        vision_downm,
        vision_downb,
        text_upm,
        text_upb,
        text_downm,
        text_downb,
    ) = ffn_full
    normed2, second_pull = jax.vjp(
        layer_norm, hidden1, gain_two.astype(jnp.float32), shift_two.astype(jnp.float32)
    )
    second_in = normed2.astype(jnp.bfloat16)
    patch_in = second_in[:, :patches].reshape(-1, model_width)
    text_in = second_in[:, patches:].reshape(-1, model_width)
    vision_out, vision_act, vision_pull = expert_forward(
        patch_in, vision_upm, vision_upb, vision_downm, vision_downb
    )
    text_out, text_act, text_pull = expert_forward(
        text_in, text_upm, text_upb, text_downm, text_downb
    )
    mixed = hidden1 + jnp.concatenate(
        [
            vision_out.reshape(item_count, patches, model_width),
            text_out.reshape(item_count, slot_count, model_width),
        ],
        axis=1,
    )
    cotangent = out_grad.astype(jnp.float32)
    branch_b = cotangent.astype(jnp.bfloat16)
    ffn_back = fetch_feedforward()
    vision_grads = expert_backward(
        patch_in,
        vision_act,
        vision_pull,
        ffn_back[2],
        ffn_back[4],
        branch_b[:, :patches].reshape(-1, model_width),
    )
    text_grads = expert_backward(
        text_in,
        text_act,
        text_pull,
        ffn_back[6],
        ffn_back[8],
        branch_b[:, patches:].reshape(-1, model_width),
    )
    grad_normed2 = jnp.concatenate(
        [
            vision_grads[4].reshape(item_count, patches, model_width),
            text_grads[4].reshape(item_count, slot_count, model_width),
        ],
        axis=1,
    )
    grad_hidden1_norm, grad_gain_two, grad_shift_two = second_pull(grad_normed2)
    grad_hidden1 = cotangent + grad_hidden1_norm
    attn_back = fetch_attention()
    grad_attn_b = grad_hidden1.reshape(-1, model_width).astype(jnp.bfloat16)
    grad_out_matrix = jnp.einsum(
        "rd,re->de", context_b, grad_attn_b, preferred_element_type=jnp.float32
    )
    grad_out_shift = jnp.sum(grad_attn_b.astype(jnp.float32), axis=0)
    grad_context = jnp.einsum(
        "re,de->rd", grad_attn_b, attn_back[6], preferred_element_type=jnp.float32
    )
    grad_context_b = grad_context.astype(jnp.bfloat16).reshape(split_shape)
    again_probs = jnp.exp(scores_of() - log_total)
    grad_probs = jnp.einsum(
        "iqhd,ikhd->ihqk", grad_context_b, value_b, preferred_element_type=jnp.float32
    )
    grad_value = jnp.einsum(
        "ihqk,iqhd->ikhd",
        again_probs.astype(jnp.bfloat16),
        grad_context_b,
        preferred_element_type=jnp.float32,
    )
    row_inner = jnp.sum(again_probs * grad_probs, axis=-1, keepdims=True)
    grad_scores_b = (again_probs * (grad_probs - row_inner)).astype(jnp.bfloat16)
    grad_query = jnp.einsum(
        "ihqk,ikhd->iqhd", grad_scores_b, key_b, preferred_element_type=jnp.float32
    )
    grad_key = jnp.einsum(
        "ihqk,iqhd->ikhd", grad_scores_b, query_b, preferred_element_type=jnp.float32
    )
    grad_query_b = grad_query.astype(jnp.bfloat16) * jnp.bfloat16(0.125)
    stacked = jnp.concatenate(
        [
            grad_query_b.reshape(-1, model_width),
            grad_key.astype(jnp.bfloat16).reshape(-1, model_width),
            grad_value.astype(jnp.bfloat16).reshape(-1, model_width),
        ],
        axis=1,
    )
    grad_qkv = jnp.einsum("rd,re->de", first_in, stacked, preferred_element_type=jnp.float32)
    grad_query_shift = jnp.sum(stacked[:, :model_width].astype(jnp.float32), axis=0)
    grad_value_shift = jnp.sum(stacked[:, 2 * model_width :].astype(jnp.float32), axis=0)
    grad_normed1 = jnp.einsum(
        "re,de->rd", stacked, attn_back[3], preferred_element_type=jnp.float32
    )
    grad_hidden0_norm, grad_gain_one, grad_shift_one = first_pull(
        grad_normed1.reshape(item_count, row_count, model_width)
    )
    grad_hidden0 = grad_hidden1 + grad_hidden0_norm
    grad_tokens = grad_hidden0 * (1.0 - mask_rows)
    grad_mask = jnp.sum(grad_hidden0 * mask_rows, axis=(0, 1))
    ffn_share = (
        lax.psum_scatter(grad_gain_two, "fsdp", scatter_dimension=0, tiled=True),
        lax.psum_scatter(grad_shift_two, "fsdp", scatter_dimension=0, tiled=True),
        lax.psum_scatter(vision_grads[0], "fsdp", scatter_dimension=0, tiled=True),
        lax.psum_scatter(vision_grads[1], "fsdp", scatter_dimension=0, tiled=True),
        lax.psum_scatter(vision_grads[2], "fsdp", scatter_dimension=0, tiled=True),
        lax.psum_scatter(vision_grads[3], "fsdp", scatter_dimension=0, tiled=True),
        lax.psum_scatter(text_grads[0], "fsdp", scatter_dimension=0, tiled=True),
        lax.psum_scatter(text_grads[1], "fsdp", scatter_dimension=0, tiled=True),
        lax.psum_scatter(text_grads[2], "fsdp", scatter_dimension=0, tiled=True),
        lax.psum_scatter(text_grads[3], "fsdp", scatter_dimension=0, tiled=True),
    )
    attn_share = (
        lax.psum_scatter(grad_mask, "fsdp", scatter_dimension=0, tiled=True),
        lax.psum_scatter(grad_gain_one, "fsdp", scatter_dimension=0, tiled=True),
        lax.psum_scatter(grad_shift_one, "fsdp", scatter_dimension=0, tiled=True),
        lax.psum_scatter(grad_qkv, "fsdp", scatter_dimension=0, tiled=True),
        lax.psum_scatter(grad_query_shift, "fsdp", scatter_dimension=0, tiled=True),
        lax.psum_scatter(grad_value_shift, "fsdp", scatter_dimension=0, tiled=True),
        lax.psum_scatter(grad_out_matrix, "fsdp", scatter_dimension=0, tiled=True),
        lax.psum_scatter(grad_out_shift, "fsdp", scatter_dimension=0, tiled=True),
    )
    quarter = (
        lax.psum_scatter(
            attn_share[0].astype(jnp.bfloat16), "rep", scatter_dimension=0, tiled=True
        ).astype(jnp.float32),
        lax.psum_scatter(
            attn_share[1].astype(jnp.bfloat16), "rep", scatter_dimension=0, tiled=True
        ).astype(jnp.float32),
        lax.psum_scatter(
            attn_share[2].astype(jnp.bfloat16), "rep", scatter_dimension=0, tiled=True
        ).astype(jnp.float32),
        lax.psum_scatter(
            attn_share[3].astype(jnp.bfloat16), "rep", scatter_dimension=0, tiled=True
        ).astype(jnp.float32),
        lax.psum_scatter(
            attn_share[4].astype(jnp.bfloat16), "rep", scatter_dimension=0, tiled=True
        ).astype(jnp.float32),
        lax.psum_scatter(
            attn_share[5].astype(jnp.bfloat16), "rep", scatter_dimension=0, tiled=True
        ).astype(jnp.float32),
        lax.psum_scatter(
            attn_share[6].astype(jnp.bfloat16), "rep", scatter_dimension=0, tiled=True
        ).astype(jnp.float32),
        lax.psum_scatter(
            attn_share[7].astype(jnp.bfloat16), "rep", scatter_dimension=0, tiled=True
        ).astype(jnp.float32),
        lax.psum_scatter(
            ffn_share[0].astype(jnp.bfloat16), "rep", scatter_dimension=0, tiled=True
        ).astype(jnp.float32),
        lax.psum_scatter(
            ffn_share[1].astype(jnp.bfloat16), "rep", scatter_dimension=0, tiled=True
        ).astype(jnp.float32),
        lax.psum_scatter(
            ffn_share[2].astype(jnp.bfloat16), "rep", scatter_dimension=0, tiled=True
        ).astype(jnp.float32),
        lax.psum_scatter(
            ffn_share[3].astype(jnp.bfloat16), "rep", scatter_dimension=0, tiled=True
        ).astype(jnp.float32),
        lax.psum_scatter(
            ffn_share[4].astype(jnp.bfloat16), "rep", scatter_dimension=0, tiled=True
        ).astype(jnp.float32),
        lax.psum_scatter(
            ffn_share[5].astype(jnp.bfloat16), "rep", scatter_dimension=0, tiled=True
        ).astype(jnp.float32),
        lax.psum_scatter(
            ffn_share[6].astype(jnp.bfloat16), "rep", scatter_dimension=0, tiled=True
        ).astype(jnp.float32),
        lax.psum_scatter(
            ffn_share[7].astype(jnp.bfloat16), "rep", scatter_dimension=0, tiled=True
        ).astype(jnp.float32),
        lax.psum_scatter(
            ffn_share[8].astype(jnp.bfloat16), "rep", scatter_dimension=0, tiled=True
        ).astype(jnp.float32),
        lax.psum_scatter(
            ffn_share[9].astype(jnp.bfloat16), "rep", scatter_dimension=0, tiled=True
        ).astype(jnp.float32),
    )
    summed = (
        lax.all_gather(quarter[0].astype(jnp.bfloat16), "rep", axis=0, tiled=True).astype(
            jnp.float32
        ),
        lax.all_gather(quarter[1].astype(jnp.bfloat16), "rep", axis=0, tiled=True).astype(
            jnp.float32
        ),
        lax.all_gather(quarter[2].astype(jnp.bfloat16), "rep", axis=0, tiled=True).astype(
            jnp.float32
        ),
        lax.all_gather(quarter[3].astype(jnp.bfloat16), "rep", axis=0, tiled=True).astype(
            jnp.float32
        ),
        lax.all_gather(quarter[4].astype(jnp.bfloat16), "rep", axis=0, tiled=True).astype(
            jnp.float32
        ),
        lax.all_gather(quarter[5].astype(jnp.bfloat16), "rep", axis=0, tiled=True).astype(
            jnp.float32
        ),
        lax.all_gather(quarter[6].astype(jnp.bfloat16), "rep", axis=0, tiled=True).astype(
            jnp.float32
        ),
        lax.all_gather(quarter[7].astype(jnp.bfloat16), "rep", axis=0, tiled=True).astype(
            jnp.float32
        ),
        lax.all_gather(quarter[8].astype(jnp.bfloat16), "rep", axis=0, tiled=True).astype(
            jnp.float32
        ),
        lax.all_gather(quarter[9].astype(jnp.bfloat16), "rep", axis=0, tiled=True).astype(
            jnp.float32
        ),
        lax.all_gather(quarter[10].astype(jnp.bfloat16), "rep", axis=0, tiled=True).astype(
            jnp.float32
        ),
        lax.all_gather(quarter[11].astype(jnp.bfloat16), "rep", axis=0, tiled=True).astype(
            jnp.float32
        ),
        lax.all_gather(quarter[12].astype(jnp.bfloat16), "rep", axis=0, tiled=True).astype(
            jnp.float32
        ),
        lax.all_gather(quarter[13].astype(jnp.bfloat16), "rep", axis=0, tiled=True).astype(
            jnp.float32
        ),
        lax.all_gather(quarter[14].astype(jnp.bfloat16), "rep", axis=0, tiled=True).astype(
            jnp.float32
        ),
        lax.all_gather(quarter[15].astype(jnp.bfloat16), "rep", axis=0, tiled=True).astype(
            jnp.float32
        ),
        lax.all_gather(quarter[16].astype(jnp.bfloat16), "rep", axis=0, tiled=True).astype(
            jnp.float32
        ),
        lax.all_gather(quarter[17].astype(jnp.bfloat16), "rep", axis=0, tiled=True).astype(
            jnp.float32
        ),
    )
    return (
        mixed.astype(jnp.bfloat16),
        grad_tokens,
        summed[0],
        summed[1],
        summed[2],
        summed[3],
        summed[4],
        summed[5],
        summed[6],
        summed[7],
        summed[8],
        summed[9],
        summed[10],
        summed[11],
        summed[12],
        summed[13],
        summed[14],
        summed[15],
        summed[16],
        summed[17],
    )


def solution(mesh):
    if mesh.shape["fsdp"] == 8 and mesh.shape["rep"] == 4:
        body = planned
    else:
        body = general
    return jax.shard_map(
        body,
        mesh=mesh,
        in_specs=(
            P(("fsdp", "rep"), None, None),
            P(("fsdp", "rep"), None, None),
            P(("fsdp", "rep"), None),
            P(("fsdp", "rep")),
            P("fsdp"),
            P("fsdp"),
            P("fsdp"),
            P("fsdp", None),
            P("fsdp"),
            P("fsdp"),
            P("fsdp", None),
            P("fsdp"),
            P("fsdp"),
            P("fsdp"),
            P("fsdp", None),
            P("fsdp"),
            P("fsdp", None),
            P("fsdp"),
            P("fsdp", None),
            P("fsdp"),
            P("fsdp", None),
            P("fsdp"),
        ),
        out_specs=(
            P(("fsdp", "rep"), None, None),
            P(("fsdp", "rep"), None, None),
            P("fsdp"),
            P("fsdp"),
            P("fsdp"),
            P("fsdp", None),
            P("fsdp"),
            P("fsdp"),
            P("fsdp", None),
            P("fsdp"),
            P("fsdp"),
            P("fsdp"),
            P("fsdp", None),
            P("fsdp"),
            P("fsdp", None),
            P("fsdp"),
            P("fsdp", None),
            P("fsdp"),
            P("fsdp", None),
            P("fsdp"),
        ),
        check_vma=False,
    )
```

```python
import functools
import math

import jax
import jax.numpy as jnp
from jax import lax
from jax.experimental import pallas as pl
from jax.experimental.pallas import tpu as pltpu
from jax.sharding import PartitionSpec as P

HEAD_DIM = 64
BF = jnp.bfloat16
F32 = jnp.float32
epsilon = 1e-06
VMEM_LIMIT = 58 * 1024 * 1024

ITEM = 256
SCALE = 0.2
TEXT_AT = 208


def cdiv(a, b):
    return -(-a // b)


def dot_nn(a, b):
    return lax.dot_general(a, b, (((1,), (0,)), ((), ())), preferred_element_type=F32)


def dot_nt(a, b):
    return lax.dot_general(a, b, (((1,), (1,)), ((), ())), preferred_element_type=F32)


def dot_tn(a, b):
    return lax.dot_general(a, b, (((0,), (0,)), ((), ())), preferred_element_type=F32)


def gelu_parts(upper):
    half = 0.5 * (1.0 + lax.erf(upper * math.sqrt(0.5)))
    slope = half + upper * (jnp.exp(-0.5 * upper * upper) * (1.0 / math.sqrt(2.0 * math.pi)))
    return upper * half, slope


def normalize(hidden):
    center = hidden - jnp.mean(hidden, axis=-1, keepdims=True)
    spread = jnp.mean(center * center, axis=-1, keepdims=True)
    scale = lax.rsqrt(spread + epsilon)
    return center * scale, scale


def start_rows(pieces, target, me, sems):
    block = target.shape[0] // 8
    copies = []
    for index, (slot, first, ref) in enumerate(pieces):
        row = pl.multiple_of((me ^ slot) * block + first, 16)
        copy = pltpu.make_async_copy(ref, target.at[pl.ds(row, ref.shape[0])], sems.at[index])
        copy.start()
        copies.append(copy)
    return copies


def mixed_in(tok, mask, vec, rows):
    keep = mask[rows, :]
    return keep * vec[0:1, :] + (1.0 - keep) * tok[rows, :].astype(F32)


def gate_kernel(count, *refs):
    del count, refs


def gate(arrays, after):
    count = len(arrays)
    return pl.pallas_call(
        functools.partial(gate_kernel, count),
        out_shape=[jax.ShapeDtypeStruct(a.shape, a.dtype) for a in arrays],
        in_specs=[pl.BlockSpec(memory_space=pl.ANY)] * (count + len(after)),
        out_specs=[pl.BlockSpec(memory_space=pl.ANY)] * count,
        input_output_aliases={i: i for i in range(count)},
        cost_estimate=pl.CostEstimate(flops=1000, bytes_accessed=1000, transcendentals=0),
    )(*arrays, *after)


def tick(token, after):
    return gate([token], after)[0]


def prep_kernel(text_rows, info, tokens, out_grad, w_out, down, up, text_up, *outs):
    tok, grad, grad_v, grad_t, sums, out_copy, down_copy, up_mine, up_other, strip0, te1, te2, te3, token = outs
    token[...] = jnp.zeros(token.shape, F32)
    items, row_count, width = tokens.shape
    patches = row_count - text_rows
    tail = ITEM - TEXT_AT - text_rows
    zeros = lambda n: jnp.zeros((n, width), F32)
    totals = [zeros(1), zeros(1)]
    texts = []
    for i in range(items):
        for source, target in ((tokens, tok), (out_grad, grad)):
            whole = source[i].astype(F32)
            patch, text = whole[:patches], whole[patches:]
            full = jnp.concatenate([patch, zeros(TEXT_AT - patches), text, zeros(tail)], axis=0)
            target[pl.ds(i * ITEM, ITEM), :] = full.astype(BF)
            if target is grad:
                grad_v[pl.ds(i * TEXT_AT, TEXT_AT), :] = full[:TEXT_AT].astype(BF)
                texts.append(text)
                totals[0] = totals[0] + jnp.sum(patch, axis=0, keepdims=True)
                totals[1] = totals[1] + jnp.sum(text, axis=0, keepdims=True)
    slots = jnp.concatenate(texts, axis=0).astype(BF)
    grad_t[...] = slots
    sums[0:1, :] = totals[0]
    sums[1:2, :] = totals[1]
    out_copy[...] = w_out[...]
    down_copy[...] = down[...]
    chip = info[0] // 2
    side = chip % 2
    block = up.shape[0]
    pair = 2 * down.shape[0]
    strip = lambda ref, c: ref[:, pl.ds(pl.multiple_of(c * pair, 128), pair)]
    for k in range(2):
        up_mine[:, k * pair : (k + 1) * pair] = strip(up, side + 2 * k)
        up_other[:, k * pair : (k + 1) * pair] = strip(up, 1 - side + 2 * k)
    strip0[...] = strip(text_up, chip)
    for k, target in ((1, te1), (2, te2), (3, te3)):
        target[pl.ds(0, block), :] = strip(text_up, chip ^ k)
        target[pl.ds(block, slots.shape[0]), :] = slots


def norm_kernel(info, tok, mask, even, odd, *refs):
    n1, vec, up_bias, shards = refs[-4:]
    me = info[0]
    total, width = tok.shape
    block = width // 8
    for slot in range(8):
        shards[me ^ slot] = (even, odd)[slot % 2][slot // 2]
    wide = jnp.concatenate([shards[b] for b in range(8)], axis=1)
    lane = lax.broadcasted_iota(jnp.int32, (1024, width), 0)
    to = lax.broadcasted_iota(jnp.int32, (1024, width), 1)
    spread = ((lane // 128) * block + lane % 128 == to) & (lane % 128 < block)
    vec[...] = dot_nn(wide, jnp.where(spread, 1.0, 0.0).astype(BF))
    hid = up_bias.shape[1] // 4
    for q in range(4):
        b = (q // 2) * 4 + q % 2 + ((me // 2) % 2) * 2
        for r in range(hid // 128):
            at = q * hid + r * 128
            up_bias[0:1, at : at + 128] = shards[b, 10 + r : 11 + r, :].astype(F32)

    @pl.loop(0, total // 64)
    def _(step):
        rows = pl.ds(pl.multiple_of(step * 64, 64), 64)
        normal, _unused = normalize(mixed_in(tok, mask, vec, rows))
        n1[rows, :] = (normal * vec[1:2, :] + vec[2:3, :]).astype(BF)


def qkv_kernel(slots, info, n1, vec, *refs):
    count = len(slots)
    pieces = refs[:count]
    qkv, weight, bias, sems = refs[-4:]
    width = n1.shape[1]
    copies = start_rows([(s, f, r) for (s, f), r in zip(slots, pieces)], weight, info[0], sems)
    bias[0:1, 0:width] = vec[3:4, :]
    bias[0:1, width : 2 * width] = jnp.zeros((1, width), F32)
    bias[0:1, 2 * width : 3 * width] = vec[4:5, :]
    for copy in copies:
        copy.wait()

    @pl.loop(0, 3 * width // 256)
    def _(step):
        cols = pl.ds(pl.multiple_of(step * 256, 256), 256)
        factor = jnp.where(step < width // 256, 0.125, 1.0).astype(F32)
        out = dot_nn(n1[...], weight[:, cols])
        qkv[:, cols] = ((out + bias[0:1, cols]) * factor).astype(BF)


def attn_kernel(info, qkv, *refs):
    probs, ctx = refs[-2:]
    total, width = ctx.shape
    items = total // ITEM
    pairs = width // 128
    patches = info[3]

    @pl.loop(0, items * pairs)
    def _(step):
        item, pair = step // pairs, step % pairs
        rows = pl.ds(pl.multiple_of(item * ITEM, ITEM), ITEM)
        lane = lambda part: pl.ds(pl.multiple_of(part * width + pair * 128, 128), 128)
        q2, k2, v2 = qkv[rows, lane(0)], qkv[rows, lane(1)], qkv[rows, lane(2)]
        low = lax.broadcasted_iota(jnp.int32, (ITEM, 128), 1) < HEAD_DIM
        zero = jnp.zeros_like(q2)
        both = jnp.concatenate([jnp.where(low, q2, zero), jnp.where(low, zero, q2)], axis=0)
        scores = dot_nt(both, k2)
        col = lax.broadcasted_iota(jnp.int32, (1, ITEM), 1)
        valid = (col < patches) | ((col >= TEXT_AT) & (col < TEXT_AT + info[1 + item]))
        scores = jnp.where(valid, scores, -1000000000.0)
        expo = jnp.exp(scores - jnp.max(scores, axis=-1, keepdims=True))
        prob = (expo * (1.0 / jnp.sum(expo, axis=-1, keepdims=True))).astype(BF)
        probs[step] = prob
        wide = jnp.concatenate([prob[:ITEM], prob[ITEM:]], axis=1)
        values = jnp.concatenate([jnp.where(low, v2, zero), jnp.where(low, zero, v2)], axis=0)
        ctx[rows, pl.ds(pl.multiple_of(pair * 128, 128), 128)] = dot_nn(wide, values).astype(BF)


def out_kernel(text_rows, info, tok, mask, vec, ctx, out_w, *refs):
    h1, n2t, *n2v = refs[-2 - tok.shape[0] // ITEM :]
    items = tok.shape[0] // ITEM
    texts = []
    for i in range(items):
        for at, size in ((0, TEXT_AT), (TEXT_AT, ITEM - TEXT_AT)):
            rows = pl.ds(i * ITEM + at, size)
            attended = dot_nn(ctx[rows, :], out_w[...]) + vec[5:6, :]
            hidden = mixed_in(tok, mask, vec, rows) + attended
            h1[rows, :] = hidden
            normal, _unused = normalize(hidden)
            second = normal * vec[6:7, :] + vec[7:8, :]
            if at == 0:
                n2v[i][...] = second.astype(BF)
            else:
                texts.append(second[:text_rows])
    n2t[...] = jnp.concatenate(texts, axis=0).astype(BF)


def pack_kernel(info, strip0, te1, te2, te3, grad_t, pack):
    block, hid = strip0.shape[0], strip0.shape[1] // 2
    rows = grad_t.shape[0]
    other = pl.ds(pl.multiple_of((1 - info[0] % 2) * hid, 128), hid)
    for k, ref in enumerate((strip0, te1, te2, te3)):
        at = (k // 2) * block
        pack[at : at + block, (k % 2) * hid : (k % 2 + 1) * hid] = ref[pl.ds(0, block), other]
        there = pl.ds(2 * block + k * rows, rows)
        pack[there, :] = grad_t[...] if k == 0 else ref[pl.ds(block, rows), :]


def up_rows(me, pieces, target, sems):
    block = target.shape[0] // 8
    copies = []
    for index, (base, ref) in enumerate(pieces):
        for k in range(2):
            row = pl.multiple_of((me ^ (base + 2 * k)) * block, 16)
            sem = sems.at[2 * index + k]
            copies.append(pltpu.make_async_copy(ref.at[k], target.at[pl.ds(row, block)], sem))
    for copy in copies:
        copy.start()
    return copies


def place_of(me):
    return (me // 4) * 2 + me % 2


def vision_kernel(pair, items, info, grad, up_bias, *refs):
    parts, refs = refs[:items], refs[items:]
    ups, downs = refs[:4], refs[4:6]
    branch, gn2, act, low, up_w, down_w, rows_in, sems = refs[-8:]
    me = info[0]
    block = downs[0].shape[1]
    copies = up_rows(me, list(zip((0, 4, 1, 5), ups)), up_w, sems)
    place = place_of(me)
    for j in range(4):
        row = pl.multiple_of((place ^ j) * block, 16)
        copy = pltpu.make_async_copy(downs[j % 2].at[j // 2], down_w.at[pl.ds(row, block)], sems.at[8 + j])
        copy.start()
        copies.append(copy)
    for copy in copies:
        copy.wait()
    mine = grad.at[(me // 2) % 2 ^ 1] if pair else grad
    for i, part in enumerate(parts):
        rows_in[pl.ds(i * TEXT_AT, TEXT_AT), :] = part[...]
    chunk = 512
    for step in range(down_w.shape[0] // chunk):
        cols = slice(step * chunk, (step + 1) * chunk)
        upper = dot_nn(rows_in[...], up_w[:, cols]) + up_bias[0:1, cols]
        active, slope = gelu_parts(upper)
        active = active.astype(BF)
        act[:, cols] = active
        back = (dot_nt(mine[...], down_w[cols, :]) * slope).astype(BF)
        low[:, cols] = back
        if step == 0:
            sum_branch = dot_nn(active, down_w[cols, :])
            sum_gn2 = dot_nt(back, up_w[:, cols])
        else:
            sum_branch = sum_branch + dot_nn(active, down_w[cols, :])
            sum_gn2 = sum_gn2 + dot_nt(back, up_w[:, cols])
    branch[...] = sum_branch.astype(branch.dtype)
    gn2[...] = sum_gn2.astype(gn2.dtype)


def vision_grad_kernel(items, info, *refs):
    ins = refs[:items], refs[items : 2 * items]
    grads, refs = refs[2 * items], refs[2 * items + 1 :]
    acts, lows = refs[:2], refs[2:4]
    up_keep, up_send, down_keep, down_send, bias_sums = refs[-11:-6]
    left_t, act_t, right, low, turn0, turn1 = refs[-6:]
    me = info[0]
    rows, width = items * ins[0][0].shape[0], ins[0][0].shape[1]
    block = width // 8
    half = down_keep.shape[1]
    place, core = place_of(me), me % 2
    for k in range(2):
        at = pl.ds(k * rows, rows)
        right[at, :] = grads[(me // 2) % 2 ^ k]
        low[at, :] = lows[k][...]
        turned = jnp.concatenate([ref[...] for ref in ins[k]], axis=0).T
        turn = (turn0, turn1)[k]
        for b in range(8):
            spot = pl.multiple_of((me ^ b) * block, 16)
            turn[pl.ds(spot, block), :] = turned[b * block : (b + 1) * block]
        left_t[:, at] = turn[...]
        act_t[:, at] = acts[k][...].T
    chunk = 512
    for step in range(4 * half // chunk):
        cols = slice(step * chunk, (step + 1) * chunk)
        grad_up = dot_nn(left_t[...], low[:, cols])
        bias_sums[0:1, cols] = jnp.sum(low[:, cols].astype(F32), axis=0, keepdims=True)
        grad_up = grad_up.astype(BF)
        for b in range(4):
            up_keep[b, :, cols] = grad_up[2 * b * block : (2 * b + 1) * block]
            up_send[b, :, cols] = grad_up[(2 * b + 1) * block : (2 * b + 2) * block]
    for q in range(4):
        grad_down = dot_nn(act_t[q * half : (q + 1) * half, :], right[...]).astype(BF)
        side = (q // 2) ^ (place // 2)

        @pl.when(core == q % 2)
        def _():
            down_keep[side] = grad_down

        @pl.when(core != q % 2)
        def _():
            down_send[side] = grad_down


def text_kernel(info, down, up_bias, strip0, te1, te2, te3, far, even, odd, *refs):
    grad0, refs = refs[0], refs[1:]
    branch_keep, branch_send, gn2_keep, gn2_send, up_keep, up_send, grad_down, bias_sums = refs[-12:-4]
    up_w, left, right, left_t = refs[-4:]
    me = info[0]
    width = down.shape[1]
    hid = down.shape[0]
    block = width // 8
    rows = even.shape[1]
    mine = pl.ds(pl.multiple_of((me % 2) * hid, 128), hid)
    spot = lambda slot: pl.ds(pl.multiple_of((me ^ slot) * block, 16), block)
    up_w[spot(0), :] = strip0[:, mine]
    for s, te in ((2, te1), (4, te2), (6, te3)):
        up_w[spot(s), :] = te[pl.ds(0, block), mine]
        right[pl.ds(s * rows, rows), :] = te[pl.ds(block, rows), :]
    up_w[spot(1), :] = far[pl.ds(0, block), pl.ds(0, hid)]
    up_w[spot(3), :] = far[pl.ds(0, block), pl.ds(hid, hid)]
    up_w[spot(5), :] = far[pl.ds(block, block), pl.ds(0, hid)]
    up_w[spot(7), :] = far[pl.ds(block, block), pl.ds(hid, hid)]
    right[pl.ds(0, rows), :] = grad0[...]
    for k in range(4):
        right[pl.ds((2 * k + 1) * rows, rows), :] = far[pl.ds(2 * block + k * rows, rows), :]
    for slot in range(8):
        left[pl.ds(slot * rows, rows), :] = (even, odd)[slot % 2][slot // 2]
    turned = left[...].T
    for b in range(8):
        left_t[spot(b), :] = turned[b * block : (b + 1) * block]
    upper = dot_nn(left[...], up_w[...]) + up_bias[...]
    active, slope = gelu_parts(upper)
    act = active.astype(BF)
    low = (dot_nt(right[...], down[...]) * slope).astype(BF)
    bias_sums[...] = jnp.sum(low.astype(F32), axis=0, keepdims=True)
    gn2 = dot_nt(low, up_w[...]).astype(BF)
    branch = dot_nn(act, down[...]).astype(BF)
    for s in range(4):
        gn2_keep[s] = gn2[2 * s * rows : (2 * s + 1) * rows]
        gn2_send[s] = gn2[(2 * s + 1) * rows : (2 * s + 2) * rows]
        branch_keep[s] = branch[2 * s * rows : (2 * s + 1) * rows]
        branch_send[s] = branch[(2 * s + 1) * rows : (2 * s + 2) * rows]
    grad_down[...] = dot_tn(act, right[...]).astype(BF)
    grad_up = dot_nn(left_t[...], low).astype(BF)
    for b in range(4):
        up_keep[b] = grad_up[2 * b * block : (2 * b + 1) * block]
        up_send[b] = grad_up[(2 * b + 1) * block : (2 * b + 2) * block]


def attn_bwd_kernel(text_rows, info, gn2v, gn2x, t0, t1, t2, t3, grad, h1, vec, qkv, probs, weight, *refs):
    gh1, low, stacked, sums, gn2, gctx = refs[-6:]
    total, width = h1.shape
    items = total // ITEM
    text = (
        t0[0].astype(F32) + t1[...].astype(F32) + t2[...].astype(F32) + t3[...].astype(F32)
    )
    for i in range(items):
        part = pl.ds(i * TEXT_AT, TEXT_AT)
        gn2[pl.ds(i * ITEM, TEXT_AT), :] = gn2v[part, :] + gn2x[part, :].astype(F32)
        gn2[pl.ds(i * ITEM + TEXT_AT, text_rows), :] = text[i * text_rows : (i + 1) * text_rows]
        pad = ITEM - TEXT_AT - text_rows
        gn2[pl.ds(i * ITEM + TEXT_AT + text_rows, pad), :] = jnp.zeros((pad, width), F32)
    sums[...] = jnp.zeros_like(sums)

    @pl.loop(0, total // 64)
    def _(step):
        rows = pl.ds(pl.multiple_of(step * 64, 64), 64)
        normal, scale = normalize(h1[rows, :])
        above = gn2[rows, :]
        inner = above * vec[6:7, :]
        back = scale * (
            inner
            - jnp.mean(inner, axis=-1, keepdims=True)
            - normal * jnp.mean(inner * normal, axis=-1, keepdims=True)
        )
        out = grad[rows, :].astype(F32)
        hidden = out + back
        gh1[rows, :] = hidden
        low[rows, :] = hidden.astype(BF)
        sums[0:1, :] += jnp.sum(above * normal, axis=0, keepdims=True)
        sums[1:2, :] += jnp.sum(above, axis=0, keepdims=True)
        sums[2:3, :] += jnp.sum(hidden.astype(BF).astype(F32), axis=0, keepdims=True)

    gctx[...] = dot_nt(low[...], weight[...]).astype(BF)
    pairs = width // 128

    @pl.loop(0, items * pairs)
    def _(step):
        item, pair = step // pairs, step % pairs
        rows = pl.ds(pl.multiple_of(item * ITEM, ITEM), ITEM)
        lane = lambda part: pl.ds(pl.multiple_of(part * width + pair * 128, 128), 128)
        q2, k2, v2 = qkv[rows, lane(0)], qkv[rows, lane(1)], qkv[rows, lane(2)]
        g2 = gctx[rows, pl.ds(pl.multiple_of(pair * 128, 128), 128)]
        lower = lax.broadcasted_iota(jnp.int32, (ITEM, 128), 1) < HEAD_DIM
        zero = jnp.zeros_like(q2)
        split = lambda a: jnp.concatenate([jnp.where(lower, a, zero), jnp.where(lower, zero, a)], axis=0)
        both_g = split(g2)
        prob_b = probs[step]
        prob = prob_b.astype(F32)
        gprob = dot_nt(both_g, v2)
        weighted = prob * gprob
        gscore = (weighted - prob * jnp.sum(weighted, axis=-1, keepdims=True)).astype(BF)
        stacked[rows, lane(2)] = dot_tn(prob_b, both_g).astype(BF)
        stacked[rows, lane(1)] = dot_tn(gscore, split(q2)).astype(BF)
        wide = jnp.concatenate([gscore[:ITEM], gscore[ITEM:]], axis=1)
        gquery = dot_nn(wide, split(k2)).astype(BF).astype(F32) * 0.125
        stacked[rows, lane(0)] = gquery.astype(BF)

    for part in (0, 2):
        cols = stacked[:, part * width : (part + 1) * width].astype(F32)
        sums[3 + part // 2 : 4 + part // 2, :] = jnp.sum(cols, axis=0, keepdims=True)


def attn_grad_kernel(last, info, left, *refs):
    me = info[0]
    width = left.shape[1]
    block = width // 8
    keep, send, left_t, other_t, right, sem = refs[-6:]
    others, stacked = (refs[:2], refs[2]) if last else ((), refs[0])
    first = 2 * width if last else 0
    copy = pltpu.make_async_copy(stacked.at[:, pl.ds(first, right.shape[1])], right, sem.at[0])
    copy.start()
    for source, target in ((left, left_t), (others[0], other_t)) if last else ((left, left_t),):
        turned = source[...].T
        for b in range(8):
            place = pl.multiple_of((me ^ b) * block, 16)
            target[pl.ds(place, block), :] = turned[b * block : (b + 1) * block]
    for part in (1, 0) if last else (0, 1):
        cols = slice(part * width, (part + 1) * width)
        if last and part == 1:
            value = dot_nn(other_t[...], others[1][...]).astype(BF)
        else:
            if part == 0:
                copy.wait()
            value = dot_nn(left_t[...], right[:, cols]).astype(BF)
        for b in range(4):
            keep[b, :, cols] = value[2 * b * block : (2 * b + 1) * block]
            send[b, :, cols] = value[(2 * b + 1) * block : (2 * b + 2) * block]


def last_kernel(slots, info, stacked, gh1, tok, mask, vec, *refs):
    count = len(slots)
    pieces = refs[:count]
    gtok, sums, weight, sems = refs[-4:]
    copies = start_rows([(s, f, r) for (s, f), r in zip(slots, pieces)], weight, info[0], sems)
    sums[...] = jnp.zeros_like(sums)
    for copy in copies:
        copy.wait()

    @pl.loop(0, tok.shape[0] // 128)
    def _(step):
        rows = pl.ds(pl.multiple_of(step * 128, 128), 128)
        above = dot_nt(stacked[rows, :], weight[...])
        normal, scale = normalize(mixed_in(tok, mask, vec, rows))
        inner = above * vec[1:2, :]
        back = scale * (
            inner
            - jnp.mean(inner, axis=-1, keepdims=True)
            - normal * jnp.mean(inner * normal, axis=-1, keepdims=True)
        )
        hidden = gh1[rows, :] + back
        keep = mask[rows, :]
        gtok[rows, :] = hidden * (1.0 - keep)
        sums[0:1, :] += jnp.sum(hidden * keep, axis=0, keepdims=True)
        sums[1:2, :] += jnp.sum(above * normal, axis=0, keepdims=True)
        sums[2:3, :] += jnp.sum(above, axis=0, keepdims=True)


def call(kernel, outs, scratch, args, pieces=(), us=1):
    in_specs = [pl.BlockSpec(memory_space=pltpu.SMEM)]
    in_specs += [pl.BlockSpec(memory_space=pltpu.VMEM)] * (len(args) - 1)
    in_specs += [pl.BlockSpec(memory_space=pl.ANY)] * len(pieces)
    return pl.pallas_call(
        kernel,
        out_shape=[jax.ShapeDtypeStruct(s, d) for s, d in outs],
        in_specs=in_specs,
        out_specs=[pl.BlockSpec(memory_space=pltpu.VMEM)] * len(outs),
        scratch_shapes=scratch,
        compiler_params=pltpu.CompilerParams(vmem_limit_bytes=VMEM_LIMIT),
        cost_estimate=pl.CostEstimate(flops=int(us * SCALE * 1.1e9), bytes_accessed=int(us * SCALE * 1e6), transcendentals=0),
    )(*args, *pieces)


def swap(array, mask):
    return lax.ppermute(array, "fsdp", [(i, i ^ mask) for i in range(8)])


def along_rep(array, pairs):
    return lax.ppermute(array, "rep", pairs)


def add(*terms):
    out = terms[0].astype(F32)
    for term in terms[1:]:
        out = out + term.astype(F32)
    return out.astype(BF)


def planned(
    tokens,
    out_grad,
    masked,
    lengths,
    mask_vec,
    norm1_gain,
    norm1_shift,
    w_qkv,
    query_bias,
    value_bias,
    w_out,
    out_bias,
    norm2_gain,
    norm2_shift,
    vision_up,
    vision_up_bias,
    vision_down,
    vision_down_bias,
    text_up,
    text_up_bias,
    text_down,
    text_down_bias,
):
    items, row_count, width = tokens.shape
    text_rows = masked.shape[1]
    patches = row_count - text_rows
    block = width // 8
    half = block // 2
    hid = vision_down.shape[0]
    pair = 2 * hid
    hidden = 8 * hid
    total = items * ITEM
    vision_rows = items * TEXT_AT
    slot_rows = items * text_rows
    te_rows = block + slot_rows
    me = lax.axis_index("fsdp").astype(jnp.int32)
    rep = lax.axis_index("rep").astype(jnp.int32)
    core, chip, side = me % 2, me // 2, (me // 2) % 2
    sem = lambda n: pltpu.SemaphoreType.DMA((n,))
    quad = lambda r, c: ((4, r, c), BF)

    names = (
        mask_vec,
        norm1_gain,
        norm1_shift,
        query_bias,
        value_bias,
        out_bias,
        norm2_gain,
        norm2_shift,
        vision_down_bias,
        text_down_bias,
    )
    own_vec = jnp.pad(jnp.stack(names), ((0, 0), (0, 128 - block)))
    own_vec = jnp.concatenate([own_vec, vision_up_bias.reshape(-1, 128)], axis=0)
    own_vec = jnp.pad(own_vec, ((0, 16 - own_vec.shape[0]), (0, 0)))[None]
    vx, vy, vxy = swap(own_vec, 2), swap(own_vec, 4), swap(own_vec, 6)
    qx, qy = swap(w_qkv, 2), swap(w_qkv, 4)
    mask = jnp.concatenate(
        [
            jnp.zeros((items, TEXT_AT), F32),
            masked.astype(F32),
            jnp.zeros((items, ITEM - TEXT_AT - text_rows), F32),
        ],
        axis=1,
    ).reshape(total, 1)
    info = jnp.concatenate([me[None], lengths, jnp.full((1,), patches, jnp.int32)])
    tok, grad, grad_v, grad_t, grad_sums, own_out, own_down, up_mine, up_other, strip0, te1, te2, te3, t = call(
        functools.partial(prep_kernel, text_rows),
        [
            ((total, width), BF),
            ((total, width), BF),
            ((vision_rows, width), BF),
            ((slot_rows, width), BF),
            ((2, width), F32),
            ((block, width), BF),
            ((hid, width), BF),
            ((block, 2 * pair), BF),
            ((block, 2 * pair), BF),
            ((block, pair), BF),
            ((te_rows, width), BF),
            ((te_rows, width), BF),
            ((te_rows, width), BF),
            ((8, 128), F32),
        ],
        [],
        [info, tokens, out_grad, w_out, vision_down, vision_up, text_up],
        us=5,
    )
    vec_four = gate([jnp.concatenate([own_vec, vx, vy, vxy], axis=0)], [t])[0]
    vec_arrays = [vec_four, swap(vec_four, 1)]
    part1, part2 = gate([qx[:half], qy[half:]], [tok, vec_arrays[1]])

    far1, far2 = swap(part1, 4), swap(part2, 2)
    near = [swap(a, 1) for a in (w_qkv, qx, qy)]
    n1, vec, up_bias = call(
        norm_kernel,
        [((total, width), BF), ((16, width), F32), ((1, 4 * hid), F32)],
        [pltpu.VMEM((8, 16, 128), BF)],
        [info, tok, mask, *vec_arrays],
        [part1],
        us=5,
    )
    far1, far2, up_other, own_down, own_out = gate([far1, far2, up_other, own_down, own_out], [n1, *near])
    out_all = lax.all_gather(own_out, "fsdp", tiled=True)
    pairs = [[0, 2], [1, 3], [4, 6], [5, 7]]
    grad_pair = lax.all_gather(grad_v, "fsdp", axis_index_groups=pairs)
    attn = [(0, 0, w_qkv), (2, 0, qx), (4, 0, qy), (6, 0, far1), (6, half, far2)]
    attn += [(1, 0, near[0]), (3, 0, near[1]), (5, 0, near[2]), (7, 0, swap(far1, 1)), (7, half, swap(far2, 1))]
    attn_slots = tuple((p[0], p[1]) for p in attn)
    attn_arrays = [p[2] for p in attn]

    up_x, down_y = swap(up_other, 2), swap(own_down, 4)
    (qkv,) = call(
        functools.partial(qkv_kernel, attn_slots),
        [((total, 3 * width), BF)],
        [pltpu.VMEM((width, 3 * width), BF), pltpu.VMEM((1, 3 * width), F32), sem(len(attn))],
        [info, n1, vec],
        attn_arrays,
        us=8,
    )
    t = tick(t, [qkv, up_x])

    up_x, te1, te2, te3 = gate([up_x, te1, te2, te3], [t])
    up_two = jnp.stack([up_mine, up_x])
    up_y, up_c = swap(up_two, 4), swap(up_two, 1)
    te1, te3 = swap(te1, 2), swap(te3, 6)
    probs, ctx = call(
        attn_kernel,
        [((items * width // 128, 2 * ITEM, ITEM), BF), ((total, width), BF)],
        [],
        [info, qkv],
        [t],
        us=10,
    )
    t = tick(t, [ctx, up_y, up_c, te1, down_y])

    up_y, te1, te2, down_y = gate([up_y, te1, te2, down_y], [t])
    te2 = swap(te2, 4)
    down_two = jnp.stack([own_down, down_y])
    up_yc, down_c = swap(up_y, 1), swap(down_two, 1)
    h1, n2t, *n2v = call(
        functools.partial(out_kernel, text_rows),
        [((total, width), F32), ((slot_rows, width), BF)] + [((TEXT_AT, width), BF)] * items,
        [],
        [info, tok, mask, vec, ctx, out_all],
        [t],
        us=5,
    )
    t = tick(t, [n2t, te2, te3, up_yc, down_c])

    te1, te2, te3, n2t, *n2v = gate([te1, te2, te3, n2t, *n2v], [t])
    (pack,) = call(
        pack_kernel,
        [((2 * block + 4 * slot_rows, width), BF)],
        [],
        [info, strip0, te1, te2, te3, grad_t],
    )
    text_in = [swap(n2t, 2), swap(n2t, 4), swap(n2t, 6)]
    n2x = [swap(n2v[0], 2)]
    far = swap(pack, 1)
    weights = [up_two, up_y, up_c, up_yc, down_two, down_c]

    def vision(rows_in, grads, kind, after):
        return call(
            functools.partial(vision_kernel, kind == BF, items),
            [
                ((vision_rows, width), kind),
                ((vision_rows, width), kind),
                ((vision_rows, 4 * hid), BF),
                ((vision_rows, 4 * hid), BF),
            ],
            [
                pltpu.VMEM((width, 4 * hid), BF),
                pltpu.VMEM((4 * hid, width), BF),
                pltpu.VMEM((vision_rows, width), BF),
                sem(12),
            ],
            [info, grads, up_bias, *rows_in],
            [*weights, *after],
            us=9,
        )

    branch_own, gn2_own, act_own, low_own = vision(n2v, grad_v, F32, [pack])
    t = tick(t, [gn2_own, *text_in, n2x[0], far, grad_pair])

    far, *text_in = gate([far, *text_in], [t])
    text_four = jnp.stack([n2t, *text_in])
    text_odd = swap(text_four, 1)
    n2x += [swap(a, 2) for a in gate(n2v[1:], [t])]
    branch_keep, branch_send, gn2_keep, gn2_send, tu_keep, tu_send, td, text_bias_sum = call(
        text_kernel,
        [
            quad(slot_rows, width),
            quad(slot_rows, width),
            quad(slot_rows, width),
            quad(slot_rows, width),
            quad(block, hid),
            quad(block, hid),
            ((hid, width), BF),
            ((1, hid), F32),
        ],
        [
            pltpu.VMEM((width, hid), BF),
            pltpu.VMEM((8 * slot_rows, width), BF),
            pltpu.VMEM((8 * slot_rows, width), BF),
            pltpu.VMEM((width, 8 * slot_rows), BF),
        ],
        [
            info,
            text_down,
            text_up_bias.astype(F32).reshape(1, hid),
            strip0,
            te1,
            te2,
            te3,
            far,
            text_four,
            text_odd,
            grad_t,
        ],
        us=6,
    )
    t = tick(t, [gn2_keep, *n2x])
    tu_keep, tu_send, td = lax.psum((tu_keep, tu_send, td), "rep")

    gn2_send, *n2x = gate([gn2_send, *n2x], [t])
    gn2_sum = add(gn2_keep, swap(gn2_send, 1))
    gn2_text = [gn2_sum] + [swap(gn2_sum[s], 2 * s) for s in (1, 2, 3)]
    branch_x, gn2_x, act_x, low_x = vision(n2x, grad_pair, BF, [gn2_sum])
    t = tick(t, [gn2_x, *gn2_text[1:]])

    (gn2_x,) = gate([gn2_x], [t])
    gn2_back = swap(gn2_x, 2)
    vu_keep, vu_send, vd_keep, vd_send, vu_bias_sum = call(
        functools.partial(vision_grad_kernel, items),
        [
            quad(block, 4 * hid),
            quad(block, 4 * hid),
            ((2, hid, width), BF),
            ((2, hid, width), BF),
            ((1, 4 * hid), F32),
        ],
        [
            pltpu.VMEM((width, 2 * vision_rows), BF),
            pltpu.VMEM((4 * hid, 2 * vision_rows), BF),
            pltpu.VMEM((2 * vision_rows, width), BF),
            pltpu.VMEM((2 * vision_rows, 4 * hid), BF),
            pltpu.VMEM((width, vision_rows), BF),
            pltpu.VMEM((width, vision_rows), BF),
        ],
        [info, *n2v, *n2x, grad_pair, act_own, act_x, low_own, low_x],
        [t],
        us=12,
    )
    t = tick(t, [vu_bias_sum, gn2_back])

    vu_send, vd_send, branch_x, branch_send, gn2_back = gate([vu_send, vd_send, branch_x, branch_send, gn2_back], [t])
    vu_got, vd_got = swap(vu_send, 1), swap(vd_send, 1)
    vd_near, vd_far = add(vd_keep[0], vd_got[0]), add(vd_keep[1], vd_got[1])
    vu_far = [add(vu_keep[k], vu_got[k]) for k in (2, 3)]
    vd_y, vu_y1 = swap(vd_far, 4), swap(vu_far[1], 4)
    branch_back = swap(branch_x, 2)
    branch_got = swap(branch_send, 1)
    gh1, low_attn, stacked, sums_two = call(
        functools.partial(attn_bwd_kernel, text_rows),
        [((total, width), F32), ((total, width), BF), ((total, 3 * width), BF), ((8, width), F32)],
        [pltpu.VMEM((total, width), F32), pltpu.VMEM((total, width), BF)],
        [info, gn2_own, gn2_back, *gn2_text, grad, h1, vec, qkv, probs, out_all],
        [vd_far, *vu_far],
        us=18,
    )
    t = tick(t, [stacked, vd_y, vu_y1, branch_back, branch_got])

    vd_y, vu_y1, vu_far0, branch_got = gate([vd_y, vu_y1, vu_far[0], branch_got], [t])
    vd_sum = add(vd_near, vd_y)
    vu_x = swap(add(vu_keep[1], vu_got[1], vu_y1), 2)
    vu_y0 = swap(vu_far0, 4)

    def attn_grads(last, after):
        return call(
            functools.partial(attn_grad_kernel, last),
            [quad(block, 2 * width), quad(block, 2 * width)],
            [
                pltpu.VMEM((width, total), BF),
                pltpu.VMEM((width, total), BF),
                pltpu.VMEM((total, (1 if last else 2) * width), BF),
                sem(1),
            ],
            [info, n1, ctx, low_attn] if last else [info, n1],
            [stacked, *after],
            us=5,
        )

    a_keep, a_send = attn_grads(False, [t])
    t = tick(t, [a_keep, vu_x, vu_y0])
    a_send, vu_x, vu_y0 = gate([a_send, vu_x, vu_y0], [t])
    a_got = swap(a_send, 1)
    branch_sum = add(branch_keep, branch_got)
    vu_both = jnp.stack([add(vu_keep[0], vu_got[0], vu_y0), vu_x])
    vu, vd = lax.psum((vu_both, vd_sum), "rep", axis_index_groups=[[1, 0, 2, 3]])
    b_keep, b_send = attn_grads(True, [t])
    t = tick(t, [b_keep, a_got])
    a_got, b_send, branch_sum = gate([a_got, b_send, branch_sum], [t])
    b_got = swap(b_send, 1)

    def begin(keep, got, one):
        i = one // 2
        return add(jnp.stack([keep[i], keep[3]]), jnp.stack([got[i], got[3]]))

    a_first, b_first = begin(a_keep, a_got, 2), begin(b_keep, b_got, 4)
    a_there, b_there = swap(a_first, 2), swap(b_first, 4)
    branch_t = [branch_sum] + [swap(branch_sum[s], 2 * s) for s in (1, 2, 3)]
    gtok, sums_one = call(
        functools.partial(last_kernel, attn_slots),
        [((total, width), F32), ((8, width), F32)],
        [pltpu.VMEM((width, 3 * width), BF), sem(len(attn))],
        [info, stacked, gh1, tok, mask, vec],
        attn_arrays + [a_first, b_first, vu_both, vd_sum],
        us=12,
    )
    t = tick(t, [sums_one, a_there, b_there, *branch_t[1:]])

    a_there, b_there = gate([a_there, b_there], [t])
    a_next, b_next = add(a_keep[2], a_got[2], a_there[1]), add(b_keep[1], b_got[1], b_there[1])
    a_beyond, b_beyond = swap(a_next, 4), swap(b_next, 2)
    (sums_one,) = gate([sums_one], [tick(t, [a_next, b_next])])
    vu_sum = vu_bias_sum.reshape(2, 1, pair)
    vu_sum = jnp.where(
        side == 0,
        jnp.concatenate([vu_sum, jnp.zeros_like(vu_sum)], axis=1),
        jnp.concatenate([jnp.zeros_like(vu_sum), vu_sum], axis=1),
    )
    count, rows = len(names), hid // block
    vec_rows = count + 2 * rows
    vu_sum = vu_sum.reshape(8, rows, block).transpose(1, 0, 2).reshape(-1, width)
    flat = jnp.concatenate(
        [sums_one[0:3], sums_two[3:5], sums_two[2:3], sums_two[0:2], grad_sums, vu_sum], axis=0
    )
    for m in (1, 2, 4):
        flat = flat + swap(flat, m)
    own_sums = lax.dynamic_slice_in_dim(flat, me * block, block, axis=1)
    own_sums = jnp.concatenate([own_sums, text_bias_sum.reshape(-1, block)], axis=0)
    ga = add(a_keep[0], a_got[0], a_there[0], a_beyond)
    gb = add(b_keep[0], b_got[0], b_there[0], b_beyond)

    inner = (rep == 1) | (rep == 2)

    def rep_sum(array):
        part = add(array, along_rep(array, [(0, 1), (3, 2)]))
        whole = add(part, along_rep(part, [(1, 2), (2, 1)]))
        return jnp.where(inner, whole, along_rep(whole, [(1, 0), (2, 3)]))

    plane_sums = [ga, gb]
    own_sums = own_sums.reshape(-1)
    own_sums = jnp.pad(own_sums, (0, 8 * 2 * width - own_sums.shape[0])).reshape(8, 2 * width)
    ga, gb = rep_sum(jnp.concatenate([ga, own_sums.astype(BF)], axis=0)), rep_sum(gb)
    last_sums = [ga, gb]
    tu_keep, tu_send, td = gate([tu_keep, tu_send, td], plane_sums)
    tu_got = swap(tu_send, 1)
    tu_wide = jnp.where(
        core == 0,
        jnp.concatenate([tu_keep, tu_got], axis=-1),
        jnp.concatenate([tu_got, tu_keep], axis=-1),
    )
    tu_all = [tu_wide[0]] + [swap(tu_wide[s], 2 * s) for s in (1, 2, 3)]
    tu_x = [jnp.where(side == 0, tu_all[k], tu_all[k ^ 1]) for k in range(4)]
    tu_y = [jnp.where(me // 4 == 0, tu_x[k], tu_x[k ^ 2]) for k in range(4)]
    grad_text_up = jnp.concatenate(tu_y, axis=1).astype(F32)
    grad_text_down = td.astype(F32)

    ga = ga.astype(F32)
    mine = ga[block:].reshape(-1)[: vec_rows * block].reshape(vec_rows, block)
    ga = ga[:block]
    vec_grad = [mine[i] for i in range(count)]
    vu_bias_grad = mine[count : count + rows].reshape(-1)
    tu_bias_grad = mine[count + rows : count + 2 * rows].reshape(-1)

    vu, vd = gate([vu, vd], last_sums)
    gb = gb.astype(F32)
    grad_w_qkv = jnp.concatenate([ga, gb[:, :width]], axis=1)
    grad_w_out = gb[:, width:]
    vu_s = [jnp.where(side == 0, vu[k], vu[1 - k]) for k in range(2)]
    grad_vision_up = jnp.concatenate(
        [vu_s[0][:, :pair], vu_s[1][:, :pair], vu_s[0][:, pair:], vu_s[1][:, pair:]], axis=1
    ).astype(F32)
    grad_vision_down = vd.astype(F32)
    h1 = h1.reshape(items, ITEM, width)
    branch_v = (branch_own + branch_back.astype(F32)).reshape(items, TEXT_AT, width)[:, :patches]
    mixed_v = h1[:, :patches] + branch_v + vec[8][None, None]
    branch_t = branch_t[0][0].astype(F32) + sum(b.astype(F32) for b in branch_t[1:])
    branch_t = branch_t.reshape(items, text_rows, width)
    mixed_t = h1[:, TEXT_AT : TEXT_AT + text_rows] + branch_t + vec[9][None, None]
    mixed = jnp.concatenate([mixed_v.astype(BF), mixed_t.astype(BF)], axis=1)
    gtok = gtok.reshape(items, ITEM, width)
    grad_tokens = jnp.concatenate(
        [gtok[:, :patches], gtok[:, TEXT_AT : TEXT_AT + text_rows]], axis=1
    )
    return (
        mixed,
        grad_tokens,
        vec_grad[0],
        vec_grad[1],
        vec_grad[2],
        grad_w_qkv,
        vec_grad[3],
        vec_grad[4],
        grad_w_out,
        vec_grad[5],
        vec_grad[6],
        vec_grad[7],
        grad_vision_up,
        vu_bias_grad,
        grad_vision_down,
        vec_grad[8],
        grad_text_up,
        tu_bias_grad,
        grad_text_down,
        vec_grad[9],
    )


def layer_norm(hidden, gain, shift):
    center = hidden - jnp.mean(hidden, axis=-1, keepdims=True)
    spread = jnp.mean(center * center, axis=-1, keepdims=True)
    return center * lax.rsqrt(spread + epsilon) * gain + shift


def exact_gelu(values):
    return jax.nn.gelu(values, approximate=False)


def expert_forward(rows_in, up_matrix, up_shift, down_matrix, down_shift):
    upper = jnp.dot(rows_in, up_matrix, preferred_element_type=jnp.float32) + up_shift.astype(
        jnp.float32
    )
    active, gelu_pull = jax.vjp(exact_gelu, upper)
    active_b = active.astype(jnp.bfloat16)
    result = jnp.dot(active_b, down_matrix, preferred_element_type=jnp.float32) + down_shift.astype(
        jnp.float32
    )
    return (result, active_b, gelu_pull)


def expert_backward(rows_in, active_b, gelu_pull, up_matrix, down_matrix, grad_b):
    grad_down = jnp.einsum("rf,rd->fd", active_b, grad_b, preferred_element_type=jnp.float32)
    grad_down_shift = jnp.sum(grad_b.astype(jnp.float32), axis=0)
    grad_active = jnp.einsum("rd,fd->rf", grad_b, down_matrix, preferred_element_type=jnp.float32)
    (grad_upper,) = gelu_pull(grad_active)
    upper_b = grad_upper.astype(jnp.bfloat16)
    grad_up = jnp.einsum("rd,rf->df", rows_in, upper_b, preferred_element_type=jnp.float32)
    grad_up_shift = jnp.sum(upper_b.astype(jnp.float32), axis=0)
    grad_rows = jnp.einsum("rf,df->rd", upper_b, up_matrix, preferred_element_type=jnp.float32)
    return (grad_up, grad_up_shift, grad_down, grad_down_shift, grad_rows)


def general(
    tokens,
    out_grad,
    masked,
    lengths,
    mask_vec,
    norm1_gain,
    norm1_shift,
    w_qkv,
    query_bias,
    value_bias,
    w_out,
    out_bias,
    norm2_gain,
    norm2_shift,
    vision_up,
    vision_up_bias,
    vision_down,
    vision_down_bias,
    text_up,
    text_up_bias,
    text_down,
    text_down_bias,
):
    item_count, row_count, model_width = tokens.shape
    slot_count = masked.shape[1]
    patches = row_count - slot_count
    head_count = model_width // HEAD_DIM
    split_shape = (item_count, row_count, head_count, HEAD_DIM)

    def fetch_attention():
        return (
            lax.all_gather(mask_vec, "fsdp", axis=0, tiled=True),
            lax.all_gather(norm1_gain, "fsdp", axis=0, tiled=True),
            lax.all_gather(norm1_shift, "fsdp", axis=0, tiled=True),
            lax.all_gather(w_qkv, "fsdp", axis=0, tiled=True),
            lax.all_gather(query_bias, "fsdp", axis=0, tiled=True),
            lax.all_gather(value_bias, "fsdp", axis=0, tiled=True),
            lax.all_gather(w_out, "fsdp", axis=0, tiled=True),
            lax.all_gather(out_bias, "fsdp", axis=0, tiled=True),
        )

    def fetch_feedforward():
        return (
            lax.all_gather(norm2_gain, "fsdp", axis=0, tiled=True),
            lax.all_gather(norm2_shift, "fsdp", axis=0, tiled=True),
            lax.all_gather(vision_up, "fsdp", axis=0, tiled=True),
            lax.all_gather(vision_up_bias, "fsdp", axis=0, tiled=True),
            lax.all_gather(vision_down, "fsdp", axis=0, tiled=True),
            lax.all_gather(vision_down_bias, "fsdp", axis=0, tiled=True),
            lax.all_gather(text_up, "fsdp", axis=0, tiled=True),
            lax.all_gather(text_up_bias, "fsdp", axis=0, tiled=True),
            lax.all_gather(text_down, "fsdp", axis=0, tiled=True),
            lax.all_gather(text_down_bias, "fsdp", axis=0, tiled=True),
        )

    attn_full = fetch_attention()
    full_mask, gain_one, shift_one, qkv_matrix, query_shift, value_shift, out_matrix, out_shift = (
        attn_full
    )
    mask_rows = jnp.concatenate(
        [jnp.zeros((item_count, patches), jnp.float32), masked.astype(jnp.float32)], axis=1
    )[:, :, None]
    hidden0 = mask_rows * full_mask.astype(jnp.float32) + (1.0 - mask_rows) * tokens.astype(
        jnp.float32
    )
    normed1, first_pull = jax.vjp(
        layer_norm, hidden0, gain_one.astype(jnp.float32), shift_one.astype(jnp.float32)
    )
    first_in = normed1.astype(jnp.bfloat16).reshape(item_count * row_count, model_width)
    projected = jnp.dot(first_in, qkv_matrix, preferred_element_type=jnp.float32)
    query_b = (
        ((projected[:, :model_width] + query_shift.astype(jnp.float32)) * 0.125)
        .astype(jnp.bfloat16)
        .reshape(split_shape)
    )
    key_b = projected[:, model_width : 2 * model_width].astype(jnp.bfloat16).reshape(split_shape)
    value_b = (
        (projected[:, 2 * model_width :] + value_shift.astype(jnp.float32))
        .astype(jnp.bfloat16)
        .reshape(split_shape)
    )
    key_index = jnp.arange(row_count, dtype=jnp.int32)
    valid_keys = (key_index[None, :] < patches + lengths[:, None])[:, None, None, :]

    def scores_of():
        raw_scores = jnp.einsum(
            "iqhd,ikhd->ihqk", query_b, key_b, preferred_element_type=jnp.float32
        )
        return jnp.where(valid_keys, raw_scores, -1000000000.0)

    scores = scores_of()
    top_score = jnp.max(scores, axis=-1, keepdims=True)
    expo = jnp.exp(scores - top_score)
    totals = jnp.sum(expo, axis=-1, keepdims=True)
    probs = expo / totals
    log_total = top_score + jnp.log(totals)
    context = jnp.einsum(
        "ihqk,ikhd->iqhd", probs.astype(jnp.bfloat16), value_b, preferred_element_type=jnp.float32
    )
    context_b = context.reshape(item_count * row_count, model_width).astype(jnp.bfloat16)
    attended = jnp.dot(
        context_b, out_matrix, preferred_element_type=jnp.float32
    ) + out_shift.astype(jnp.float32)
    hidden1 = hidden0 + attended.reshape(item_count, row_count, model_width)
    ffn_full = fetch_feedforward()
    (
        gain_two,
        shift_two,
        vision_upm,
        vision_upb,
        vision_downm,
        vision_downb,
        text_upm,
        text_upb,
        text_downm,
        text_downb,
    ) = ffn_full
    normed2, second_pull = jax.vjp(
        layer_norm, hidden1, gain_two.astype(jnp.float32), shift_two.astype(jnp.float32)
    )
    second_in = normed2.astype(jnp.bfloat16)
    patch_in = second_in[:, :patches].reshape(-1, model_width)
    text_in = second_in[:, patches:].reshape(-1, model_width)
    vision_out, vision_act, vision_pull = expert_forward(
        patch_in, vision_upm, vision_upb, vision_downm, vision_downb
    )
    text_out, text_act, text_pull = expert_forward(
        text_in, text_upm, text_upb, text_downm, text_downb
    )
    mixed = hidden1 + jnp.concatenate(
        [
            vision_out.reshape(item_count, patches, model_width),
            text_out.reshape(item_count, slot_count, model_width),
        ],
        axis=1,
    )
    cotangent = out_grad.astype(jnp.float32)
    branch_b = cotangent.astype(jnp.bfloat16)
    ffn_back = fetch_feedforward()
    vision_grads = expert_backward(
        patch_in,
        vision_act,
        vision_pull,
        ffn_back[2],
        ffn_back[4],
        branch_b[:, :patches].reshape(-1, model_width),
    )
    text_grads = expert_backward(
        text_in,
        text_act,
        text_pull,
        ffn_back[6],
        ffn_back[8],
        branch_b[:, patches:].reshape(-1, model_width),
    )
    grad_normed2 = jnp.concatenate(
        [
            vision_grads[4].reshape(item_count, patches, model_width),
            text_grads[4].reshape(item_count, slot_count, model_width),
        ],
        axis=1,
    )
    grad_hidden1_norm, grad_gain_two, grad_shift_two = second_pull(grad_normed2)
    grad_hidden1 = cotangent + grad_hidden1_norm
    attn_back = fetch_attention()
    grad_attn_b = grad_hidden1.reshape(-1, model_width).astype(jnp.bfloat16)
    grad_out_matrix = jnp.einsum(
        "rd,re->de", context_b, grad_attn_b, preferred_element_type=jnp.float32
    )
    grad_out_shift = jnp.sum(grad_attn_b.astype(jnp.float32), axis=0)
    grad_context = jnp.einsum(
        "re,de->rd", grad_attn_b, attn_back[6], preferred_element_type=jnp.float32
    )
    grad_context_b = grad_context.astype(jnp.bfloat16).reshape(split_shape)
    again_probs = jnp.exp(scores_of() - log_total)
    grad_probs = jnp.einsum(
        "iqhd,ikhd->ihqk", grad_context_b, value_b, preferred_element_type=jnp.float32
    )
    grad_value = jnp.einsum(
        "ihqk,iqhd->ikhd",
        again_probs.astype(jnp.bfloat16),
        grad_context_b,
        preferred_element_type=jnp.float32,
    )
    row_inner = jnp.sum(again_probs * grad_probs, axis=-1, keepdims=True)
    grad_scores_b = (again_probs * (grad_probs - row_inner)).astype(jnp.bfloat16)
    grad_query = jnp.einsum(
        "ihqk,ikhd->iqhd", grad_scores_b, key_b, preferred_element_type=jnp.float32
    )
    grad_key = jnp.einsum(
        "ihqk,iqhd->ikhd", grad_scores_b, query_b, preferred_element_type=jnp.float32
    )
    grad_query_b = grad_query.astype(jnp.bfloat16) * jnp.bfloat16(0.125)
    stacked = jnp.concatenate(
        [
            grad_query_b.reshape(-1, model_width),
            grad_key.astype(jnp.bfloat16).reshape(-1, model_width),
            grad_value.astype(jnp.bfloat16).reshape(-1, model_width),
        ],
        axis=1,
    )
    grad_qkv = jnp.einsum("rd,re->de", first_in, stacked, preferred_element_type=jnp.float32)
    grad_query_shift = jnp.sum(stacked[:, :model_width].astype(jnp.float32), axis=0)
    grad_value_shift = jnp.sum(stacked[:, 2 * model_width :].astype(jnp.float32), axis=0)
    grad_normed1 = jnp.einsum(
        "re,de->rd", stacked, attn_back[3], preferred_element_type=jnp.float32
    )
    grad_hidden0_norm, grad_gain_one, grad_shift_one = first_pull(
        grad_normed1.reshape(item_count, row_count, model_width)
    )
    grad_hidden0 = grad_hidden1 + grad_hidden0_norm
    grad_tokens = grad_hidden0 * (1.0 - mask_rows)
    grad_mask = jnp.sum(grad_hidden0 * mask_rows, axis=(0, 1))
    ffn_share = (
        lax.psum_scatter(grad_gain_two, "fsdp", scatter_dimension=0, tiled=True),
        lax.psum_scatter(grad_shift_two, "fsdp", scatter_dimension=0, tiled=True),
        lax.psum_scatter(vision_grads[0], "fsdp", scatter_dimension=0, tiled=True),
        lax.psum_scatter(vision_grads[1], "fsdp", scatter_dimension=0, tiled=True),
        lax.psum_scatter(vision_grads[2], "fsdp", scatter_dimension=0, tiled=True),
        lax.psum_scatter(vision_grads[3], "fsdp", scatter_dimension=0, tiled=True),
        lax.psum_scatter(text_grads[0], "fsdp", scatter_dimension=0, tiled=True),
        lax.psum_scatter(text_grads[1], "fsdp", scatter_dimension=0, tiled=True),
        lax.psum_scatter(text_grads[2], "fsdp", scatter_dimension=0, tiled=True),
        lax.psum_scatter(text_grads[3], "fsdp", scatter_dimension=0, tiled=True),
    )
    attn_share = (
        lax.psum_scatter(grad_mask, "fsdp", scatter_dimension=0, tiled=True),
        lax.psum_scatter(grad_gain_one, "fsdp", scatter_dimension=0, tiled=True),
        lax.psum_scatter(grad_shift_one, "fsdp", scatter_dimension=0, tiled=True),
        lax.psum_scatter(grad_qkv, "fsdp", scatter_dimension=0, tiled=True),
        lax.psum_scatter(grad_query_shift, "fsdp", scatter_dimension=0, tiled=True),
        lax.psum_scatter(grad_value_shift, "fsdp", scatter_dimension=0, tiled=True),
        lax.psum_scatter(grad_out_matrix, "fsdp", scatter_dimension=0, tiled=True),
        lax.psum_scatter(grad_out_shift, "fsdp", scatter_dimension=0, tiled=True),
    )
    quarter = (
        lax.psum_scatter(
            attn_share[0].astype(jnp.bfloat16), "rep", scatter_dimension=0, tiled=True
        ).astype(jnp.float32),
        lax.psum_scatter(
            attn_share[1].astype(jnp.bfloat16), "rep", scatter_dimension=0, tiled=True
        ).astype(jnp.float32),
        lax.psum_scatter(
            attn_share[2].astype(jnp.bfloat16), "rep", scatter_dimension=0, tiled=True
        ).astype(jnp.float32),
        lax.psum_scatter(
            attn_share[3].astype(jnp.bfloat16), "rep", scatter_dimension=0, tiled=True
        ).astype(jnp.float32),
        lax.psum_scatter(
            attn_share[4].astype(jnp.bfloat16), "rep", scatter_dimension=0, tiled=True
        ).astype(jnp.float32),
        lax.psum_scatter(
            attn_share[5].astype(jnp.bfloat16), "rep", scatter_dimension=0, tiled=True
        ).astype(jnp.float32),
        lax.psum_scatter(
            attn_share[6].astype(jnp.bfloat16), "rep", scatter_dimension=0, tiled=True
        ).astype(jnp.float32),
        lax.psum_scatter(
            attn_share[7].astype(jnp.bfloat16), "rep", scatter_dimension=0, tiled=True
        ).astype(jnp.float32),
        lax.psum_scatter(
            ffn_share[0].astype(jnp.bfloat16), "rep", scatter_dimension=0, tiled=True
        ).astype(jnp.float32),
        lax.psum_scatter(
            ffn_share[1].astype(jnp.bfloat16), "rep", scatter_dimension=0, tiled=True
        ).astype(jnp.float32),
        lax.psum_scatter(
            ffn_share[2].astype(jnp.bfloat16), "rep", scatter_dimension=0, tiled=True
        ).astype(jnp.float32),
        lax.psum_scatter(
            ffn_share[3].astype(jnp.bfloat16), "rep", scatter_dimension=0, tiled=True
        ).astype(jnp.float32),
        lax.psum_scatter(
            ffn_share[4].astype(jnp.bfloat16), "rep", scatter_dimension=0, tiled=True
        ).astype(jnp.float32),
        lax.psum_scatter(
            ffn_share[5].astype(jnp.bfloat16), "rep", scatter_dimension=0, tiled=True
        ).astype(jnp.float32),
        lax.psum_scatter(
            ffn_share[6].astype(jnp.bfloat16), "rep", scatter_dimension=0, tiled=True
        ).astype(jnp.float32),
        lax.psum_scatter(
            ffn_share[7].astype(jnp.bfloat16), "rep", scatter_dimension=0, tiled=True
        ).astype(jnp.float32),
        lax.psum_scatter(
            ffn_share[8].astype(jnp.bfloat16), "rep", scatter_dimension=0, tiled=True
        ).astype(jnp.float32),
        lax.psum_scatter(
            ffn_share[9].astype(jnp.bfloat16), "rep", scatter_dimension=0, tiled=True
        ).astype(jnp.float32),
    )
    summed = (
        lax.all_gather(quarter[0].astype(jnp.bfloat16), "rep", axis=0, tiled=True).astype(
            jnp.float32
        ),
        lax.all_gather(quarter[1].astype(jnp.bfloat16), "rep", axis=0, tiled=True).astype(
            jnp.float32
        ),
        lax.all_gather(quarter[2].astype(jnp.bfloat16), "rep", axis=0, tiled=True).astype(
            jnp.float32
        ),
        lax.all_gather(quarter[3].astype(jnp.bfloat16), "rep", axis=0, tiled=True).astype(
            jnp.float32
        ),
        lax.all_gather(quarter[4].astype(jnp.bfloat16), "rep", axis=0, tiled=True).astype(
            jnp.float32
        ),
        lax.all_gather(quarter[5].astype(jnp.bfloat16), "rep", axis=0, tiled=True).astype(
            jnp.float32
        ),
        lax.all_gather(quarter[6].astype(jnp.bfloat16), "rep", axis=0, tiled=True).astype(
            jnp.float32
        ),
        lax.all_gather(quarter[7].astype(jnp.bfloat16), "rep", axis=0, tiled=True).astype(
            jnp.float32
        ),
        lax.all_gather(quarter[8].astype(jnp.bfloat16), "rep", axis=0, tiled=True).astype(
            jnp.float32
        ),
        lax.all_gather(quarter[9].astype(jnp.bfloat16), "rep", axis=0, tiled=True).astype(
            jnp.float32
        ),
        lax.all_gather(quarter[10].astype(jnp.bfloat16), "rep", axis=0, tiled=True).astype(
            jnp.float32
        ),
        lax.all_gather(quarter[11].astype(jnp.bfloat16), "rep", axis=0, tiled=True).astype(
            jnp.float32
        ),
        lax.all_gather(quarter[12].astype(jnp.bfloat16), "rep", axis=0, tiled=True).astype(
            jnp.float32
        ),
        lax.all_gather(quarter[13].astype(jnp.bfloat16), "rep", axis=0, tiled=True).astype(
            jnp.float32
        ),
        lax.all_gather(quarter[14].astype(jnp.bfloat16), "rep", axis=0, tiled=True).astype(
            jnp.float32
        ),
        lax.all_gather(quarter[15].astype(jnp.bfloat16), "rep", axis=0, tiled=True).astype(
            jnp.float32
        ),
        lax.all_gather(quarter[16].astype(jnp.bfloat16), "rep", axis=0, tiled=True).astype(
            jnp.float32
        ),
        lax.all_gather(quarter[17].astype(jnp.bfloat16), "rep", axis=0, tiled=True).astype(
            jnp.float32
        ),
    )
    return (
        mixed.astype(jnp.bfloat16),
        grad_tokens,
        summed[0],
        summed[1],
        summed[2],
        summed[3],
        summed[4],
        summed[5],
        summed[6],
        summed[7],
        summed[8],
        summed[9],
        summed[10],
        summed[11],
        summed[12],
        summed[13],
        summed[14],
        summed[15],
        summed[16],
        summed[17],
    )


def solution(mesh):
    if mesh.shape["fsdp"] == 8 and mesh.shape["rep"] == 4:
        body = planned
    else:
        body = general
    return jax.shard_map(
        body,
        mesh=mesh,
        in_specs=(
            P(("fsdp", "rep"), None, None),
            P(("fsdp", "rep"), None, None),
            P(("fsdp", "rep"), None),
            P(("fsdp", "rep")),
            P("fsdp"),
            P("fsdp"),
            P("fsdp"),
            P("fsdp", None),
            P("fsdp"),
            P("fsdp"),
            P("fsdp", None),
            P("fsdp"),
            P("fsdp"),
            P("fsdp"),
            P("fsdp", None),
            P("fsdp"),
            P("fsdp", None),
            P("fsdp"),
            P("fsdp", None),
            P("fsdp"),
            P("fsdp", None),
            P("fsdp"),
        ),
        out_specs=(
            P(("fsdp", "rep"), None, None),
            P(("fsdp", "rep"), None, None),
            P("fsdp"),
            P("fsdp"),
            P("fsdp"),
            P("fsdp", None),
            P("fsdp"),
            P("fsdp"),
            P("fsdp", None),
            P("fsdp"),
            P("fsdp"),
            P("fsdp"),
            P("fsdp", None),
            P("fsdp"),
            P("fsdp", None),
            P("fsdp"),
            P("fsdp", None),
            P("fsdp"),
            P("fsdp", None),
            P("fsdp"),
        ),
        check_vma=False,
    )
```

```python
import functools
import math

import jax
import jax.numpy as jnp
from jax import lax
from jax.experimental import pallas as pl
from jax.experimental.pallas import tpu as pltpu
from jax.sharding import PartitionSpec as P

HEAD_DIM = 64
BF = jnp.bfloat16
F32 = jnp.float32
epsilon = 1e-06
VMEM_LIMIT = 58 * 1024 * 1024

ITEM = 256
SCALE = 0.2
TEXT_AT = 208


def cdiv(a, b):
    return -(-a // b)


def dot_nn(a, b):
    return lax.dot_general(a, b, (((1,), (0,)), ((), ())), preferred_element_type=F32)


def dot_nt(a, b):
    return lax.dot_general(a, b, (((1,), (1,)), ((), ())), preferred_element_type=F32)


def dot_tn(a, b):
    return lax.dot_general(a, b, (((0,), (0,)), ((), ())), preferred_element_type=F32)


def gelu_parts(upper):
    half = 0.5 * (1.0 + lax.erf(upper * math.sqrt(0.5)))
    slope = half + upper * (jnp.exp(-0.5 * upper * upper) * (1.0 / math.sqrt(2.0 * math.pi)))
    return upper * half, slope


def normalize(hidden):
    center = hidden - jnp.mean(hidden, axis=-1, keepdims=True)
    spread = jnp.mean(center * center, axis=-1, keepdims=True)
    scale = lax.rsqrt(spread + epsilon)
    return center * scale, scale


def start_rows(pieces, target, me, sems):
    block = target.shape[0] // 8
    copies = []
    for index, (slot, first, ref) in enumerate(pieces):
        row = pl.multiple_of((me ^ slot) * block + first, 16)
        copy = pltpu.make_async_copy(ref, target.at[pl.ds(row, ref.shape[0])], sems.at[index])
        copy.start()
        copies.append(copy)
    return copies


def mixed_in(tok, mask, vec, rows):
    keep = mask[rows, :]
    return keep * vec[0:1, :] + (1.0 - keep) * tok[rows, :].astype(F32)


def gate_kernel(count, *refs):
    del count, refs


def gate(arrays, after):
    count = len(arrays)
    return pl.pallas_call(
        functools.partial(gate_kernel, count),
        out_shape=[jax.ShapeDtypeStruct(a.shape, a.dtype) for a in arrays],
        in_specs=[pl.BlockSpec(memory_space=pl.ANY)] * (count + len(after)),
        out_specs=[pl.BlockSpec(memory_space=pl.ANY)] * count,
        input_output_aliases={i: i for i in range(count)},
        cost_estimate=pl.CostEstimate(flops=1000, bytes_accessed=1000, transcendentals=0),
    )(*arrays, *after)


def tick(token, after):
    return gate([token], after)[0]


def prep_kernel(text_rows, info, tokens, out_grad, w_out, down, up, text_up, *outs):
    tok, grad, grad_v, grad_t, sums, out_copy, down_copy, up_mine, up_other, strip0, te1, te2, te3, token = outs
    token[...] = jnp.zeros(token.shape, F32)
    items, row_count, width = tokens.shape
    patches = row_count - text_rows
    tail = ITEM - TEXT_AT - text_rows
    zeros = lambda n: jnp.zeros((n, width), F32)
    totals = [zeros(1), zeros(1)]
    texts = []
    for i in range(items):
        for source, target in ((tokens, tok), (out_grad, grad)):
            whole = source[i].astype(F32)
            patch, text = whole[:patches], whole[patches:]
            full = jnp.concatenate([patch, zeros(TEXT_AT - patches), text, zeros(tail)], axis=0)
            target[pl.ds(i * ITEM, ITEM), :] = full.astype(BF)
            if target is grad:
                grad_v[pl.ds(i * TEXT_AT, TEXT_AT), :] = full[:TEXT_AT].astype(BF)
                texts.append(text)
                totals[0] = totals[0] + jnp.sum(patch, axis=0, keepdims=True)
                totals[1] = totals[1] + jnp.sum(text, axis=0, keepdims=True)
    slots = jnp.concatenate(texts, axis=0).astype(BF)
    grad_t[...] = slots
    sums[0:1, :] = totals[0]
    sums[1:2, :] = totals[1]
    out_copy[...] = w_out[...]
    down_copy[...] = down[...]
    chip = info[0] // 2
    side = chip % 2
    block = up.shape[0]
    pair = 2 * down.shape[0]
    strip = lambda ref, c: ref[:, pl.ds(pl.multiple_of(c * pair, 128), pair)]
    for k in range(2):
        up_mine[:, k * pair : (k + 1) * pair] = strip(up, side + 2 * k)
        up_other[:, k * pair : (k + 1) * pair] = strip(up, 1 - side + 2 * k)
    strip0[...] = strip(text_up, chip)
    for k, target in ((1, te1), (2, te2), (3, te3)):
        target[pl.ds(0, block), :] = strip(text_up, chip ^ k)
        target[pl.ds(block, slots.shape[0]), :] = slots


def norm_kernel(info, tok, mask, even, odd, *refs):
    n1, vec, up_bias, shards = refs[-4:]
    me = info[0]
    total, width = tok.shape
    block = width // 8
    for slot in range(8):
        shards[me ^ slot] = (even, odd)[slot % 2][slot // 2]
    wide = jnp.concatenate([shards[b] for b in range(8)], axis=1)
    lane = lax.broadcasted_iota(jnp.int32, (1024, width), 0)
    to = lax.broadcasted_iota(jnp.int32, (1024, width), 1)
    spread = ((lane // 128) * block + lane % 128 == to) & (lane % 128 < block)
    vec[...] = dot_nn(wide, jnp.where(spread, 1.0, 0.0).astype(BF))
    hid = up_bias.shape[1] // 4
    for q in range(4):
        b = (q // 2) * 4 + q % 2 + ((me // 2) % 2) * 2
        for r in range(hid // 128):
            at = q * hid + r * 128
            up_bias[0:1, at : at + 128] = shards[b, 10 + r : 11 + r, :].astype(F32)

    @pl.loop(0, total // 64)
    def _(step):
        rows = pl.ds(pl.multiple_of(step * 64, 64), 64)
        normal, _unused = normalize(mixed_in(tok, mask, vec, rows))
        n1[rows, :] = (normal * vec[1:2, :] + vec[2:3, :]).astype(BF)


def qkv_kernel(slots, info, n1, vec, *refs):
    count = len(slots)
    pieces = refs[:count]
    qkv, weight, bias, sems = refs[-4:]
    width = n1.shape[1]
    copies = start_rows([(s, f, r) for (s, f), r in zip(slots, pieces)], weight, info[0], sems)
    bias[0:1, 0:width] = vec[3:4, :]
    bias[0:1, width : 2 * width] = jnp.zeros((1, width), F32)
    bias[0:1, 2 * width : 3 * width] = vec[4:5, :]
    for copy in copies:
        copy.wait()

    @pl.loop(0, 3 * width // 256)
    def _(step):
        cols = pl.ds(pl.multiple_of(step * 256, 256), 256)
        factor = jnp.where(step < width // 256, 0.125, 1.0).astype(F32)
        out = dot_nn(n1[...], weight[:, cols])
        qkv[:, cols] = ((out + bias[0:1, cols]) * factor).astype(BF)


def attn_kernel(info, qkv, *refs):
    probs, ctx = refs[-2:]
    total, width = ctx.shape
    items = total // ITEM
    pairs = width // 128
    patches = info[3]

    @pl.loop(0, items * pairs)
    def _(step):
        item, pair = step // pairs, step % pairs
        rows = pl.ds(pl.multiple_of(item * ITEM, ITEM), ITEM)
        lane = lambda part: pl.ds(pl.multiple_of(part * width + pair * 128, 128), 128)
        q2, k2, v2 = qkv[rows, lane(0)], qkv[rows, lane(1)], qkv[rows, lane(2)]
        low = lax.broadcasted_iota(jnp.int32, (ITEM, 128), 1) < HEAD_DIM
        zero = jnp.zeros_like(q2)
        both = jnp.concatenate([jnp.where(low, q2, zero), jnp.where(low, zero, q2)], axis=0)
        scores = dot_nt(both, k2)
        col = lax.broadcasted_iota(jnp.int32, (1, ITEM), 1)
        valid = (col < patches) | ((col >= TEXT_AT) & (col < TEXT_AT + info[1 + item]))
        scores = jnp.where(valid, scores, -1000000000.0)
        expo = jnp.exp(scores - jnp.max(scores, axis=-1, keepdims=True))
        prob = (expo * (1.0 / jnp.sum(expo, axis=-1, keepdims=True))).astype(BF)
        probs[step] = prob
        wide = jnp.concatenate([prob[:ITEM], prob[ITEM:]], axis=1)
        values = jnp.concatenate([jnp.where(low, v2, zero), jnp.where(low, zero, v2)], axis=0)
        ctx[rows, pl.ds(pl.multiple_of(pair * 128, 128), 128)] = dot_nn(wide, values).astype(BF)


def out_kernel(text_rows, info, tok, mask, vec, ctx, out_w, *refs):
    h1, n2t, *n2v = refs[-2 - tok.shape[0] // ITEM :]
    items = tok.shape[0] // ITEM
    texts = []
    for i in range(items):
        for at, size in ((0, TEXT_AT), (TEXT_AT, ITEM - TEXT_AT)):
            rows = pl.ds(i * ITEM + at, size)
            attended = dot_nn(ctx[rows, :], out_w[...]) + vec[5:6, :]
            hidden = mixed_in(tok, mask, vec, rows) + attended
            h1[rows, :] = hidden
            normal, _unused = normalize(hidden)
            second = normal * vec[6:7, :] + vec[7:8, :]
            if at == 0:
                n2v[i][...] = second.astype(BF)
            else:
                texts.append(second[:text_rows])
    n2t[...] = jnp.concatenate(texts, axis=0).astype(BF)


def pack_kernel(info, strip0, te1, te2, te3, grad_t, pack):
    block, hid = strip0.shape[0], strip0.shape[1] // 2
    rows = grad_t.shape[0]
    other = pl.ds(pl.multiple_of((1 - info[0] % 2) * hid, 128), hid)
    for k, ref in enumerate((strip0, te1, te2, te3)):
        at = (k // 2) * block
        pack[at : at + block, (k % 2) * hid : (k % 2 + 1) * hid] = ref[pl.ds(0, block), other]
        there = pl.ds(2 * block + k * rows, rows)
        pack[there, :] = grad_t[...] if k == 0 else ref[pl.ds(block, rows), :]


def up_rows(me, pieces, target, sems):
    block = target.shape[0] // 8
    copies = []
    for index, (base, ref) in enumerate(pieces):
        for k in range(2):
            row = pl.multiple_of((me ^ (base + 2 * k)) * block, 16)
            sem = sems.at[2 * index + k]
            copies.append(pltpu.make_async_copy(ref.at[k], target.at[pl.ds(row, block)], sem))
    for copy in copies:
        copy.start()
    return copies


def place_of(me):
    return (me // 4) * 2 + me % 2


def vision_kernel(pair, items, info, grad, up_bias, *refs):
    parts, refs = refs[:items], refs[items:]
    ups, downs = refs[:4], refs[4:6]
    branch, gn2, act, low, up_w, down_w, rows_in, sems = refs[-8:]
    me = info[0]
    block = downs[0].shape[1]
    copies = up_rows(me, list(zip((0, 4, 1, 5), ups)), up_w, sems)
    place = place_of(me)
    for j in range(4):
        row = pl.multiple_of((place ^ j) * block, 16)
        copy = pltpu.make_async_copy(downs[j % 2].at[j // 2], down_w.at[pl.ds(row, block)], sems.at[8 + j])
        copy.start()
        copies.append(copy)
    for copy in copies:
        copy.wait()
    mine = grad.at[(me // 2) % 2 ^ 1] if pair else grad
    for i, part in enumerate(parts):
        rows_in[pl.ds(i * TEXT_AT, TEXT_AT), :] = part[...]
    chunk = 512
    for step in range(down_w.shape[0] // chunk):
        cols = slice(step * chunk, (step + 1) * chunk)
        upper = dot_nn(rows_in[...], up_w[:, cols]) + up_bias[0:1, cols]
        active, slope = gelu_parts(upper)
        active = active.astype(BF)
        act[:, cols] = active
        back = (dot_nt(mine[...], down_w[cols, :]) * slope).astype(BF)
        low[:, cols] = back
        if step == 0:
            sum_branch = dot_nn(active, down_w[cols, :])
            sum_gn2 = dot_nt(back, up_w[:, cols])
        else:
            sum_branch = sum_branch + dot_nn(active, down_w[cols, :])
            sum_gn2 = sum_gn2 + dot_nt(back, up_w[:, cols])
    branch[...] = sum_branch.astype(branch.dtype)
    gn2[...] = sum_gn2.astype(gn2.dtype)


def vision_grad_kernel(items, info, *refs):
    ins = refs[:items], refs[items : 2 * items]
    grads, refs = refs[2 * items], refs[2 * items + 1 :]
    acts, lows = refs[:2], refs[2:4]
    up_keep, up_send, down_keep, down_send, bias_sums = refs[-11:-6]
    left_t, act_t, right, low, turn0, turn1 = refs[-6:]
    me = info[0]
    rows, width = items * ins[0][0].shape[0], ins[0][0].shape[1]
    block = width // 8
    half = down_keep.shape[1]
    place, core = place_of(me), me % 2
    for k in range(2):
        at = pl.ds(k * rows, rows)
        right[at, :] = grads[(me // 2) % 2 ^ k]
        low[at, :] = lows[k][...]
        turned = jnp.concatenate([ref[...] for ref in ins[k]], axis=0).T
        turn = (turn0, turn1)[k]
        for b in range(8):
            spot = pl.multiple_of((me ^ b) * block, 16)
            turn[pl.ds(spot, block), :] = turned[b * block : (b + 1) * block]
        left_t[:, at] = turn[...]
        act_t[:, at] = acts[k][...].T
    chunk = 512
    for step in range(4 * half // chunk):
        cols = slice(step * chunk, (step + 1) * chunk)
        grad_up = dot_nn(left_t[...], low[:, cols])
        bias_sums[0:1, cols] = jnp.sum(low[:, cols].astype(F32), axis=0, keepdims=True)
        grad_up = grad_up.astype(BF)
        for b in range(4):
            up_keep[b, :, cols] = grad_up[2 * b * block : (2 * b + 1) * block]
            up_send[b, :, cols] = grad_up[(2 * b + 1) * block : (2 * b + 2) * block]
    for q in range(4):
        grad_down = dot_nn(act_t[q * half : (q + 1) * half, :], right[...]).astype(BF)
        side = (q // 2) ^ (place // 2)

        @pl.when(core == q % 2)
        def _():
            down_keep[side] = grad_down

        @pl.when(core != q % 2)
        def _():
            down_send[side] = grad_down


def text_kernel(info, down, up_bias, strip0, te1, te2, te3, far, even, odd, *refs):
    grad0, refs = refs[0], refs[1:]
    branch_keep, branch_send, gn2_keep, gn2_send, up_keep, up_send, grad_down, bias_sums = refs[-12:-4]
    up_w, left, right, left_t = refs[-4:]
    me = info[0]
    width = down.shape[1]
    hid = down.shape[0]
    block = width // 8
    rows = even.shape[1]
    mine = pl.ds(pl.multiple_of((me % 2) * hid, 128), hid)
    spot = lambda slot: pl.ds(pl.multiple_of((me ^ slot) * block, 16), block)
    up_w[spot(0), :] = strip0[:, mine]
    for s, te in ((2, te1), (4, te2), (6, te3)):
        up_w[spot(s), :] = te[pl.ds(0, block), mine]
        right[pl.ds(s * rows, rows), :] = te[pl.ds(block, rows), :]
    up_w[spot(1), :] = far[pl.ds(0, block), pl.ds(0, hid)]
    up_w[spot(3), :] = far[pl.ds(0, block), pl.ds(hid, hid)]
    up_w[spot(5), :] = far[pl.ds(block, block), pl.ds(0, hid)]
    up_w[spot(7), :] = far[pl.ds(block, block), pl.ds(hid, hid)]
    right[pl.ds(0, rows), :] = grad0[...]
    for k in range(4):
        right[pl.ds((2 * k + 1) * rows, rows), :] = far[pl.ds(2 * block + k * rows, rows), :]
    for slot in range(8):
        left[pl.ds(slot * rows, rows), :] = (even, odd)[slot % 2][slot // 2]
    turned = left[...].T
    for b in range(8):
        left_t[spot(b), :] = turned[b * block : (b + 1) * block]
    upper = dot_nn(left[...], up_w[...]) + up_bias[...]
    active, slope = gelu_parts(upper)
    act = active.astype(BF)
    low = (dot_nt(right[...], down[...]) * slope).astype(BF)
    bias_sums[...] = jnp.sum(low.astype(F32), axis=0, keepdims=True)
    gn2 = dot_nt(low, up_w[...]).astype(BF)
    branch = dot_nn(act, down[...]).astype(BF)
    for s in range(4):
        gn2_keep[s] = gn2[2 * s * rows : (2 * s + 1) * rows]
        gn2_send[s] = gn2[(2 * s + 1) * rows : (2 * s + 2) * rows]
        branch_keep[s] = branch[2 * s * rows : (2 * s + 1) * rows]
        branch_send[s] = branch[(2 * s + 1) * rows : (2 * s + 2) * rows]
    grad_down[...] = dot_tn(act, right[...]).astype(BF)
    grad_up = dot_nn(left_t[...], low).astype(BF)
    for b in range(4):
        up_keep[b] = grad_up[2 * b * block : (2 * b + 1) * block]
        up_send[b] = grad_up[(2 * b + 1) * block : (2 * b + 2) * block]


def attn_bwd_kernel(text_rows, info, gn2v, gn2x, t0, t1, t2, t3, grad, h1, vec, qkv, probs, weight, *refs):
    gh1, low, stacked, sums, gn2, gctx = refs[-6:]
    total, width = h1.shape
    items = total // ITEM
    text = (
        t0[0].astype(F32) + t1[...].astype(F32) + t2[...].astype(F32) + t3[...].astype(F32)
    )
    for i in range(items):
        part = pl.ds(i * TEXT_AT, TEXT_AT)
        gn2[pl.ds(i * ITEM, TEXT_AT), :] = gn2v[part, :] + gn2x[part, :].astype(F32)
        gn2[pl.ds(i * ITEM + TEXT_AT, text_rows), :] = text[i * text_rows : (i + 1) * text_rows]
        pad = ITEM - TEXT_AT - text_rows
        gn2[pl.ds(i * ITEM + TEXT_AT + text_rows, pad), :] = jnp.zeros((pad, width), F32)
    sums[...] = jnp.zeros_like(sums)

    @pl.loop(0, total // 64)
    def _(step):
        rows = pl.ds(pl.multiple_of(step * 64, 64), 64)
        normal, scale = normalize(h1[rows, :])
        above = gn2[rows, :]
        inner = above * vec[6:7, :]
        back = scale * (
            inner
            - jnp.mean(inner, axis=-1, keepdims=True)
            - normal * jnp.mean(inner * normal, axis=-1, keepdims=True)
        )
        out = grad[rows, :].astype(F32)
        hidden = out + back
        gh1[rows, :] = hidden
        low[rows, :] = hidden.astype(BF)
        sums[0:1, :] += jnp.sum(above * normal, axis=0, keepdims=True)
        sums[1:2, :] += jnp.sum(above, axis=0, keepdims=True)
        sums[2:3, :] += jnp.sum(hidden.astype(BF).astype(F32), axis=0, keepdims=True)

    gctx[...] = dot_nt(low[...], weight[...]).astype(BF)
    pairs = width // 128

    @pl.loop(0, items * pairs)
    def _(step):
        item, pair = step // pairs, step % pairs
        rows = pl.ds(pl.multiple_of(item * ITEM, ITEM), ITEM)
        lane = lambda part: pl.ds(pl.multiple_of(part * width + pair * 128, 128), 128)
        q2, k2, v2 = qkv[rows, lane(0)], qkv[rows, lane(1)], qkv[rows, lane(2)]
        g2 = gctx[rows, pl.ds(pl.multiple_of(pair * 128, 128), 128)]
        lower = lax.broadcasted_iota(jnp.int32, (ITEM, 128), 1) < HEAD_DIM
        zero = jnp.zeros_like(q2)
        split = lambda a: jnp.concatenate([jnp.where(lower, a, zero), jnp.where(lower, zero, a)], axis=0)
        both_g = split(g2)
        prob_b = probs[step]
        prob = prob_b.astype(F32)
        gprob = dot_nt(both_g, v2)
        weighted = prob * gprob
        gscore = (weighted - prob * jnp.sum(weighted, axis=-1, keepdims=True)).astype(BF)
        stacked[rows, lane(2)] = dot_tn(prob_b, both_g).astype(BF)
        stacked[rows, lane(1)] = dot_tn(gscore, split(q2)).astype(BF)
        wide = jnp.concatenate([gscore[:ITEM], gscore[ITEM:]], axis=1)
        gquery = dot_nn(wide, split(k2)).astype(BF).astype(F32) * 0.125
        stacked[rows, lane(0)] = gquery.astype(BF)

    for part in (0, 2):
        cols = stacked[:, part * width : (part + 1) * width].astype(F32)
        sums[3 + part // 2 : 4 + part // 2, :] = jnp.sum(cols, axis=0, keepdims=True)


def attn_grad_kernel(last, info, left, *refs):
    me = info[0]
    width = left.shape[1]
    block = width // 8
    keep, send, left_t, other_t, right, sem = refs[-6:]
    others, stacked = (refs[:2], refs[2]) if last else ((), refs[0])
    first = 2 * width if last else 0
    copy = pltpu.make_async_copy(stacked.at[:, pl.ds(first, right.shape[1])], right, sem.at[0])
    copy.start()
    for source, target in ((left, left_t), (others[0], other_t)) if last else ((left, left_t),):
        turned = source[...].T
        for b in range(8):
            place = pl.multiple_of((me ^ b) * block, 16)
            target[pl.ds(place, block), :] = turned[b * block : (b + 1) * block]
    for part in (1, 0) if last else (0, 1):
        cols = slice(part * width, (part + 1) * width)
        if last and part == 1:
            value = dot_nn(other_t[...], others[1][...]).astype(BF)
        else:
            if part == 0:
                copy.wait()
            value = dot_nn(left_t[...], right[:, cols]).astype(BF)
        for b in range(4):
            keep[b, :, cols] = value[2 * b * block : (2 * b + 1) * block]
            send[b, :, cols] = value[(2 * b + 1) * block : (2 * b + 2) * block]


def last_kernel(slots, info, stacked, gh1, tok, mask, vec, *refs):
    count = len(slots)
    pieces = refs[:count]
    gtok, sums, weight, sems = refs[-4:]
    copies = start_rows([(s, f, r) for (s, f), r in zip(slots, pieces)], weight, info[0], sems)
    sums[...] = jnp.zeros_like(sums)
    for copy in copies:
        copy.wait()

    @pl.loop(0, tok.shape[0] // 128)
    def _(step):
        rows = pl.ds(pl.multiple_of(step * 128, 128), 128)
        above = dot_nt(stacked[rows, :], weight[...])
        normal, scale = normalize(mixed_in(tok, mask, vec, rows))
        inner = above * vec[1:2, :]
        back = scale * (
            inner
            - jnp.mean(inner, axis=-1, keepdims=True)
            - normal * jnp.mean(inner * normal, axis=-1, keepdims=True)
        )
        hidden = gh1[rows, :] + back
        keep = mask[rows, :]
        gtok[rows, :] = hidden * (1.0 - keep)
        sums[0:1, :] += jnp.sum(hidden * keep, axis=0, keepdims=True)
        sums[1:2, :] += jnp.sum(above * normal, axis=0, keepdims=True)
        sums[2:3, :] += jnp.sum(above, axis=0, keepdims=True)


def call(kernel, outs, scratch, args, pieces=(), us=1):
    in_specs = [pl.BlockSpec(memory_space=pltpu.SMEM)]
    in_specs += [pl.BlockSpec(memory_space=pltpu.VMEM)] * (len(args) - 1)
    in_specs += [pl.BlockSpec(memory_space=pl.ANY)] * len(pieces)
    return pl.pallas_call(
        kernel,
        out_shape=[jax.ShapeDtypeStruct(s, d) for s, d in outs],
        in_specs=in_specs,
        out_specs=[pl.BlockSpec(memory_space=pltpu.VMEM)] * len(outs),
        scratch_shapes=scratch,
        compiler_params=pltpu.CompilerParams(vmem_limit_bytes=VMEM_LIMIT),
        cost_estimate=pl.CostEstimate(flops=int(us * SCALE * 1.1e9), bytes_accessed=int(us * SCALE * 1e6), transcendentals=0),
    )(*args, *pieces)


def swap(array, mask):
    return lax.ppermute(array, "fsdp", [(i, i ^ mask) for i in range(8)])


def along_rep(array, pairs):
    return lax.ppermute(array, "rep", pairs)


def add(*terms):
    out = terms[0].astype(F32)
    for term in terms[1:]:
        out = out + term.astype(F32)
    return out.astype(BF)


def planned(
    tokens,
    out_grad,
    masked,
    lengths,
    mask_vec,
    norm1_gain,
    norm1_shift,
    w_qkv,
    query_bias,
    value_bias,
    w_out,
    out_bias,
    norm2_gain,
    norm2_shift,
    vision_up,
    vision_up_bias,
    vision_down,
    vision_down_bias,
    text_up,
    text_up_bias,
    text_down,
    text_down_bias,
):
    items, row_count, width = tokens.shape
    text_rows = masked.shape[1]
    patches = row_count - text_rows
    block = width // 8
    half = block // 2
    hid = vision_down.shape[0]
    pair = 2 * hid
    hidden = 8 * hid
    total = items * ITEM
    vision_rows = items * TEXT_AT
    slot_rows = items * text_rows
    te_rows = block + slot_rows
    me = lax.axis_index("fsdp").astype(jnp.int32)
    rep = lax.axis_index("rep").astype(jnp.int32)
    core, chip, side = me % 2, me // 2, (me // 2) % 2
    sem = lambda n: pltpu.SemaphoreType.DMA((n,))
    quad = lambda r, c: ((4, r, c), BF)

    names = (
        mask_vec,
        norm1_gain,
        norm1_shift,
        query_bias,
        value_bias,
        out_bias,
        norm2_gain,
        norm2_shift,
        vision_down_bias,
        text_down_bias,
    )
    own_vec = jnp.pad(jnp.stack(names), ((0, 0), (0, 128 - block)))
    own_vec = jnp.concatenate([own_vec, vision_up_bias.reshape(-1, 128)], axis=0)
    own_vec = jnp.pad(own_vec, ((0, 16 - own_vec.shape[0]), (0, 0)))[None]
    vx, vy, vxy = swap(own_vec, 2), swap(own_vec, 4), swap(own_vec, 6)
    qx, qy = swap(w_qkv, 2), swap(w_qkv, 4)
    mask = jnp.concatenate(
        [
            jnp.zeros((items, TEXT_AT), F32),
            masked.astype(F32),
            jnp.zeros((items, ITEM - TEXT_AT - text_rows), F32),
        ],
        axis=1,
    ).reshape(total, 1)
    info = jnp.concatenate([me[None], lengths, jnp.full((1,), patches, jnp.int32)])
    tok, grad, grad_v, grad_t, grad_sums, own_out, own_down, up_mine, up_other, strip0, te1, te2, te3, t = call(
        functools.partial(prep_kernel, text_rows),
        [
            ((total, width), BF),
            ((total, width), BF),
            ((vision_rows, width), BF),
            ((slot_rows, width), BF),
            ((2, width), F32),
            ((block, width), BF),
            ((hid, width), BF),
            ((block, 2 * pair), BF),
            ((block, 2 * pair), BF),
            ((block, pair), BF),
            ((te_rows, width), BF),
            ((te_rows, width), BF),
            ((te_rows, width), BF),
            ((8, 128), F32),
        ],
        [],
        [info, tokens, out_grad, w_out, vision_down, vision_up, text_up],
        us=5,
    )
    vec_four = gate([jnp.concatenate([own_vec, vx, vy, vxy], axis=0)], [t])[0]
    vec_arrays = [vec_four, swap(vec_four, 1)]
    part1, part2 = gate([qx[:half], qy[half:]], [tok, vec_arrays[1]])

    far1, far2 = swap(part1, 4), swap(part2, 2)
    near = [swap(a, 1) for a in (w_qkv, qx, qy)]
    n1, vec, up_bias = call(
        norm_kernel,
        [((total, width), BF), ((16, width), F32), ((1, 4 * hid), F32)],
        [pltpu.VMEM((8, 16, 128), BF)],
        [info, tok, mask, *vec_arrays],
        [part1],
        us=5,
    )
    far1, far2, up_other, own_down, own_out = gate([far1, far2, up_other, own_down, own_out], [n1, *near])
    out_all = lax.all_gather(own_out, "fsdp", tiled=True)
    pairs = [[0, 2], [1, 3], [4, 6], [5, 7]]
    grad_pair = lax.all_gather(grad_v, "fsdp", axis_index_groups=pairs)
    attn = [(0, 0, w_qkv), (2, 0, qx), (4, 0, qy), (6, 0, far1), (6, half, far2)]
    attn += [(1, 0, near[0]), (3, 0, near[1]), (5, 0, near[2]), (7, 0, swap(far1, 1)), (7, half, swap(far2, 1))]
    attn_slots = tuple((p[0], p[1]) for p in attn)
    attn_arrays = [p[2] for p in attn]

    up_x, down_y = swap(up_other, 2), swap(own_down, 4)
    (qkv,) = call(
        functools.partial(qkv_kernel, attn_slots),
        [((total, 3 * width), BF)],
        [pltpu.VMEM((width, 3 * width), BF), pltpu.VMEM((1, 3 * width), F32), sem(len(attn))],
        [info, n1, vec],
        attn_arrays,
        us=8,
    )
    t = tick(t, [qkv, up_x])

    up_x, te1, te2, te3 = gate([up_x, te1, te2, te3], [t])
    up_two = jnp.stack([up_mine, up_x])
    up_y, up_c = swap(up_two, 4), swap(up_two, 1)
    te1, te3 = swap(te1, 2), swap(te3, 6)
    probs, ctx = call(
        attn_kernel,
        [((items * width // 128, 2 * ITEM, ITEM), BF), ((total, width), BF)],
        [],
        [info, qkv],
        [t],
        us=10,
    )
    t = tick(t, [ctx, up_y, up_c, te1, te3, down_y])

    up_y, te1, te2, te3, down_y = gate([up_y, te1, te2, te3, down_y], [t])
    te2 = swap(te2, 4)
    down_two = jnp.stack([own_down, down_y])
    up_yc, down_c = swap(up_y, 1), swap(down_two, 1)
    h1, n2t, *n2v = call(
        functools.partial(out_kernel, text_rows),
        [((total, width), F32), ((slot_rows, width), BF)] + [((TEXT_AT, width), BF)] * items,
        [],
        [info, tok, mask, vec, ctx, out_all],
        [t],
        us=5,
    )
    t = tick(t, [n2t, te2, up_yc, down_c, grad_pair])

    te1, te2, te3, n2t, *n2v = gate([te1, te2, te3, n2t, *n2v], [t])
    (pack,) = call(
        pack_kernel,
        [((2 * block + 4 * slot_rows, width), BF)],
        [],
        [info, strip0, te1, te2, te3, grad_t],
    )
    text_in = [swap(n2t, 2), swap(n2t, 4), swap(n2t, 6)]
    n2x = [swap(n2v[0], 2)]
    far = swap(pack, 1)
    weights = [up_two, up_y, up_c, up_yc, down_two, down_c]

    def vision(rows_in, grads, kind, after):
        return call(
            functools.partial(vision_kernel, kind == BF, items),
            [
                ((vision_rows, width), kind),
                ((vision_rows, width), kind),
                ((vision_rows, 4 * hid), BF),
                ((vision_rows, 4 * hid), BF),
            ],
            [
                pltpu.VMEM((width, 4 * hid), BF),
                pltpu.VMEM((4 * hid, width), BF),
                pltpu.VMEM((vision_rows, width), BF),
                sem(12),
            ],
            [info, grads, up_bias, *rows_in],
            [*weights, *after],
            us=9,
        )

    branch_own, gn2_own, act_own, low_own = vision(n2v, grad_v, F32, [pack])
    t = tick(t, [gn2_own, *text_in, n2x[0], far])

    far, *text_in = gate([far, *text_in], [t])
    text_four = jnp.stack([n2t, *text_in])
    text_odd = swap(text_four, 1)
    n2x += [swap(a, 2) for a in gate(n2v[1:], [t])]
    branch_keep, branch_send, gn2_keep, gn2_send, tu_keep, tu_send, td, text_bias_sum = call(
        text_kernel,
        [
            quad(slot_rows, width),
            quad(slot_rows, width),
            quad(slot_rows, width),
            quad(slot_rows, width),
            quad(block, hid),
            quad(block, hid),
            ((hid, width), BF),
            ((1, hid), F32),
        ],
        [
            pltpu.VMEM((width, hid), BF),
            pltpu.VMEM((8 * slot_rows, width), BF),
            pltpu.VMEM((8 * slot_rows, width), BF),
            pltpu.VMEM((width, 8 * slot_rows), BF),
        ],
        [
            info,
            text_down,
            text_up_bias.astype(F32).reshape(1, hid),
            strip0,
            te1,
            te2,
            te3,
            far,
            text_four,
            text_odd,
            grad_t,
        ],
        us=6,
    )
    t = tick(t, [gn2_keep, *n2x])
    tu_keep, tu_send, td = lax.psum((tu_keep, tu_send, td), "rep")

    gn2_send, *n2x = gate([gn2_send, *n2x], [t])
    gn2_sum = add(gn2_keep, swap(gn2_send, 1))
    gn2_text = [gn2_sum] + [swap(gn2_sum[s], 2 * s) for s in (1, 2, 3)]
    branch_x, gn2_x, act_x, low_x = vision(n2x, grad_pair, BF, [gn2_sum])
    t = tick(t, [gn2_x, *gn2_text[1:]])

    (gn2_x,) = gate([gn2_x], [t])
    gn2_back = swap(gn2_x, 2)
    vu_keep, vu_send, vd_keep, vd_send, vu_bias_sum = call(
        functools.partial(vision_grad_kernel, items),
        [
            quad(block, 4 * hid),
            quad(block, 4 * hid),
            ((2, hid, width), BF),
            ((2, hid, width), BF),
            ((1, 4 * hid), F32),
        ],
        [
            pltpu.VMEM((width, 2 * vision_rows), BF),
            pltpu.VMEM((4 * hid, 2 * vision_rows), BF),
            pltpu.VMEM((2 * vision_rows, width), BF),
            pltpu.VMEM((2 * vision_rows, 4 * hid), BF),
            pltpu.VMEM((width, vision_rows), BF),
            pltpu.VMEM((width, vision_rows), BF),
        ],
        [info, *n2v, *n2x, grad_pair, act_own, act_x, low_own, low_x],
        [t],
        us=12,
    )
    t = tick(t, [vu_bias_sum, gn2_back])

    vu_send, vd_send, branch_x, branch_send, gn2_back = gate([vu_send, vd_send, branch_x, branch_send, gn2_back], [t])
    vu_got, vd_got = swap(vu_send, 1), swap(vd_send, 1)
    vd_near, vd_far = add(vd_keep[0], vd_got[0]), add(vd_keep[1], vd_got[1])
    vu_far = [add(vu_keep[k], vu_got[k]) for k in (2, 3)]
    vd_y, vu_y1 = swap(vd_far, 4), swap(vu_far[1], 4)
    branch_back = swap(branch_x, 2)
    branch_got = swap(branch_send, 1)
    gh1, low_attn, stacked, sums_two = call(
        functools.partial(attn_bwd_kernel, text_rows),
        [((total, width), F32), ((total, width), BF), ((total, 3 * width), BF), ((8, width), F32)],
        [pltpu.VMEM((total, width), F32), pltpu.VMEM((total, width), BF)],
        [info, gn2_own, gn2_back, *gn2_text, grad, h1, vec, qkv, probs, out_all],
        [vd_far, *vu_far],
        us=18,
    )
    t = tick(t, [stacked, vd_y, vu_y1, branch_back, branch_got])

    vd_y, vu_y1, vu_far0, branch_got = gate([vd_y, vu_y1, vu_far[0], branch_got], [t])
    vd_sum = add(vd_near, vd_y)
    vu_x = swap(add(vu_keep[1], vu_got[1], vu_y1), 2)
    vu_y0 = swap(vu_far0, 4)

    def attn_grads(last, after):
        return call(
            functools.partial(attn_grad_kernel, last),
            [quad(block, 2 * width), quad(block, 2 * width)],
            [
                pltpu.VMEM((width, total), BF),
                pltpu.VMEM((width, total), BF),
                pltpu.VMEM((total, (1 if last else 2) * width), BF),
                sem(1),
            ],
            [info, n1, ctx, low_attn] if last else [info, n1],
            [stacked, *after],
            us=5,
        )

    a_keep, a_send = attn_grads(False, [t])
    t = tick(t, [a_keep, vu_x, vu_y0])
    a_send, vu_x, vu_y0 = gate([a_send, vu_x, vu_y0], [t])
    a_got = swap(a_send, 1)
    branch_sum = add(branch_keep, branch_got)
    vu_both = jnp.stack([add(vu_keep[0], vu_got[0], vu_y0), vu_x])
    vu, vd = lax.psum((vu_both, vd_sum), "rep", axis_index_groups=[[1, 0, 2, 3]])
    b_keep, b_send = attn_grads(True, [t])
    t = tick(t, [b_keep, a_got])
    a_got, b_send, branch_sum = gate([a_got, b_send, branch_sum], [t])
    b_got = swap(b_send, 1)

    def begin(keep, got, one):
        i = one // 2
        return add(jnp.stack([keep[i], keep[3]]), jnp.stack([got[i], got[3]]))

    a_first, b_first = begin(a_keep, a_got, 2), begin(b_keep, b_got, 4)
    a_there, b_there = swap(a_first, 2), swap(b_first, 4)
    branch_t = [branch_sum] + [swap(branch_sum[s], 2 * s) for s in (1, 2, 3)]
    gtok, sums_one = call(
        functools.partial(last_kernel, attn_slots),
        [((total, width), F32), ((8, width), F32)],
        [pltpu.VMEM((width, 3 * width), BF), sem(len(attn))],
        [info, stacked, gh1, tok, mask, vec],
        attn_arrays + [a_first, b_first, vu_both, vd_sum],
        us=12,
    )
    t = tick(t, [sums_one, a_there, b_there, *branch_t[1:]])

    a_there, b_there = gate([a_there, b_there], [t])
    a_next, b_next = add(a_keep[2], a_got[2], a_there[1]), add(b_keep[1], b_got[1], b_there[1])
    a_beyond, b_beyond = swap(a_next, 4), swap(b_next, 2)
    (sums_one,) = gate([sums_one], [tick(t, [a_next, b_next])])
    vu_sum = vu_bias_sum.reshape(2, 1, pair)
    vu_sum = jnp.where(
        side == 0,
        jnp.concatenate([vu_sum, jnp.zeros_like(vu_sum)], axis=1),
        jnp.concatenate([jnp.zeros_like(vu_sum), vu_sum], axis=1),
    )
    count, rows = len(names), hid // block
    vec_rows = count + 2 * rows
    vu_sum = vu_sum.reshape(8, rows, block).transpose(1, 0, 2).reshape(-1, width)
    flat = jnp.concatenate(
        [sums_one[0:3], sums_two[3:5], sums_two[2:3], sums_two[0:2], grad_sums, vu_sum], axis=0
    )
    for m in (1, 2, 4):
        flat = flat + swap(flat, m)
    own_sums = lax.dynamic_slice_in_dim(flat, me * block, block, axis=1)
    own_sums = jnp.concatenate([own_sums, text_bias_sum.reshape(-1, block)], axis=0)
    ga = add(a_keep[0], a_got[0], a_there[0], a_beyond)
    gb = add(b_keep[0], b_got[0], b_there[0], b_beyond)

    inner = (rep == 1) | (rep == 2)

    def rep_sum(array):
        part = add(array, along_rep(array, [(0, 1), (3, 2)]))
        whole = add(part, along_rep(part, [(1, 2), (2, 1)]))
        return jnp.where(inner, whole, along_rep(whole, [(1, 0), (2, 3)]))

    plane_sums = [ga, gb]
    own_sums = own_sums.reshape(-1)
    own_sums = jnp.pad(own_sums, (0, 8 * 2 * width - own_sums.shape[0])).reshape(8, 2 * width)
    ga, gb = rep_sum(jnp.concatenate([ga, own_sums.astype(BF)], axis=0)), rep_sum(gb)
    last_sums = [ga, gb]
    tu_keep, tu_send, td = gate([tu_keep, tu_send, td], plane_sums)
    tu_got = swap(tu_send, 1)
    tu_wide = jnp.where(
        core == 0,
        jnp.concatenate([tu_keep, tu_got], axis=-1),
        jnp.concatenate([tu_got, tu_keep], axis=-1),
    )
    tu_all = [tu_wide[0]] + [swap(tu_wide[s], 2 * s) for s in (1, 2, 3)]
    tu_x = [jnp.where(side == 0, tu_all[k], tu_all[k ^ 1]) for k in range(4)]
    tu_y = [jnp.where(me // 4 == 0, tu_x[k], tu_x[k ^ 2]) for k in range(4)]
    grad_text_up = jnp.concatenate(tu_y, axis=1).astype(F32)
    grad_text_down = td.astype(F32)

    ga = ga.astype(F32)
    mine = ga[block:].reshape(-1)[: vec_rows * block].reshape(vec_rows, block)
    ga = ga[:block]
    vec_grad = [mine[i] for i in range(count)]
    vu_bias_grad = mine[count : count + rows].reshape(-1)
    tu_bias_grad = mine[count + rows : count + 2 * rows].reshape(-1)

    vu, vd = gate([vu, vd], last_sums)
    gb = gb.astype(F32)
    grad_w_qkv = jnp.concatenate([ga, gb[:, :width]], axis=1)
    grad_w_out = gb[:, width:]
    vu_s = [jnp.where(side == 0, vu[k], vu[1 - k]) for k in range(2)]
    grad_vision_up = jnp.concatenate(
        [vu_s[0][:, :pair], vu_s[1][:, :pair], vu_s[0][:, pair:], vu_s[1][:, pair:]], axis=1
    ).astype(F32)
    grad_vision_down = vd.astype(F32)
    h1 = h1.reshape(items, ITEM, width)
    branch_v = (branch_own + branch_back.astype(F32)).reshape(items, TEXT_AT, width)[:, :patches]
    mixed_v = h1[:, :patches] + branch_v + vec[8][None, None]
    branch_t = branch_t[0][0].astype(F32) + sum(b.astype(F32) for b in branch_t[1:])
    branch_t = branch_t.reshape(items, text_rows, width)
    mixed_t = h1[:, TEXT_AT : TEXT_AT + text_rows] + branch_t + vec[9][None, None]
    mixed = jnp.concatenate([mixed_v.astype(BF), mixed_t.astype(BF)], axis=1)
    gtok = gtok.reshape(items, ITEM, width)
    grad_tokens = jnp.concatenate(
        [gtok[:, :patches], gtok[:, TEXT_AT : TEXT_AT + text_rows]], axis=1
    )
    return (
        mixed,
        grad_tokens,
        vec_grad[0],
        vec_grad[1],
        vec_grad[2],
        grad_w_qkv,
        vec_grad[3],
        vec_grad[4],
        grad_w_out,
        vec_grad[5],
        vec_grad[6],
        vec_grad[7],
        grad_vision_up,
        vu_bias_grad,
        grad_vision_down,
        vec_grad[8],
        grad_text_up,
        tu_bias_grad,
        grad_text_down,
        vec_grad[9],
    )


def layer_norm(hidden, gain, shift):
    center = hidden - jnp.mean(hidden, axis=-1, keepdims=True)
    spread = jnp.mean(center * center, axis=-1, keepdims=True)
    return center * lax.rsqrt(spread + epsilon) * gain + shift


def exact_gelu(values):
    return jax.nn.gelu(values, approximate=False)


def expert_forward(rows_in, up_matrix, up_shift, down_matrix, down_shift):
    upper = jnp.dot(rows_in, up_matrix, preferred_element_type=jnp.float32) + up_shift.astype(
        jnp.float32
    )
    active, gelu_pull = jax.vjp(exact_gelu, upper)
    active_b = active.astype(jnp.bfloat16)
    result = jnp.dot(active_b, down_matrix, preferred_element_type=jnp.float32) + down_shift.astype(
        jnp.float32
    )
    return (result, active_b, gelu_pull)


def expert_backward(rows_in, active_b, gelu_pull, up_matrix, down_matrix, grad_b):
    grad_down = jnp.einsum("rf,rd->fd", active_b, grad_b, preferred_element_type=jnp.float32)
    grad_down_shift = jnp.sum(grad_b.astype(jnp.float32), axis=0)
    grad_active = jnp.einsum("rd,fd->rf", grad_b, down_matrix, preferred_element_type=jnp.float32)
    (grad_upper,) = gelu_pull(grad_active)
    upper_b = grad_upper.astype(jnp.bfloat16)
    grad_up = jnp.einsum("rd,rf->df", rows_in, upper_b, preferred_element_type=jnp.float32)
    grad_up_shift = jnp.sum(upper_b.astype(jnp.float32), axis=0)
    grad_rows = jnp.einsum("rf,df->rd", upper_b, up_matrix, preferred_element_type=jnp.float32)
    return (grad_up, grad_up_shift, grad_down, grad_down_shift, grad_rows)


def general(
    tokens,
    out_grad,
    masked,
    lengths,
    mask_vec,
    norm1_gain,
    norm1_shift,
    w_qkv,
    query_bias,
    value_bias,
    w_out,
    out_bias,
    norm2_gain,
    norm2_shift,
    vision_up,
    vision_up_bias,
    vision_down,
    vision_down_bias,
    text_up,
    text_up_bias,
    text_down,
    text_down_bias,
):
    item_count, row_count, model_width = tokens.shape
    slot_count = masked.shape[1]
    patches = row_count - slot_count
    head_count = model_width // HEAD_DIM
    split_shape = (item_count, row_count, head_count, HEAD_DIM)

    def fetch_attention():
        return (
            lax.all_gather(mask_vec, "fsdp", axis=0, tiled=True),
            lax.all_gather(norm1_gain, "fsdp", axis=0, tiled=True),
            lax.all_gather(norm1_shift, "fsdp", axis=0, tiled=True),
            lax.all_gather(w_qkv, "fsdp", axis=0, tiled=True),
            lax.all_gather(query_bias, "fsdp", axis=0, tiled=True),
            lax.all_gather(value_bias, "fsdp", axis=0, tiled=True),
            lax.all_gather(w_out, "fsdp", axis=0, tiled=True),
            lax.all_gather(out_bias, "fsdp", axis=0, tiled=True),
        )

    def fetch_feedforward():
        return (
            lax.all_gather(norm2_gain, "fsdp", axis=0, tiled=True),
            lax.all_gather(norm2_shift, "fsdp", axis=0, tiled=True),
            lax.all_gather(vision_up, "fsdp", axis=0, tiled=True),
            lax.all_gather(vision_up_bias, "fsdp", axis=0, tiled=True),
            lax.all_gather(vision_down, "fsdp", axis=0, tiled=True),
            lax.all_gather(vision_down_bias, "fsdp", axis=0, tiled=True),
            lax.all_gather(text_up, "fsdp", axis=0, tiled=True),
            lax.all_gather(text_up_bias, "fsdp", axis=0, tiled=True),
            lax.all_gather(text_down, "fsdp", axis=0, tiled=True),
            lax.all_gather(text_down_bias, "fsdp", axis=0, tiled=True),
        )

    attn_full = fetch_attention()
    full_mask, gain_one, shift_one, qkv_matrix, query_shift, value_shift, out_matrix, out_shift = (
        attn_full
    )
    mask_rows = jnp.concatenate(
        [jnp.zeros((item_count, patches), jnp.float32), masked.astype(jnp.float32)], axis=1
    )[:, :, None]
    hidden0 = mask_rows * full_mask.astype(jnp.float32) + (1.0 - mask_rows) * tokens.astype(
        jnp.float32
    )
    normed1, first_pull = jax.vjp(
        layer_norm, hidden0, gain_one.astype(jnp.float32), shift_one.astype(jnp.float32)
    )
    first_in = normed1.astype(jnp.bfloat16).reshape(item_count * row_count, model_width)
    projected = jnp.dot(first_in, qkv_matrix, preferred_element_type=jnp.float32)
    query_b = (
        ((projected[:, :model_width] + query_shift.astype(jnp.float32)) * 0.125)
        .astype(jnp.bfloat16)
        .reshape(split_shape)
    )
    key_b = projected[:, model_width : 2 * model_width].astype(jnp.bfloat16).reshape(split_shape)
    value_b = (
        (projected[:, 2 * model_width :] + value_shift.astype(jnp.float32))
        .astype(jnp.bfloat16)
        .reshape(split_shape)
    )
    key_index = jnp.arange(row_count, dtype=jnp.int32)
    valid_keys = (key_index[None, :] < patches + lengths[:, None])[:, None, None, :]

    def scores_of():
        raw_scores = jnp.einsum(
            "iqhd,ikhd->ihqk", query_b, key_b, preferred_element_type=jnp.float32
        )
        return jnp.where(valid_keys, raw_scores, -1000000000.0)

    scores = scores_of()
    top_score = jnp.max(scores, axis=-1, keepdims=True)
    expo = jnp.exp(scores - top_score)
    totals = jnp.sum(expo, axis=-1, keepdims=True)
    probs = expo / totals
    log_total = top_score + jnp.log(totals)
    context = jnp.einsum(
        "ihqk,ikhd->iqhd", probs.astype(jnp.bfloat16), value_b, preferred_element_type=jnp.float32
    )
    context_b = context.reshape(item_count * row_count, model_width).astype(jnp.bfloat16)
    attended = jnp.dot(
        context_b, out_matrix, preferred_element_type=jnp.float32
    ) + out_shift.astype(jnp.float32)
    hidden1 = hidden0 + attended.reshape(item_count, row_count, model_width)
    ffn_full = fetch_feedforward()
    (
        gain_two,
        shift_two,
        vision_upm,
        vision_upb,
        vision_downm,
        vision_downb,
        text_upm,
        text_upb,
        text_downm,
        text_downb,
    ) = ffn_full
    normed2, second_pull = jax.vjp(
        layer_norm, hidden1, gain_two.astype(jnp.float32), shift_two.astype(jnp.float32)
    )
    second_in = normed2.astype(jnp.bfloat16)
    patch_in = second_in[:, :patches].reshape(-1, model_width)
    text_in = second_in[:, patches:].reshape(-1, model_width)
    vision_out, vision_act, vision_pull = expert_forward(
        patch_in, vision_upm, vision_upb, vision_downm, vision_downb
    )
    text_out, text_act, text_pull = expert_forward(
        text_in, text_upm, text_upb, text_downm, text_downb
    )
    mixed = hidden1 + jnp.concatenate(
        [
            vision_out.reshape(item_count, patches, model_width),
            text_out.reshape(item_count, slot_count, model_width),
        ],
        axis=1,
    )
    cotangent = out_grad.astype(jnp.float32)
    branch_b = cotangent.astype(jnp.bfloat16)
    ffn_back = fetch_feedforward()
    vision_grads = expert_backward(
        patch_in,
        vision_act,
        vision_pull,
        ffn_back[2],
        ffn_back[4],
        branch_b[:, :patches].reshape(-1, model_width),
    )
    text_grads = expert_backward(
        text_in,
        text_act,
        text_pull,
        ffn_back[6],
        ffn_back[8],
        branch_b[:, patches:].reshape(-1, model_width),
    )
    grad_normed2 = jnp.concatenate(
        [
            vision_grads[4].reshape(item_count, patches, model_width),
            text_grads[4].reshape(item_count, slot_count, model_width),
        ],
        axis=1,
    )
    grad_hidden1_norm, grad_gain_two, grad_shift_two = second_pull(grad_normed2)
    grad_hidden1 = cotangent + grad_hidden1_norm
    attn_back = fetch_attention()
    grad_attn_b = grad_hidden1.reshape(-1, model_width).astype(jnp.bfloat16)
    grad_out_matrix = jnp.einsum(
        "rd,re->de", context_b, grad_attn_b, preferred_element_type=jnp.float32
    )
    grad_out_shift = jnp.sum(grad_attn_b.astype(jnp.float32), axis=0)
    grad_context = jnp.einsum(
        "re,de->rd", grad_attn_b, attn_back[6], preferred_element_type=jnp.float32
    )
    grad_context_b = grad_context.astype(jnp.bfloat16).reshape(split_shape)
    again_probs = jnp.exp(scores_of() - log_total)
    grad_probs = jnp.einsum(
        "iqhd,ikhd->ihqk", grad_context_b, value_b, preferred_element_type=jnp.float32
    )
    grad_value = jnp.einsum(
        "ihqk,iqhd->ikhd",
        again_probs.astype(jnp.bfloat16),
        grad_context_b,
        preferred_element_type=jnp.float32,
    )
    row_inner = jnp.sum(again_probs * grad_probs, axis=-1, keepdims=True)
    grad_scores_b = (again_probs * (grad_probs - row_inner)).astype(jnp.bfloat16)
    grad_query = jnp.einsum(
        "ihqk,ikhd->iqhd", grad_scores_b, key_b, preferred_element_type=jnp.float32
    )
    grad_key = jnp.einsum(
        "ihqk,iqhd->ikhd", grad_scores_b, query_b, preferred_element_type=jnp.float32
    )
    grad_query_b = grad_query.astype(jnp.bfloat16) * jnp.bfloat16(0.125)
    stacked = jnp.concatenate(
        [
            grad_query_b.reshape(-1, model_width),
            grad_key.astype(jnp.bfloat16).reshape(-1, model_width),
            grad_value.astype(jnp.bfloat16).reshape(-1, model_width),
        ],
        axis=1,
    )
    grad_qkv = jnp.einsum("rd,re->de", first_in, stacked, preferred_element_type=jnp.float32)
    grad_query_shift = jnp.sum(stacked[:, :model_width].astype(jnp.float32), axis=0)
    grad_value_shift = jnp.sum(stacked[:, 2 * model_width :].astype(jnp.float32), axis=0)
    grad_normed1 = jnp.einsum(
        "re,de->rd", stacked, attn_back[3], preferred_element_type=jnp.float32
    )
    grad_hidden0_norm, grad_gain_one, grad_shift_one = first_pull(
        grad_normed1.reshape(item_count, row_count, model_width)
    )
    grad_hidden0 = grad_hidden1 + grad_hidden0_norm
    grad_tokens = grad_hidden0 * (1.0 - mask_rows)
    grad_mask = jnp.sum(grad_hidden0 * mask_rows, axis=(0, 1))
    ffn_share = (
        lax.psum_scatter(grad_gain_two, "fsdp", scatter_dimension=0, tiled=True),
        lax.psum_scatter(grad_shift_two, "fsdp", scatter_dimension=0, tiled=True),
        lax.psum_scatter(vision_grads[0], "fsdp", scatter_dimension=0, tiled=True),
        lax.psum_scatter(vision_grads[1], "fsdp", scatter_dimension=0, tiled=True),
        lax.psum_scatter(vision_grads[2], "fsdp", scatter_dimension=0, tiled=True),
        lax.psum_scatter(vision_grads[3], "fsdp", scatter_dimension=0, tiled=True),
        lax.psum_scatter(text_grads[0], "fsdp", scatter_dimension=0, tiled=True),
        lax.psum_scatter(text_grads[1], "fsdp", scatter_dimension=0, tiled=True),
        lax.psum_scatter(text_grads[2], "fsdp", scatter_dimension=0, tiled=True),
        lax.psum_scatter(text_grads[3], "fsdp", scatter_dimension=0, tiled=True),
    )
    attn_share = (
        lax.psum_scatter(grad_mask, "fsdp", scatter_dimension=0, tiled=True),
        lax.psum_scatter(grad_gain_one, "fsdp", scatter_dimension=0, tiled=True),
        lax.psum_scatter(grad_shift_one, "fsdp", scatter_dimension=0, tiled=True),
        lax.psum_scatter(grad_qkv, "fsdp", scatter_dimension=0, tiled=True),
        lax.psum_scatter(grad_query_shift, "fsdp", scatter_dimension=0, tiled=True),
        lax.psum_scatter(grad_value_shift, "fsdp", scatter_dimension=0, tiled=True),
        lax.psum_scatter(grad_out_matrix, "fsdp", scatter_dimension=0, tiled=True),
        lax.psum_scatter(grad_out_shift, "fsdp", scatter_dimension=0, tiled=True),
    )
    quarter = (
        lax.psum_scatter(
            attn_share[0].astype(jnp.bfloat16), "rep", scatter_dimension=0, tiled=True
        ).astype(jnp.float32),
        lax.psum_scatter(
            attn_share[1].astype(jnp.bfloat16), "rep", scatter_dimension=0, tiled=True
        ).astype(jnp.float32),
        lax.psum_scatter(
            attn_share[2].astype(jnp.bfloat16), "rep", scatter_dimension=0, tiled=True
        ).astype(jnp.float32),
        lax.psum_scatter(
            attn_share[3].astype(jnp.bfloat16), "rep", scatter_dimension=0, tiled=True
        ).astype(jnp.float32),
        lax.psum_scatter(
            attn_share[4].astype(jnp.bfloat16), "rep", scatter_dimension=0, tiled=True
        ).astype(jnp.float32),
        lax.psum_scatter(
            attn_share[5].astype(jnp.bfloat16), "rep", scatter_dimension=0, tiled=True
        ).astype(jnp.float32),
        lax.psum_scatter(
            attn_share[6].astype(jnp.bfloat16), "rep", scatter_dimension=0, tiled=True
        ).astype(jnp.float32),
        lax.psum_scatter(
            attn_share[7].astype(jnp.bfloat16), "rep", scatter_dimension=0, tiled=True
        ).astype(jnp.float32),
        lax.psum_scatter(
            ffn_share[0].astype(jnp.bfloat16), "rep", scatter_dimension=0, tiled=True
        ).astype(jnp.float32),
        lax.psum_scatter(
            ffn_share[1].astype(jnp.bfloat16), "rep", scatter_dimension=0, tiled=True
        ).astype(jnp.float32),
        lax.psum_scatter(
            ffn_share[2].astype(jnp.bfloat16), "rep", scatter_dimension=0, tiled=True
        ).astype(jnp.float32),
        lax.psum_scatter(
            ffn_share[3].astype(jnp.bfloat16), "rep", scatter_dimension=0, tiled=True
        ).astype(jnp.float32),
        lax.psum_scatter(
            ffn_share[4].astype(jnp.bfloat16), "rep", scatter_dimension=0, tiled=True
        ).astype(jnp.float32),
        lax.psum_scatter(
            ffn_share[5].astype(jnp.bfloat16), "rep", scatter_dimension=0, tiled=True
        ).astype(jnp.float32),
        lax.psum_scatter(
            ffn_share[6].astype(jnp.bfloat16), "rep", scatter_dimension=0, tiled=True
        ).astype(jnp.float32),
        lax.psum_scatter(
            ffn_share[7].astype(jnp.bfloat16), "rep", scatter_dimension=0, tiled=True
        ).astype(jnp.float32),
        lax.psum_scatter(
            ffn_share[8].astype(jnp.bfloat16), "rep", scatter_dimension=0, tiled=True
        ).astype(jnp.float32),
        lax.psum_scatter(
            ffn_share[9].astype(jnp.bfloat16), "rep", scatter_dimension=0, tiled=True
        ).astype(jnp.float32),
    )
    summed = (
        lax.all_gather(quarter[0].astype(jnp.bfloat16), "rep", axis=0, tiled=True).astype(
            jnp.float32
        ),
        lax.all_gather(quarter[1].astype(jnp.bfloat16), "rep", axis=0, tiled=True).astype(
            jnp.float32
        ),
        lax.all_gather(quarter[2].astype(jnp.bfloat16), "rep", axis=0, tiled=True).astype(
            jnp.float32
        ),
        lax.all_gather(quarter[3].astype(jnp.bfloat16), "rep", axis=0, tiled=True).astype(
            jnp.float32
        ),
        lax.all_gather(quarter[4].astype(jnp.bfloat16), "rep", axis=0, tiled=True).astype(
            jnp.float32
        ),
        lax.all_gather(quarter[5].astype(jnp.bfloat16), "rep", axis=0, tiled=True).astype(
            jnp.float32
        ),
        lax.all_gather(quarter[6].astype(jnp.bfloat16), "rep", axis=0, tiled=True).astype(
            jnp.float32
        ),
        lax.all_gather(quarter[7].astype(jnp.bfloat16), "rep", axis=0, tiled=True).astype(
            jnp.float32
        ),
        lax.all_gather(quarter[8].astype(jnp.bfloat16), "rep", axis=0, tiled=True).astype(
            jnp.float32
        ),
        lax.all_gather(quarter[9].astype(jnp.bfloat16), "rep", axis=0, tiled=True).astype(
            jnp.float32
        ),
        lax.all_gather(quarter[10].astype(jnp.bfloat16), "rep", axis=0, tiled=True).astype(
            jnp.float32
        ),
        lax.all_gather(quarter[11].astype(jnp.bfloat16), "rep", axis=0, tiled=True).astype(
            jnp.float32
        ),
        lax.all_gather(quarter[12].astype(jnp.bfloat16), "rep", axis=0, tiled=True).astype(
            jnp.float32
        ),
        lax.all_gather(quarter[13].astype(jnp.bfloat16), "rep", axis=0, tiled=True).astype(
            jnp.float32
        ),
        lax.all_gather(quarter[14].astype(jnp.bfloat16), "rep", axis=0, tiled=True).astype(
            jnp.float32
        ),
        lax.all_gather(quarter[15].astype(jnp.bfloat16), "rep", axis=0, tiled=True).astype(
            jnp.float32
        ),
        lax.all_gather(quarter[16].astype(jnp.bfloat16), "rep", axis=0, tiled=True).astype(
            jnp.float32
        ),
        lax.all_gather(quarter[17].astype(jnp.bfloat16), "rep", axis=0, tiled=True).astype(
            jnp.float32
        ),
    )
    return (
        mixed.astype(jnp.bfloat16),
        grad_tokens,
        summed[0],
        summed[1],
        summed[2],
        summed[3],
        summed[4],
        summed[5],
        summed[6],
        summed[7],
        summed[8],
        summed[9],
        summed[10],
        summed[11],
        summed[12],
        summed[13],
        summed[14],
        summed[15],
        summed[16],
        summed[17],
    )


def solution(mesh):
    if mesh.shape["fsdp"] == 8 and mesh.shape["rep"] == 4:
        body = planned
    else:
        body = general
    return jax.shard_map(
        body,
        mesh=mesh,
        in_specs=(
            P(("fsdp", "rep"), None, None),
            P(("fsdp", "rep"), None, None),
            P(("fsdp", "rep"), None),
            P(("fsdp", "rep")),
            P("fsdp"),
            P("fsdp"),
            P("fsdp"),
            P("fsdp", None),
            P("fsdp"),
            P("fsdp"),
            P("fsdp", None),
            P("fsdp"),
            P("fsdp"),
            P("fsdp"),
            P("fsdp", None),
            P("fsdp"),
            P("fsdp", None),
            P("fsdp"),
            P("fsdp", None),
            P("fsdp"),
            P("fsdp", None),
            P("fsdp"),
        ),
        out_specs=(
            P(("fsdp", "rep"), None, None),
            P(("fsdp", "rep"), None, None),
            P("fsdp"),
            P("fsdp"),
            P("fsdp"),
            P("fsdp", None),
            P("fsdp"),
            P("fsdp"),
            P("fsdp", None),
            P("fsdp"),
            P("fsdp"),
            P("fsdp"),
            P("fsdp", None),
            P("fsdp"),
            P("fsdp", None),
            P("fsdp"),
            P("fsdp", None),
            P("fsdp"),
            P("fsdp", None),
            P("fsdp"),
        ),
        check_vma=False,
    )
```

```python
import functools
import math

import jax
import jax.numpy as jnp
from jax import lax
from jax.experimental import pallas as pl
from jax.experimental.pallas import tpu as pltpu
from jax.sharding import PartitionSpec as P

HEAD_DIM = 64
BF = jnp.bfloat16
F32 = jnp.float32
epsilon = 1e-06
VMEM_LIMIT = 58 * 1024 * 1024

ITEM = 256
SCALE = 0.3
TEXT_AT = 208


def cdiv(a, b):
    return -(-a // b)


def dot_nn(a, b):
    return lax.dot_general(a, b, (((1,), (0,)), ((), ())), preferred_element_type=F32)


def dot_nt(a, b):
    return lax.dot_general(a, b, (((1,), (1,)), ((), ())), preferred_element_type=F32)


def dot_tn(a, b):
    return lax.dot_general(a, b, (((0,), (0,)), ((), ())), preferred_element_type=F32)


def gelu_parts(upper):
    half = 0.5 * (1.0 + lax.erf(upper * math.sqrt(0.5)))
    slope = half + upper * (jnp.exp(-0.5 * upper * upper) * (1.0 / math.sqrt(2.0 * math.pi)))
    return upper * half, slope


def normalize(hidden):
    center = hidden - jnp.mean(hidden, axis=-1, keepdims=True)
    spread = jnp.mean(center * center, axis=-1, keepdims=True)
    scale = lax.rsqrt(spread + epsilon)
    return center * scale, scale


def start_rows(pieces, target, me, sems):
    block = target.shape[0] // 8
    copies = []
    for index, (slot, first, ref) in enumerate(pieces):
        row = pl.multiple_of((me ^ slot) * block + first, 16)
        copy = pltpu.make_async_copy(ref, target.at[pl.ds(row, ref.shape[0])], sems.at[index])
        copy.start()
        copies.append(copy)
    return copies


def mixed_in(tok, mask, vec, rows):
    keep = mask[rows, :]
    return keep * vec[0:1, :] + (1.0 - keep) * tok[rows, :].astype(F32)


def gate_kernel(count, *refs):
    del count, refs


def gate(arrays, after):
    count = len(arrays)
    return pl.pallas_call(
        functools.partial(gate_kernel, count),
        out_shape=[jax.ShapeDtypeStruct(a.shape, a.dtype) for a in arrays],
        in_specs=[pl.BlockSpec(memory_space=pl.ANY)] * (count + len(after)),
        out_specs=[pl.BlockSpec(memory_space=pl.ANY)] * count,
        input_output_aliases={i: i for i in range(count)},
        cost_estimate=pl.CostEstimate(flops=1000, bytes_accessed=1000, transcendentals=0),
    )(*arrays, *after)


def tick(token, after):
    return gate([token], after)[0]


def prep_kernel(text_rows, info, tokens, out_grad, w_out, down, up, text_up, *outs):
    tok, grad, grad_v, grad_t, sums, out_copy, down_copy, up_mine, up_other, strip0, te1, te2, te3, token = outs
    token[...] = jnp.zeros(token.shape, F32)
    items, row_count, width = tokens.shape
    patches = row_count - text_rows
    tail = ITEM - TEXT_AT - text_rows
    zeros = lambda n: jnp.zeros((n, width), F32)
    totals = [zeros(1), zeros(1)]
    texts = []
    for i in range(items):
        for source, target in ((tokens, tok), (out_grad, grad)):
            whole = source[i].astype(F32)
            patch, text = whole[:patches], whole[patches:]
            full = jnp.concatenate([patch, zeros(TEXT_AT - patches), text, zeros(tail)], axis=0)
            target[pl.ds(i * ITEM, ITEM), :] = full.astype(BF)
            if target is grad:
                grad_v[pl.ds(i * TEXT_AT, TEXT_AT), :] = full[:TEXT_AT].astype(BF)
                texts.append(text)
                totals[0] = totals[0] + jnp.sum(patch, axis=0, keepdims=True)
                totals[1] = totals[1] + jnp.sum(text, axis=0, keepdims=True)
    slots = jnp.concatenate(texts, axis=0).astype(BF)
    grad_t[...] = slots
    sums[0:1, :] = totals[0]
    sums[1:2, :] = totals[1]
    out_copy[...] = w_out[...]
    down_copy[...] = down[...]
    chip = info[0] // 2
    side = chip % 2
    block = up.shape[0]
    pair = 2 * down.shape[0]
    strip = lambda ref, c: ref[:, pl.ds(pl.multiple_of(c * pair, 128), pair)]
    for k in range(2):
        up_mine[:, k * pair : (k + 1) * pair] = strip(up, side + 2 * k)
        up_other[:, k * pair : (k + 1) * pair] = strip(up, 1 - side + 2 * k)
    strip0[...] = strip(text_up, chip)
    for k, target in ((1, te1), (2, te2), (3, te3)):
        target[pl.ds(0, block), :] = strip(text_up, chip ^ k)
        target[pl.ds(block, slots.shape[0]), :] = slots


def norm_kernel(info, tok, mask, even, odd, *refs):
    n1, vec, up_bias, shards = refs[-4:]
    me = info[0]
    total, width = tok.shape
    block = width // 8
    for slot in range(8):
        shards[me ^ slot] = (even, odd)[slot % 2][slot // 2]
    wide = jnp.concatenate([shards[b] for b in range(8)], axis=1)
    lane = lax.broadcasted_iota(jnp.int32, (1024, width), 0)
    to = lax.broadcasted_iota(jnp.int32, (1024, width), 1)
    spread = ((lane // 128) * block + lane % 128 == to) & (lane % 128 < block)
    vec[...] = dot_nn(wide, jnp.where(spread, 1.0, 0.0).astype(BF))
    hid = up_bias.shape[1] // 4
    for q in range(4):
        b = (q // 2) * 4 + q % 2 + ((me // 2) % 2) * 2
        for r in range(hid // 128):
            at = q * hid + r * 128
            up_bias[0:1, at : at + 128] = shards[b, 10 + r : 11 + r, :].astype(F32)

    @pl.loop(0, total // 64)
    def _(step):
        rows = pl.ds(pl.multiple_of(step * 64, 64), 64)
        normal, _unused = normalize(mixed_in(tok, mask, vec, rows))
        n1[rows, :] = (normal * vec[1:2, :] + vec[2:3, :]).astype(BF)


def qkv_kernel(slots, info, n1, vec, *refs):
    count = len(slots)
    pieces = refs[:count]
    qkv, weight, bias, sems = refs[-4:]
    width = n1.shape[1]
    copies = start_rows([(s, f, r) for (s, f), r in zip(slots, pieces)], weight, info[0], sems)
    bias[0:1, 0:width] = vec[3:4, :]
    bias[0:1, width : 2 * width] = jnp.zeros((1, width), F32)
    bias[0:1, 2 * width : 3 * width] = vec[4:5, :]
    for copy in copies:
        copy.wait()

    @pl.loop(0, 3 * width // 256)
    def _(step):
        cols = pl.ds(pl.multiple_of(step * 256, 256), 256)
        factor = jnp.where(step < width // 256, 0.125, 1.0).astype(F32)
        out = dot_nn(n1[...], weight[:, cols])
        qkv[:, cols] = ((out + bias[0:1, cols]) * factor).astype(BF)


def attn_kernel(info, qkv, *refs):
    probs, ctx = refs[-2:]
    total, width = ctx.shape
    items = total // ITEM
    pairs = width // 128
    patches = info[3]

    @pl.loop(0, items * pairs)
    def _(step):
        item, pair = step // pairs, step % pairs
        rows = pl.ds(pl.multiple_of(item * ITEM, ITEM), ITEM)
        lane = lambda part: pl.ds(pl.multiple_of(part * width + pair * 128, 128), 128)
        q2, k2, v2 = qkv[rows, lane(0)], qkv[rows, lane(1)], qkv[rows, lane(2)]
        low = lax.broadcasted_iota(jnp.int32, (ITEM, 128), 1) < HEAD_DIM
        zero = jnp.zeros_like(q2)
        both = jnp.concatenate([jnp.where(low, q2, zero), jnp.where(low, zero, q2)], axis=0)
        scores = dot_nt(both, k2)
        col = lax.broadcasted_iota(jnp.int32, (1, ITEM), 1)
        valid = (col < patches) | ((col >= TEXT_AT) & (col < TEXT_AT + info[1 + item]))
        scores = jnp.where(valid, scores, -1000000000.0)
        expo = jnp.exp(scores - jnp.max(scores, axis=-1, keepdims=True))
        prob = (expo * (1.0 / jnp.sum(expo, axis=-1, keepdims=True))).astype(BF)
        probs[step] = prob
        wide = jnp.concatenate([prob[:ITEM], prob[ITEM:]], axis=1)
        values = jnp.concatenate([jnp.where(low, v2, zero), jnp.where(low, zero, v2)], axis=0)
        ctx[rows, pl.ds(pl.multiple_of(pair * 128, 128), 128)] = dot_nn(wide, values).astype(BF)


def out_kernel(text_rows, info, tok, mask, vec, ctx, out_w, *refs):
    h1, n2t, *n2v = refs[-2 - tok.shape[0] // ITEM :]
    items = tok.shape[0] // ITEM
    texts = []
    for i in range(items):
        for at, size in ((0, TEXT_AT), (TEXT_AT, ITEM - TEXT_AT)):
            rows = pl.ds(i * ITEM + at, size)
            attended = dot_nn(ctx[rows, :], out_w[...]) + vec[5:6, :]
            hidden = mixed_in(tok, mask, vec, rows) + attended
            h1[rows, :] = hidden
            normal, _unused = normalize(hidden)
            second = normal * vec[6:7, :] + vec[7:8, :]
            if at == 0:
                n2v[i][...] = second.astype(BF)
            else:
                texts.append(second[:text_rows])
    n2t[...] = jnp.concatenate(texts, axis=0).astype(BF)


def pack_kernel(info, strip0, te1, te2, te3, grad_t, pack):
    block, hid = strip0.shape[0], strip0.shape[1] // 2
    rows = grad_t.shape[0]
    other = pl.ds(pl.multiple_of((1 - info[0] % 2) * hid, 128), hid)
    for k, ref in enumerate((strip0, te1, te2, te3)):
        at = (k // 2) * block
        pack[at : at + block, (k % 2) * hid : (k % 2 + 1) * hid] = ref[pl.ds(0, block), other]
        there = pl.ds(2 * block + k * rows, rows)
        pack[there, :] = grad_t[...] if k == 0 else ref[pl.ds(block, rows), :]


def up_rows(me, pieces, target, sems):
    block = target.shape[0] // 8
    copies = []
    for index, (base, ref) in enumerate(pieces):
        for k in range(2):
            row = pl.multiple_of((me ^ (base + 2 * k)) * block, 16)
            sem = sems.at[2 * index + k]
            copies.append(pltpu.make_async_copy(ref.at[k], target.at[pl.ds(row, block)], sem))
    for copy in copies:
        copy.start()
    return copies


def place_of(me):
    return (me // 4) * 2 + me % 2


def vision_kernel(pair, items, info, grad, up_bias, *refs):
    parts, refs = refs[:items], refs[items:]
    ups, downs = refs[:4], refs[4:6]
    branch, gn2, act, low, up_w, down_w, rows_in, sems = refs[-8:]
    me = info[0]
    block = downs[0].shape[1]
    copies = up_rows(me, list(zip((0, 4, 1, 5), ups)), up_w, sems)
    place = place_of(me)
    for j in range(4):
        row = pl.multiple_of((place ^ j) * block, 16)
        copy = pltpu.make_async_copy(downs[j % 2].at[j // 2], down_w.at[pl.ds(row, block)], sems.at[8 + j])
        copy.start()
        copies.append(copy)
    for copy in copies:
        copy.wait()
    mine = grad.at[(me // 2) % 2 ^ 1] if pair else grad
    for i, part in enumerate(parts):
        rows_in[pl.ds(i * TEXT_AT, TEXT_AT), :] = part[...]
    chunk = 512
    for step in range(down_w.shape[0] // chunk):
        cols = slice(step * chunk, (step + 1) * chunk)
        upper = dot_nn(rows_in[...], up_w[:, cols]) + up_bias[0:1, cols]
        active, slope = gelu_parts(upper)
        active = active.astype(BF)
        act[:, cols] = active
        back = (dot_nt(mine[...], down_w[cols, :]) * slope).astype(BF)
        low[:, cols] = back
        if step == 0:
            sum_branch = dot_nn(active, down_w[cols, :])
            sum_gn2 = dot_nt(back, up_w[:, cols])
        else:
            sum_branch = sum_branch + dot_nn(active, down_w[cols, :])
            sum_gn2 = sum_gn2 + dot_nt(back, up_w[:, cols])
    branch[...] = sum_branch.astype(branch.dtype)
    gn2[...] = sum_gn2.astype(gn2.dtype)


def vision_grad_kernel(items, info, *refs):
    ins = refs[:items], refs[items : 2 * items]
    grads, refs = refs[2 * items], refs[2 * items + 1 :]
    acts, lows = refs[:2], refs[2:4]
    up_keep, up_send, down_keep, down_send, bias_sums = refs[-11:-6]
    left_t, act_t, right, low, turn0, turn1 = refs[-6:]
    me = info[0]
    rows, width = items * ins[0][0].shape[0], ins[0][0].shape[1]
    block = width // 8
    half = down_keep.shape[1]
    place, core = place_of(me), me % 2
    for k in range(2):
        at = pl.ds(k * rows, rows)
        right[at, :] = grads[(me // 2) % 2 ^ k]
        low[at, :] = lows[k][...]
        turned = jnp.concatenate([ref[...] for ref in ins[k]], axis=0).T
        turn = (turn0, turn1)[k]
        for b in range(8):
            spot = pl.multiple_of((me ^ b) * block, 16)
            turn[pl.ds(spot, block), :] = turned[b * block : (b + 1) * block]
        left_t[:, at] = turn[...]
        act_t[:, at] = acts[k][...].T
    chunk = 512
    for step in range(4 * half // chunk):
        cols = slice(step * chunk, (step + 1) * chunk)
        grad_up = dot_nn(left_t[...], low[:, cols])
        bias_sums[0:1, cols] = jnp.sum(low[:, cols].astype(F32), axis=0, keepdims=True)
        grad_up = grad_up.astype(BF)
        for b in range(4):
            up_keep[b, :, cols] = grad_up[2 * b * block : (2 * b + 1) * block]
            up_send[b, :, cols] = grad_up[(2 * b + 1) * block : (2 * b + 2) * block]
    for q in range(4):
        grad_down = dot_nn(act_t[q * half : (q + 1) * half, :], right[...]).astype(BF)
        side = (q // 2) ^ (place // 2)

        @pl.when(core == q % 2)
        def _():
            down_keep[side] = grad_down

        @pl.when(core != q % 2)
        def _():
            down_send[side] = grad_down


def text_kernel(info, down, up_bias, strip0, te1, te2, te3, far, even, odd, *refs):
    grad0, refs = refs[0], refs[1:]
    branch_keep, branch_send, gn2_keep, gn2_send, up_keep, up_send, grad_down, bias_sums = refs[-12:-4]
    up_w, left, right, left_t = refs[-4:]
    me = info[0]
    width = down.shape[1]
    hid = down.shape[0]
    block = width // 8
    rows = even.shape[1]
    mine = pl.ds(pl.multiple_of((me % 2) * hid, 128), hid)
    spot = lambda slot: pl.ds(pl.multiple_of((me ^ slot) * block, 16), block)
    up_w[spot(0), :] = strip0[:, mine]
    for s, te in ((2, te1), (4, te2), (6, te3)):
        up_w[spot(s), :] = te[pl.ds(0, block), mine]
        right[pl.ds(s * rows, rows), :] = te[pl.ds(block, rows), :]
    up_w[spot(1), :] = far[pl.ds(0, block), pl.ds(0, hid)]
    up_w[spot(3), :] = far[pl.ds(0, block), pl.ds(hid, hid)]
    up_w[spot(5), :] = far[pl.ds(block, block), pl.ds(0, hid)]
    up_w[spot(7), :] = far[pl.ds(block, block), pl.ds(hid, hid)]
    right[pl.ds(0, rows), :] = grad0[...]
    for k in range(4):
        right[pl.ds((2 * k + 1) * rows, rows), :] = far[pl.ds(2 * block + k * rows, rows), :]
    for slot in range(8):
        left[pl.ds(slot * rows, rows), :] = (even, odd)[slot % 2][slot // 2]
    turned = left[...].T
    for b in range(8):
        left_t[spot(b), :] = turned[b * block : (b + 1) * block]
    upper = dot_nn(left[...], up_w[...]) + up_bias[...]
    active, slope = gelu_parts(upper)
    act = active.astype(BF)
    low = (dot_nt(right[...], down[...]) * slope).astype(BF)
    bias_sums[...] = jnp.sum(low.astype(F32), axis=0, keepdims=True)
    gn2 = dot_nt(low, up_w[...]).astype(BF)
    branch = dot_nn(act, down[...]).astype(BF)
    for s in range(4):
        gn2_keep[s] = gn2[2 * s * rows : (2 * s + 1) * rows]
        gn2_send[s] = gn2[(2 * s + 1) * rows : (2 * s + 2) * rows]
        branch_keep[s] = branch[2 * s * rows : (2 * s + 1) * rows]
        branch_send[s] = branch[(2 * s + 1) * rows : (2 * s + 2) * rows]
    grad_down[...] = dot_tn(act, right[...]).astype(BF)
    grad_up = dot_nn(left_t[...], low).astype(BF)
    for b in range(4):
        up_keep[b] = grad_up[2 * b * block : (2 * b + 1) * block]
        up_send[b] = grad_up[(2 * b + 1) * block : (2 * b + 2) * block]


def attn_bwd_kernel(text_rows, info, gn2v, gn2x, t0, t1, t2, t3, grad, h1, vec, qkv, probs, weight, *refs):
    gh1, low, stacked, sums, gn2, gctx = refs[-6:]
    total, width = h1.shape
    items = total // ITEM
    text = (
        t0[0].astype(F32) + t1[...].astype(F32) + t2[...].astype(F32) + t3[...].astype(F32)
    )
    for i in range(items):
        part = pl.ds(i * TEXT_AT, TEXT_AT)
        gn2[pl.ds(i * ITEM, TEXT_AT), :] = gn2v[part, :] + gn2x[part, :].astype(F32)
        gn2[pl.ds(i * ITEM + TEXT_AT, text_rows), :] = text[i * text_rows : (i + 1) * text_rows]
        pad = ITEM - TEXT_AT - text_rows
        gn2[pl.ds(i * ITEM + TEXT_AT + text_rows, pad), :] = jnp.zeros((pad, width), F32)
    sums[...] = jnp.zeros_like(sums)

    @pl.loop(0, total // 64)
    def _(step):
        rows = pl.ds(pl.multiple_of(step * 64, 64), 64)
        normal, scale = normalize(h1[rows, :])
        above = gn2[rows, :]
        inner = above * vec[6:7, :]
        back = scale * (
            inner
            - jnp.mean(inner, axis=-1, keepdims=True)
            - normal * jnp.mean(inner * normal, axis=-1, keepdims=True)
        )
        out = grad[rows, :].astype(F32)
        hidden = out + back
        gh1[rows, :] = hidden
        low[rows, :] = hidden.astype(BF)
        sums[0:1, :] += jnp.sum(above * normal, axis=0, keepdims=True)
        sums[1:2, :] += jnp.sum(above, axis=0, keepdims=True)
        sums[2:3, :] += jnp.sum(hidden.astype(BF).astype(F32), axis=0, keepdims=True)

    gctx[...] = dot_nt(low[...], weight[...]).astype(BF)
    pairs = width // 128

    @pl.loop(0, items * pairs)
    def _(step):
        item, pair = step // pairs, step % pairs
        rows = pl.ds(pl.multiple_of(item * ITEM, ITEM), ITEM)
        lane = lambda part: pl.ds(pl.multiple_of(part * width + pair * 128, 128), 128)
        q2, k2, v2 = qkv[rows, lane(0)], qkv[rows, lane(1)], qkv[rows, lane(2)]
        g2 = gctx[rows, pl.ds(pl.multiple_of(pair * 128, 128), 128)]
        lower = lax.broadcasted_iota(jnp.int32, (ITEM, 128), 1) < HEAD_DIM
        zero = jnp.zeros_like(q2)
        split = lambda a: jnp.concatenate([jnp.where(lower, a, zero), jnp.where(lower, zero, a)], axis=0)
        both_g = split(g2)
        prob_b = probs[step]
        prob = prob_b.astype(F32)
        gprob = dot_nt(both_g, v2)
        weighted = prob * gprob
        gscore = (weighted - prob * jnp.sum(weighted, axis=-1, keepdims=True)).astype(BF)
        stacked[rows, lane(2)] = dot_tn(prob_b, both_g).astype(BF)
        stacked[rows, lane(1)] = dot_tn(gscore, split(q2)).astype(BF)
        wide = jnp.concatenate([gscore[:ITEM], gscore[ITEM:]], axis=1)
        gquery = dot_nn(wide, split(k2)).astype(BF).astype(F32) * 0.125
        stacked[rows, lane(0)] = gquery.astype(BF)

    for part in (0, 2):
        cols = stacked[:, part * width : (part + 1) * width].astype(F32)
        sums[3 + part // 2 : 4 + part // 2, :] = jnp.sum(cols, axis=0, keepdims=True)


def attn_grad_kernel(last, info, left, *refs):
    me = info[0]
    width = left.shape[1]
    block = width // 8
    keep, send, left_t, other_t, right, sem = refs[-6:]
    others, stacked = (refs[:2], refs[2]) if last else ((), refs[0])
    first = 2 * width if last else 0
    copy = pltpu.make_async_copy(stacked.at[:, pl.ds(first, right.shape[1])], right, sem.at[0])
    copy.start()
    for source, target in ((left, left_t), (others[0], other_t)) if last else ((left, left_t),):
        turned = source[...].T
        for b in range(8):
            place = pl.multiple_of((me ^ b) * block, 16)
            target[pl.ds(place, block), :] = turned[b * block : (b + 1) * block]
    for part in (1, 0) if last else (0, 1):
        cols = slice(part * width, (part + 1) * width)
        if last and part == 1:
            value = dot_nn(other_t[...], others[1][...]).astype(BF)
        else:
            if part == 0:
                copy.wait()
            value = dot_nn(left_t[...], right[:, cols]).astype(BF)
        for b in range(4):
            keep[b, :, cols] = value[2 * b * block : (2 * b + 1) * block]
            send[b, :, cols] = value[(2 * b + 1) * block : (2 * b + 2) * block]


def last_kernel(slots, info, stacked, gh1, tok, mask, vec, *refs):
    count = len(slots)
    pieces = refs[:count]
    gtok, sums, weight, sems = refs[-4:]
    copies = start_rows([(s, f, r) for (s, f), r in zip(slots, pieces)], weight, info[0], sems)
    sums[...] = jnp.zeros_like(sums)
    for copy in copies:
        copy.wait()

    @pl.loop(0, tok.shape[0] // 128)
    def _(step):
        rows = pl.ds(pl.multiple_of(step * 128, 128), 128)
        above = dot_nt(stacked[rows, :], weight[...])
        normal, scale = normalize(mixed_in(tok, mask, vec, rows))
        inner = above * vec[1:2, :]
        back = scale * (
            inner
            - jnp.mean(inner, axis=-1, keepdims=True)
            - normal * jnp.mean(inner * normal, axis=-1, keepdims=True)
        )
        hidden = gh1[rows, :] + back
        keep = mask[rows, :]
        gtok[rows, :] = hidden * (1.0 - keep)
        sums[0:1, :] += jnp.sum(hidden * keep, axis=0, keepdims=True)
        sums[1:2, :] += jnp.sum(above * normal, axis=0, keepdims=True)
        sums[2:3, :] += jnp.sum(above, axis=0, keepdims=True)


def call(kernel, outs, scratch, args, pieces=(), us=1):
    in_specs = [pl.BlockSpec(memory_space=pltpu.SMEM)]
    in_specs += [pl.BlockSpec(memory_space=pltpu.VMEM)] * (len(args) - 1)
    in_specs += [pl.BlockSpec(memory_space=pl.ANY)] * len(pieces)
    return pl.pallas_call(
        kernel,
        out_shape=[jax.ShapeDtypeStruct(s, d) for s, d in outs],
        in_specs=in_specs,
        out_specs=[pl.BlockSpec(memory_space=pltpu.VMEM)] * len(outs),
        scratch_shapes=scratch,
        compiler_params=pltpu.CompilerParams(vmem_limit_bytes=VMEM_LIMIT),
        cost_estimate=pl.CostEstimate(flops=int(us * SCALE * 1.1e9), bytes_accessed=int(us * SCALE * 1e6), transcendentals=0),
    )(*args, *pieces)


def swap(array, mask):
    return lax.ppermute(array, "fsdp", [(i, i ^ mask) for i in range(8)])


def along_rep(array, pairs):
    return lax.ppermute(array, "rep", pairs)


def add(*terms):
    out = terms[0].astype(F32)
    for term in terms[1:]:
        out = out + term.astype(F32)
    return out.astype(BF)


def planned(
    tokens,
    out_grad,
    masked,
    lengths,
    mask_vec,
    norm1_gain,
    norm1_shift,
    w_qkv,
    query_bias,
    value_bias,
    w_out,
    out_bias,
    norm2_gain,
    norm2_shift,
    vision_up,
    vision_up_bias,
    vision_down,
    vision_down_bias,
    text_up,
    text_up_bias,
    text_down,
    text_down_bias,
):
    items, row_count, width = tokens.shape
    text_rows = masked.shape[1]
    patches = row_count - text_rows
    block = width // 8
    half = block // 2
    hid = vision_down.shape[0]
    pair = 2 * hid
    hidden = 8 * hid
    total = items * ITEM
    vision_rows = items * TEXT_AT
    slot_rows = items * text_rows
    te_rows = block + slot_rows
    me = lax.axis_index("fsdp").astype(jnp.int32)
    rep = lax.axis_index("rep").astype(jnp.int32)
    core, chip, side = me % 2, me // 2, (me // 2) % 2
    sem = lambda n: pltpu.SemaphoreType.DMA((n,))
    quad = lambda r, c: ((4, r, c), BF)

    names = (
        mask_vec,
        norm1_gain,
        norm1_shift,
        query_bias,
        value_bias,
        out_bias,
        norm2_gain,
        norm2_shift,
        vision_down_bias,
        text_down_bias,
    )
    own_vec = jnp.pad(jnp.stack(names), ((0, 0), (0, 128 - block)))
    own_vec = jnp.concatenate([own_vec, vision_up_bias.reshape(-1, 128)], axis=0)
    own_vec = jnp.pad(own_vec, ((0, 16 - own_vec.shape[0]), (0, 0)))[None]
    vx, vy, vxy = swap(own_vec, 2), swap(own_vec, 4), swap(own_vec, 6)
    qx, qy = swap(w_qkv, 2), swap(w_qkv, 4)
    mask = jnp.concatenate(
        [
            jnp.zeros((items, TEXT_AT), F32),
            masked.astype(F32),
            jnp.zeros((items, ITEM - TEXT_AT - text_rows), F32),
        ],
        axis=1,
    ).reshape(total, 1)
    info = jnp.concatenate([me[None], lengths, jnp.full((1,), patches, jnp.int32)])
    tok, grad, grad_v, grad_t, grad_sums, own_out, own_down, up_mine, up_other, strip0, te1, te2, te3, t = call(
        functools.partial(prep_kernel, text_rows),
        [
            ((total, width), BF),
            ((total, width), BF),
            ((vision_rows, width), BF),
            ((slot_rows, width), BF),
            ((2, width), F32),
            ((block, width), BF),
            ((hid, width), BF),
            ((block, 2 * pair), BF),
            ((block, 2 * pair), BF),
            ((block, pair), BF),
            ((te_rows, width), BF),
            ((te_rows, width), BF),
            ((te_rows, width), BF),
            ((8, 128), F32),
        ],
        [],
        [info, tokens, out_grad, w_out, vision_down, vision_up, text_up],
        us=5,
    )
    vec_four = gate([jnp.concatenate([own_vec, vx, vy, vxy], axis=0)], [t])[0]
    vec_arrays = [vec_four, swap(vec_four, 1)]
    part1, part2 = gate([qx[:half], qy[half:]], [tok, vec_arrays[1]])

    far1, far2 = swap(part1, 4), swap(part2, 2)
    near = [swap(a, 1) for a in (w_qkv, qx, qy)]
    n1, vec, up_bias = call(
        norm_kernel,
        [((total, width), BF), ((16, width), F32), ((1, 4 * hid), F32)],
        [pltpu.VMEM((8, 16, 128), BF)],
        [info, tok, mask, *vec_arrays],
        [part1],
        us=5,
    )
    far1, far2, up_other, own_down, own_out = gate([far1, far2, up_other, own_down, own_out], [n1, *near])
    out_all = lax.all_gather(own_out, "fsdp", tiled=True)
    pairs = [[0, 2], [1, 3], [4, 6], [5, 7]]
    grad_pair = lax.all_gather(grad_v, "fsdp", axis_index_groups=pairs)
    attn = [(0, 0, w_qkv), (2, 0, qx), (4, 0, qy), (6, 0, far1), (6, half, far2)]
    attn += [(1, 0, near[0]), (3, 0, near[1]), (5, 0, near[2]), (7, 0, swap(far1, 1)), (7, half, swap(far2, 1))]
    attn_slots = tuple((p[0], p[1]) for p in attn)
    attn_arrays = [p[2] for p in attn]

    up_x, down_y = swap(up_other, 2), swap(own_down, 4)
    (qkv,) = call(
        functools.partial(qkv_kernel, attn_slots),
        [((total, 3 * width), BF)],
        [pltpu.VMEM((width, 3 * width), BF), pltpu.VMEM((1, 3 * width), F32), sem(len(attn))],
        [info, n1, vec],
        attn_arrays,
        us=8,
    )
    t = tick(t, [qkv, up_x])

    up_x, te1, te2, te3 = gate([up_x, te1, te2, te3], [t])
    up_two = jnp.stack([up_mine, up_x])
    up_y, up_c = swap(up_two, 4), swap(up_two, 1)
    te1, te3 = swap(te1, 2), swap(te3, 6)
    probs, ctx = call(
        attn_kernel,
        [((items * width // 128, 2 * ITEM, ITEM), BF), ((total, width), BF)],
        [],
        [info, qkv],
        [t],
        us=10,
    )
    t = tick(t, [ctx, up_y, up_c, te1, te3, down_y])

    up_y, te1, te2, te3, down_y = gate([up_y, te1, te2, te3, down_y], [t])
    te2 = swap(te2, 4)
    down_two = jnp.stack([own_down, down_y])
    up_yc, down_c = swap(up_y, 1), swap(down_two, 1)
    h1, n2t, *n2v = call(
        functools.partial(out_kernel, text_rows),
        [((total, width), F32), ((slot_rows, width), BF)] + [((TEXT_AT, width), BF)] * items,
        [],
        [info, tok, mask, vec, ctx, out_all],
        [t],
        us=5,
    )
    t = tick(t, [n2t, te2, up_yc, down_c, grad_pair])

    te1, te2, te3, n2t, *n2v = gate([te1, te2, te3, n2t, *n2v], [t])
    (pack,) = call(
        pack_kernel,
        [((2 * block + 4 * slot_rows, width), BF)],
        [],
        [info, strip0, te1, te2, te3, grad_t],
    )
    text_in = [swap(n2t, 2), swap(n2t, 4), swap(n2t, 6)]
    n2x = [swap(n2v[0], 2)]
    far = swap(pack, 1)
    weights = [up_two, up_y, up_c, up_yc, down_two, down_c]

    def vision(rows_in, grads, kind, after):
        return call(
            functools.partial(vision_kernel, kind == BF, items),
            [
                ((vision_rows, width), kind),
                ((vision_rows, width), kind),
                ((vision_rows, 4 * hid), BF),
                ((vision_rows, 4 * hid), BF),
            ],
            [
                pltpu.VMEM((width, 4 * hid), BF),
                pltpu.VMEM((4 * hid, width), BF),
                pltpu.VMEM((vision_rows, width), BF),
                sem(12),
            ],
            [info, grads, up_bias, *rows_in],
            [*weights, *after],
            us=9,
        )

    branch_own, gn2_own, act_own, low_own = vision(n2v, grad_v, F32, [pack])
    t = tick(t, [gn2_own, *text_in, n2x[0], far])

    far, *text_in = gate([far, *text_in], [t])
    text_four = jnp.stack([n2t, *text_in])
    text_odd = swap(text_four, 1)
    n2x += [swap(a, 2) for a in gate(n2v[1:], [t])]
    branch_keep, branch_send, gn2_keep, gn2_send, tu_keep, tu_send, td, text_bias_sum = call(
        text_kernel,
        [
            quad(slot_rows, width),
            quad(slot_rows, width),
            quad(slot_rows, width),
            quad(slot_rows, width),
            quad(block, hid),
            quad(block, hid),
            ((hid, width), BF),
            ((1, hid), F32),
        ],
        [
            pltpu.VMEM((width, hid), BF),
            pltpu.VMEM((8 * slot_rows, width), BF),
            pltpu.VMEM((8 * slot_rows, width), BF),
            pltpu.VMEM((width, 8 * slot_rows), BF),
        ],
        [
            info,
            text_down,
            text_up_bias.astype(F32).reshape(1, hid),
            strip0,
            te1,
            te2,
            te3,
            far,
            text_four,
            text_odd,
            grad_t,
        ],
        us=6,
    )
    t = tick(t, [gn2_keep, *n2x])
    tu_keep, tu_send, td = lax.psum((tu_keep, tu_send, td), "rep")

    gn2_send, *n2x = gate([gn2_send, *n2x], [t])
    gn2_sum = add(gn2_keep, swap(gn2_send, 1))
    gn2_text = [gn2_sum] + [swap(gn2_sum[s], 2 * s) for s in (1, 2, 3)]
    branch_x, gn2_x, act_x, low_x = vision(n2x, grad_pair, BF, [gn2_sum])
    t = tick(t, [gn2_x, *gn2_text[1:]])

    (gn2_x,) = gate([gn2_x], [t])
    gn2_back = swap(gn2_x, 2)
    vu_keep, vu_send, vd_keep, vd_send, vu_bias_sum = call(
        functools.partial(vision_grad_kernel, items),
        [
            quad(block, 4 * hid),
            quad(block, 4 * hid),
            ((2, hid, width), BF),
            ((2, hid, width), BF),
            ((1, 4 * hid), F32),
        ],
        [
            pltpu.VMEM((width, 2 * vision_rows), BF),
            pltpu.VMEM((4 * hid, 2 * vision_rows), BF),
            pltpu.VMEM((2 * vision_rows, width), BF),
            pltpu.VMEM((2 * vision_rows, 4 * hid), BF),
            pltpu.VMEM((width, vision_rows), BF),
            pltpu.VMEM((width, vision_rows), BF),
        ],
        [info, *n2v, *n2x, grad_pair, act_own, act_x, low_own, low_x],
        [t],
        us=12,
    )
    t = tick(t, [vu_bias_sum, gn2_back])

    vu_send, vd_send, branch_x, branch_send, gn2_back = gate([vu_send, vd_send, branch_x, branch_send, gn2_back], [t])
    vu_got, vd_got = swap(vu_send, 1), swap(vd_send, 1)
    vd_near, vd_far = add(vd_keep[0], vd_got[0]), add(vd_keep[1], vd_got[1])
    vu_far = [add(vu_keep[k], vu_got[k]) for k in (2, 3)]
    vd_y, vu_y1 = swap(vd_far, 4), swap(vu_far[1], 4)
    branch_back = swap(branch_x, 2)
    branch_got = swap(branch_send, 1)
    gh1, low_attn, stacked, sums_two = call(
        functools.partial(attn_bwd_kernel, text_rows),
        [((total, width), F32), ((total, width), BF), ((total, 3 * width), BF), ((8, width), F32)],
        [pltpu.VMEM((total, width), F32), pltpu.VMEM((total, width), BF)],
        [info, gn2_own, gn2_back, *gn2_text, grad, h1, vec, qkv, probs, out_all],
        [vd_far, *vu_far],
        us=18,
    )
    t = tick(t, [stacked, vd_y, vu_y1, branch_back, branch_got])

    vd_y, vu_y1, vu_far0, branch_got = gate([vd_y, vu_y1, vu_far[0], branch_got], [t])
    vd_sum = add(vd_near, vd_y)
    vu_x = swap(add(vu_keep[1], vu_got[1], vu_y1), 2)
    vu_y0 = swap(vu_far0, 4)

    def attn_grads(last, after):
        return call(
            functools.partial(attn_grad_kernel, last),
            [quad(block, 2 * width), quad(block, 2 * width)],
            [
                pltpu.VMEM((width, total), BF),
                pltpu.VMEM((width, total), BF),
                pltpu.VMEM((total, (1 if last else 2) * width), BF),
                sem(1),
            ],
            [info, n1, ctx, low_attn] if last else [info, n1],
            [stacked, *after],
            us=5,
        )

    a_keep, a_send = attn_grads(False, [t])
    t = tick(t, [a_keep, vu_x, vu_y0])
    a_send, vu_x, vu_y0 = gate([a_send, vu_x, vu_y0], [t])
    a_got = swap(a_send, 1)
    branch_sum = add(branch_keep, branch_got)
    vu_both = jnp.stack([add(vu_keep[0], vu_got[0], vu_y0), vu_x])
    vu, vd = lax.psum((vu_both, vd_sum), "rep", axis_index_groups=[[1, 0, 2, 3]])
    b_keep, b_send = attn_grads(True, [t])
    t = tick(t, [b_keep, a_got])
    a_got, b_send, branch_sum = gate([a_got, b_send, branch_sum], [t])
    b_got = swap(b_send, 1)

    def begin(keep, got, one):
        i = one // 2
        return add(jnp.stack([keep[i], keep[3]]), jnp.stack([got[i], got[3]]))

    a_first, b_first = begin(a_keep, a_got, 2), begin(b_keep, b_got, 4)
    a_there, b_there = swap(a_first, 2), swap(b_first, 4)
    gtok, sums_one = call(
        functools.partial(last_kernel, attn_slots),
        [((total, width), F32), ((8, width), F32)],
        [pltpu.VMEM((width, 3 * width), BF), sem(len(attn))],
        [info, stacked, gh1, tok, mask, vec],
        attn_arrays + [a_first, b_first, vu_both, vd_sum],
        us=12,
    )
    t = tick(t, [sums_one, a_there, b_there])

    a_there, b_there = gate([a_there, b_there], [t])
    a_next, b_next = add(a_keep[2], a_got[2], a_there[1]), add(b_keep[1], b_got[1], b_there[1])
    a_beyond, b_beyond = swap(a_next, 4), swap(b_next, 2)
    (sums_one,) = gate([sums_one], [tick(t, [a_next, b_next])])
    vu_sum = vu_bias_sum.reshape(2, 1, pair)
    vu_sum = jnp.where(
        side == 0,
        jnp.concatenate([vu_sum, jnp.zeros_like(vu_sum)], axis=1),
        jnp.concatenate([jnp.zeros_like(vu_sum), vu_sum], axis=1),
    )
    count, rows = len(names), hid // block
    vec_rows = count + 2 * rows
    vu_sum = vu_sum.reshape(8, rows, block).transpose(1, 0, 2).reshape(-1, width)
    flat = jnp.concatenate(
        [sums_one[0:3], sums_two[3:5], sums_two[2:3], sums_two[0:2], grad_sums, vu_sum], axis=0
    )
    for m in (1, 2, 4):
        flat = flat + swap(flat, m)
    own_sums = lax.dynamic_slice_in_dim(flat, me * block, block, axis=1)
    own_sums = jnp.concatenate([own_sums, text_bias_sum.reshape(-1, block)], axis=0)
    ga = add(a_keep[0], a_got[0], a_there[0], a_beyond)
    gb = add(b_keep[0], b_got[0], b_there[0], b_beyond)

    inner = (rep == 1) | (rep == 2)

    def rep_sum(array):
        part = add(array, along_rep(array, [(0, 1), (3, 2)]))
        whole = add(part, along_rep(part, [(1, 2), (2, 1)]))
        return jnp.where(inner, whole, along_rep(whole, [(1, 0), (2, 3)]))

    plane_sums = [ga, gb]
    own_sums = own_sums.reshape(-1)
    own_sums = jnp.pad(own_sums, (0, 8 * 2 * width - own_sums.shape[0])).reshape(8, 2 * width)
    ga, gb = rep_sum(jnp.concatenate([ga, own_sums.astype(BF)], axis=0)), rep_sum(gb)
    last_sums = [ga, gb]
    tu_keep, tu_send, td, branch_sum, branch_back = gate([tu_keep, tu_send, td, branch_sum, branch_back], plane_sums)
    branch_t = [branch_sum] + [swap(branch_sum[s], 2 * s) for s in (1, 2, 3)]
    tu_got = swap(tu_send, 1)
    tu_wide = jnp.where(
        core == 0,
        jnp.concatenate([tu_keep, tu_got], axis=-1),
        jnp.concatenate([tu_got, tu_keep], axis=-1),
    )
    tu_all = [tu_wide[0]] + [swap(tu_wide[s], 2 * s) for s in (1, 2, 3)]
    tu_x = [jnp.where(side == 0, tu_all[k], tu_all[k ^ 1]) for k in range(4)]
    tu_y = [jnp.where(me // 4 == 0, tu_x[k], tu_x[k ^ 2]) for k in range(4)]
    grad_text_up = jnp.concatenate(tu_y, axis=1).astype(F32)
    grad_text_down = td.astype(F32)

    ga = ga.astype(F32)
    mine = ga[block:].reshape(-1)[: vec_rows * block].reshape(vec_rows, block)
    ga = ga[:block]
    vec_grad = [mine[i] for i in range(count)]
    vu_bias_grad = mine[count : count + rows].reshape(-1)
    tu_bias_grad = mine[count + rows : count + 2 * rows].reshape(-1)

    vu, vd = gate([vu, vd], last_sums)
    gb = gb.astype(F32)
    grad_w_qkv = jnp.concatenate([ga, gb[:, :width]], axis=1)
    grad_w_out = gb[:, width:]
    vu_s = [jnp.where(side == 0, vu[k], vu[1 - k]) for k in range(2)]
    grad_vision_up = jnp.concatenate(
        [vu_s[0][:, :pair], vu_s[1][:, :pair], vu_s[0][:, pair:], vu_s[1][:, pair:]], axis=1
    ).astype(F32)
    grad_vision_down = vd.astype(F32)
    h1 = h1.reshape(items, ITEM, width)
    branch_v = (branch_own + branch_back.astype(F32)).reshape(items, TEXT_AT, width)[:, :patches]
    mixed_v = h1[:, :patches] + branch_v + vec[8][None, None]
    branch_t = branch_t[0][0].astype(F32) + sum(b.astype(F32) for b in branch_t[1:])
    branch_t = branch_t.reshape(items, text_rows, width)
    mixed_t = h1[:, TEXT_AT : TEXT_AT + text_rows] + branch_t + vec[9][None, None]
    mixed = jnp.concatenate([mixed_v.astype(BF), mixed_t.astype(BF)], axis=1)
    gtok = gtok.reshape(items, ITEM, width)
    grad_tokens = jnp.concatenate(
        [gtok[:, :patches], gtok[:, TEXT_AT : TEXT_AT + text_rows]], axis=1
    )
    return (
        mixed,
        grad_tokens,
        vec_grad[0],
        vec_grad[1],
        vec_grad[2],
        grad_w_qkv,
        vec_grad[3],
        vec_grad[4],
        grad_w_out,
        vec_grad[5],
        vec_grad[6],
        vec_grad[7],
        grad_vision_up,
        vu_bias_grad,
        grad_vision_down,
        vec_grad[8],
        grad_text_up,
        tu_bias_grad,
        grad_text_down,
        vec_grad[9],
    )


def layer_norm(hidden, gain, shift):
    center = hidden - jnp.mean(hidden, axis=-1, keepdims=True)
    spread = jnp.mean(center * center, axis=-1, keepdims=True)
    return center * lax.rsqrt(spread + epsilon) * gain + shift


def exact_gelu(values):
    return jax.nn.gelu(values, approximate=False)


def expert_forward(rows_in, up_matrix, up_shift, down_matrix, down_shift):
    upper = jnp.dot(rows_in, up_matrix, preferred_element_type=jnp.float32) + up_shift.astype(
        jnp.float32
    )
    active, gelu_pull = jax.vjp(exact_gelu, upper)
    active_b = active.astype(jnp.bfloat16)
    result = jnp.dot(active_b, down_matrix, preferred_element_type=jnp.float32) + down_shift.astype(
        jnp.float32
    )
    return (result, active_b, gelu_pull)


def expert_backward(rows_in, active_b, gelu_pull, up_matrix, down_matrix, grad_b):
    grad_down = jnp.einsum("rf,rd->fd", active_b, grad_b, preferred_element_type=jnp.float32)
    grad_down_shift = jnp.sum(grad_b.astype(jnp.float32), axis=0)
    grad_active = jnp.einsum("rd,fd->rf", grad_b, down_matrix, preferred_element_type=jnp.float32)
    (grad_upper,) = gelu_pull(grad_active)
    upper_b = grad_upper.astype(jnp.bfloat16)
    grad_up = jnp.einsum("rd,rf->df", rows_in, upper_b, preferred_element_type=jnp.float32)
    grad_up_shift = jnp.sum(upper_b.astype(jnp.float32), axis=0)
    grad_rows = jnp.einsum("rf,df->rd", upper_b, up_matrix, preferred_element_type=jnp.float32)
    return (grad_up, grad_up_shift, grad_down, grad_down_shift, grad_rows)


def general(
    tokens,
    out_grad,
    masked,
    lengths,
    mask_vec,
    norm1_gain,
    norm1_shift,
    w_qkv,
    query_bias,
    value_bias,
    w_out,
    out_bias,
    norm2_gain,
    norm2_shift,
    vision_up,
    vision_up_bias,
    vision_down,
    vision_down_bias,
    text_up,
    text_up_bias,
    text_down,
    text_down_bias,
):
    item_count, row_count, model_width = tokens.shape
    slot_count = masked.shape[1]
    patches = row_count - slot_count
    head_count = model_width // HEAD_DIM
    split_shape = (item_count, row_count, head_count, HEAD_DIM)

    def fetch_attention():
        return (
            lax.all_gather(mask_vec, "fsdp", axis=0, tiled=True),
            lax.all_gather(norm1_gain, "fsdp", axis=0, tiled=True),
            lax.all_gather(norm1_shift, "fsdp", axis=0, tiled=True),
            lax.all_gather(w_qkv, "fsdp", axis=0, tiled=True),
            lax.all_gather(query_bias, "fsdp", axis=0, tiled=True),
            lax.all_gather(value_bias, "fsdp", axis=0, tiled=True),
            lax.all_gather(w_out, "fsdp", axis=0, tiled=True),
            lax.all_gather(out_bias, "fsdp", axis=0, tiled=True),
        )

    def fetch_feedforward():
        return (
            lax.all_gather(norm2_gain, "fsdp", axis=0, tiled=True),
            lax.all_gather(norm2_shift, "fsdp", axis=0, tiled=True),
            lax.all_gather(vision_up, "fsdp", axis=0, tiled=True),
            lax.all_gather(vision_up_bias, "fsdp", axis=0, tiled=True),
            lax.all_gather(vision_down, "fsdp", axis=0, tiled=True),
            lax.all_gather(vision_down_bias, "fsdp", axis=0, tiled=True),
            lax.all_gather(text_up, "fsdp", axis=0, tiled=True),
            lax.all_gather(text_up_bias, "fsdp", axis=0, tiled=True),
            lax.all_gather(text_down, "fsdp", axis=0, tiled=True),
            lax.all_gather(text_down_bias, "fsdp", axis=0, tiled=True),
        )

    attn_full = fetch_attention()
    full_mask, gain_one, shift_one, qkv_matrix, query_shift, value_shift, out_matrix, out_shift = (
        attn_full
    )
    mask_rows = jnp.concatenate(
        [jnp.zeros((item_count, patches), jnp.float32), masked.astype(jnp.float32)], axis=1
    )[:, :, None]
    hidden0 = mask_rows * full_mask.astype(jnp.float32) + (1.0 - mask_rows) * tokens.astype(
        jnp.float32
    )
    normed1, first_pull = jax.vjp(
        layer_norm, hidden0, gain_one.astype(jnp.float32), shift_one.astype(jnp.float32)
    )
    first_in = normed1.astype(jnp.bfloat16).reshape(item_count * row_count, model_width)
    projected = jnp.dot(first_in, qkv_matrix, preferred_element_type=jnp.float32)
    query_b = (
        ((projected[:, :model_width] + query_shift.astype(jnp.float32)) * 0.125)
        .astype(jnp.bfloat16)
        .reshape(split_shape)
    )
    key_b = projected[:, model_width : 2 * model_width].astype(jnp.bfloat16).reshape(split_shape)
    value_b = (
        (projected[:, 2 * model_width :] + value_shift.astype(jnp.float32))
        .astype(jnp.bfloat16)
        .reshape(split_shape)
    )
    key_index = jnp.arange(row_count, dtype=jnp.int32)
    valid_keys = (key_index[None, :] < patches + lengths[:, None])[:, None, None, :]

    def scores_of():
        raw_scores = jnp.einsum(
            "iqhd,ikhd->ihqk", query_b, key_b, preferred_element_type=jnp.float32
        )
        return jnp.where(valid_keys, raw_scores, -1000000000.0)

    scores = scores_of()
    top_score = jnp.max(scores, axis=-1, keepdims=True)
    expo = jnp.exp(scores - top_score)
    totals = jnp.sum(expo, axis=-1, keepdims=True)
    probs = expo / totals
    log_total = top_score + jnp.log(totals)
    context = jnp.einsum(
        "ihqk,ikhd->iqhd", probs.astype(jnp.bfloat16), value_b, preferred_element_type=jnp.float32
    )
    context_b = context.reshape(item_count * row_count, model_width).astype(jnp.bfloat16)
    attended = jnp.dot(
        context_b, out_matrix, preferred_element_type=jnp.float32
    ) + out_shift.astype(jnp.float32)
    hidden1 = hidden0 + attended.reshape(item_count, row_count, model_width)
    ffn_full = fetch_feedforward()
    (
        gain_two,
        shift_two,
        vision_upm,
        vision_upb,
        vision_downm,
        vision_downb,
        text_upm,
        text_upb,
        text_downm,
        text_downb,
    ) = ffn_full
    normed2, second_pull = jax.vjp(
        layer_norm, hidden1, gain_two.astype(jnp.float32), shift_two.astype(jnp.float32)
    )
    second_in = normed2.astype(jnp.bfloat16)
    patch_in = second_in[:, :patches].reshape(-1, model_width)
    text_in = second_in[:, patches:].reshape(-1, model_width)
    vision_out, vision_act, vision_pull = expert_forward(
        patch_in, vision_upm, vision_upb, vision_downm, vision_downb
    )
    text_out, text_act, text_pull = expert_forward(
        text_in, text_upm, text_upb, text_downm, text_downb
    )
    mixed = hidden1 + jnp.concatenate(
        [
            vision_out.reshape(item_count, patches, model_width),
            text_out.reshape(item_count, slot_count, model_width),
        ],
        axis=1,
    )
    cotangent = out_grad.astype(jnp.float32)
    branch_b = cotangent.astype(jnp.bfloat16)
    ffn_back = fetch_feedforward()
    vision_grads = expert_backward(
        patch_in,
        vision_act,
        vision_pull,
        ffn_back[2],
        ffn_back[4],
        branch_b[:, :patches].reshape(-1, model_width),
    )
    text_grads = expert_backward(
        text_in,
        text_act,
        text_pull,
        ffn_back[6],
        ffn_back[8],
        branch_b[:, patches:].reshape(-1, model_width),
    )
    grad_normed2 = jnp.concatenate(
        [
            vision_grads[4].reshape(item_count, patches, model_width),
            text_grads[4].reshape(item_count, slot_count, model_width),
        ],
        axis=1,
    )
    grad_hidden1_norm, grad_gain_two, grad_shift_two = second_pull(grad_normed2)
    grad_hidden1 = cotangent + grad_hidden1_norm
    attn_back = fetch_attention()
    grad_attn_b = grad_hidden1.reshape(-1, model_width).astype(jnp.bfloat16)
    grad_out_matrix = jnp.einsum(
        "rd,re->de", context_b, grad_attn_b, preferred_element_type=jnp.float32
    )
    grad_out_shift = jnp.sum(grad_attn_b.astype(jnp.float32), axis=0)
    grad_context = jnp.einsum(
        "re,de->rd", grad_attn_b, attn_back[6], preferred_element_type=jnp.float32
    )
    grad_context_b = grad_context.astype(jnp.bfloat16).reshape(split_shape)
    again_probs = jnp.exp(scores_of() - log_total)
    grad_probs = jnp.einsum(
        "iqhd,ikhd->ihqk", grad_context_b, value_b, preferred_element_type=jnp.float32
    )
    grad_value = jnp.einsum(
        "ihqk,iqhd->ikhd",
        again_probs.astype(jnp.bfloat16),
        grad_context_b,
        preferred_element_type=jnp.float32,
    )
    row_inner = jnp.sum(again_probs * grad_probs, axis=-1, keepdims=True)
    grad_scores_b = (again_probs * (grad_probs - row_inner)).astype(jnp.bfloat16)
    grad_query = jnp.einsum(
        "ihqk,ikhd->iqhd", grad_scores_b, key_b, preferred_element_type=jnp.float32
    )
    grad_key = jnp.einsum(
        "ihqk,iqhd->ikhd", grad_scores_b, query_b, preferred_element_type=jnp.float32
    )
    grad_query_b = grad_query.astype(jnp.bfloat16) * jnp.bfloat16(0.125)
    stacked = jnp.concatenate(
        [
            grad_query_b.reshape(-1, model_width),
            grad_key.astype(jnp.bfloat16).reshape(-1, model_width),
            grad_value.astype(jnp.bfloat16).reshape(-1, model_width),
        ],
        axis=1,
    )
    grad_qkv = jnp.einsum("rd,re->de", first_in, stacked, preferred_element_type=jnp.float32)
    grad_query_shift = jnp.sum(stacked[:, :model_width].astype(jnp.float32), axis=0)
    grad_value_shift = jnp.sum(stacked[:, 2 * model_width :].astype(jnp.float32), axis=0)
    grad_normed1 = jnp.einsum(
        "re,de->rd", stacked, attn_back[3], preferred_element_type=jnp.float32
    )
    grad_hidden0_norm, grad_gain_one, grad_shift_one = first_pull(
        grad_normed1.reshape(item_count, row_count, model_width)
    )
    grad_hidden0 = grad_hidden1 + grad_hidden0_norm
    grad_tokens = grad_hidden0 * (1.0 - mask_rows)
    grad_mask = jnp.sum(grad_hidden0 * mask_rows, axis=(0, 1))
    ffn_share = (
        lax.psum_scatter(grad_gain_two, "fsdp", scatter_dimension=0, tiled=True),
        lax.psum_scatter(grad_shift_two, "fsdp", scatter_dimension=0, tiled=True),
        lax.psum_scatter(vision_grads[0], "fsdp", scatter_dimension=0, tiled=True),
        lax.psum_scatter(vision_grads[1], "fsdp", scatter_dimension=0, tiled=True),
        lax.psum_scatter(vision_grads[2], "fsdp", scatter_dimension=0, tiled=True),
        lax.psum_scatter(vision_grads[3], "fsdp", scatter_dimension=0, tiled=True),
        lax.psum_scatter(text_grads[0], "fsdp", scatter_dimension=0, tiled=True),
        lax.psum_scatter(text_grads[1], "fsdp", scatter_dimension=0, tiled=True),
        lax.psum_scatter(text_grads[2], "fsdp", scatter_dimension=0, tiled=True),
        lax.psum_scatter(text_grads[3], "fsdp", scatter_dimension=0, tiled=True),
    )
    attn_share = (
        lax.psum_scatter(grad_mask, "fsdp", scatter_dimension=0, tiled=True),
        lax.psum_scatter(grad_gain_one, "fsdp", scatter_dimension=0, tiled=True),
        lax.psum_scatter(grad_shift_one, "fsdp", scatter_dimension=0, tiled=True),
        lax.psum_scatter(grad_qkv, "fsdp", scatter_dimension=0, tiled=True),
        lax.psum_scatter(grad_query_shift, "fsdp", scatter_dimension=0, tiled=True),
        lax.psum_scatter(grad_value_shift, "fsdp", scatter_dimension=0, tiled=True),
        lax.psum_scatter(grad_out_matrix, "fsdp", scatter_dimension=0, tiled=True),
        lax.psum_scatter(grad_out_shift, "fsdp", scatter_dimension=0, tiled=True),
    )
    quarter = (
        lax.psum_scatter(
            attn_share[0].astype(jnp.bfloat16), "rep", scatter_dimension=0, tiled=True
        ).astype(jnp.float32),
        lax.psum_scatter(
            attn_share[1].astype(jnp.bfloat16), "rep", scatter_dimension=0, tiled=True
        ).astype(jnp.float32),
        lax.psum_scatter(
            attn_share[2].astype(jnp.bfloat16), "rep", scatter_dimension=0, tiled=True
        ).astype(jnp.float32),
        lax.psum_scatter(
            attn_share[3].astype(jnp.bfloat16), "rep", scatter_dimension=0, tiled=True
        ).astype(jnp.float32),
        lax.psum_scatter(
            attn_share[4].astype(jnp.bfloat16), "rep", scatter_dimension=0, tiled=True
        ).astype(jnp.float32),
        lax.psum_scatter(
            attn_share[5].astype(jnp.bfloat16), "rep", scatter_dimension=0, tiled=True
        ).astype(jnp.float32),
        lax.psum_scatter(
            attn_share[6].astype(jnp.bfloat16), "rep", scatter_dimension=0, tiled=True
        ).astype(jnp.float32),
        lax.psum_scatter(
            attn_share[7].astype(jnp.bfloat16), "rep", scatter_dimension=0, tiled=True
        ).astype(jnp.float32),
        lax.psum_scatter(
            ffn_share[0].astype(jnp.bfloat16), "rep", scatter_dimension=0, tiled=True
        ).astype(jnp.float32),
        lax.psum_scatter(
            ffn_share[1].astype(jnp.bfloat16), "rep", scatter_dimension=0, tiled=True
        ).astype(jnp.float32),
        lax.psum_scatter(
            ffn_share[2].astype(jnp.bfloat16), "rep", scatter_dimension=0, tiled=True
        ).astype(jnp.float32),
        lax.psum_scatter(
            ffn_share[3].astype(jnp.bfloat16), "rep", scatter_dimension=0, tiled=True
        ).astype(jnp.float32),
        lax.psum_scatter(
            ffn_share[4].astype(jnp.bfloat16), "rep", scatter_dimension=0, tiled=True
        ).astype(jnp.float32),
        lax.psum_scatter(
            ffn_share[5].astype(jnp.bfloat16), "rep", scatter_dimension=0, tiled=True
        ).astype(jnp.float32),
        lax.psum_scatter(
            ffn_share[6].astype(jnp.bfloat16), "rep", scatter_dimension=0, tiled=True
        ).astype(jnp.float32),
        lax.psum_scatter(
            ffn_share[7].astype(jnp.bfloat16), "rep", scatter_dimension=0, tiled=True
        ).astype(jnp.float32),
        lax.psum_scatter(
            ffn_share[8].astype(jnp.bfloat16), "rep", scatter_dimension=0, tiled=True
        ).astype(jnp.float32),
        lax.psum_scatter(
            ffn_share[9].astype(jnp.bfloat16), "rep", scatter_dimension=0, tiled=True
        ).astype(jnp.float32),
    )
    summed = (
        lax.all_gather(quarter[0].astype(jnp.bfloat16), "rep", axis=0, tiled=True).astype(
            jnp.float32
        ),
        lax.all_gather(quarter[1].astype(jnp.bfloat16), "rep", axis=0, tiled=True).astype(
            jnp.float32
        ),
        lax.all_gather(quarter[2].astype(jnp.bfloat16), "rep", axis=0, tiled=True).astype(
            jnp.float32
        ),
        lax.all_gather(quarter[3].astype(jnp.bfloat16), "rep", axis=0, tiled=True).astype(
            jnp.float32
        ),
        lax.all_gather(quarter[4].astype(jnp.bfloat16), "rep", axis=0, tiled=True).astype(
            jnp.float32
        ),
        lax.all_gather(quarter[5].astype(jnp.bfloat16), "rep", axis=0, tiled=True).astype(
            jnp.float32
        ),
        lax.all_gather(quarter[6].astype(jnp.bfloat16), "rep", axis=0, tiled=True).astype(
            jnp.float32
        ),
        lax.all_gather(quarter[7].astype(jnp.bfloat16), "rep", axis=0, tiled=True).astype(
            jnp.float32
        ),
        lax.all_gather(quarter[8].astype(jnp.bfloat16), "rep", axis=0, tiled=True).astype(
            jnp.float32
        ),
        lax.all_gather(quarter[9].astype(jnp.bfloat16), "rep", axis=0, tiled=True).astype(
            jnp.float32
        ),
        lax.all_gather(quarter[10].astype(jnp.bfloat16), "rep", axis=0, tiled=True).astype(
            jnp.float32
        ),
        lax.all_gather(quarter[11].astype(jnp.bfloat16), "rep", axis=0, tiled=True).astype(
            jnp.float32
        ),
        lax.all_gather(quarter[12].astype(jnp.bfloat16), "rep", axis=0, tiled=True).astype(
            jnp.float32
        ),
        lax.all_gather(quarter[13].astype(jnp.bfloat16), "rep", axis=0, tiled=True).astype(
            jnp.float32
        ),
        lax.all_gather(quarter[14].astype(jnp.bfloat16), "rep", axis=0, tiled=True).astype(
            jnp.float32
        ),
        lax.all_gather(quarter[15].astype(jnp.bfloat16), "rep", axis=0, tiled=True).astype(
            jnp.float32
        ),
        lax.all_gather(quarter[16].astype(jnp.bfloat16), "rep", axis=0, tiled=True).astype(
            jnp.float32
        ),
        lax.all_gather(quarter[17].astype(jnp.bfloat16), "rep", axis=0, tiled=True).astype(
            jnp.float32
        ),
    )
    return (
        mixed.astype(jnp.bfloat16),
        grad_tokens,
        summed[0],
        summed[1],
        summed[2],
        summed[3],
        summed[4],
        summed[5],
        summed[6],
        summed[7],
        summed[8],
        summed[9],
        summed[10],
        summed[11],
        summed[12],
        summed[13],
        summed[14],
        summed[15],
        summed[16],
        summed[17],
    )


def solution(mesh):
    if mesh.shape["fsdp"] == 8 and mesh.shape["rep"] == 4:
        body = planned
    else:
        body = general
    return jax.shard_map(
        body,
        mesh=mesh,
        in_specs=(
            P(("fsdp", "rep"), None, None),
            P(("fsdp", "rep"), None, None),
            P(("fsdp", "rep"), None),
            P(("fsdp", "rep")),
            P("fsdp"),
            P("fsdp"),
            P("fsdp"),
            P("fsdp", None),
            P("fsdp"),
            P("fsdp"),
            P("fsdp", None),
            P("fsdp"),
            P("fsdp"),
            P("fsdp"),
            P("fsdp", None),
            P("fsdp"),
            P("fsdp", None),
            P("fsdp"),
            P("fsdp", None),
            P("fsdp"),
            P("fsdp", None),
            P("fsdp"),
        ),
        out_specs=(
            P(("fsdp", "rep"), None, None),
            P(("fsdp", "rep"), None, None),
            P("fsdp"),
            P("fsdp"),
            P("fsdp"),
            P("fsdp", None),
            P("fsdp"),
            P("fsdp"),
            P("fsdp", None),
            P("fsdp"),
            P("fsdp"),
            P("fsdp"),
            P("fsdp", None),
            P("fsdp"),
            P("fsdp", None),
            P("fsdp"),
            P("fsdp", None),
            P("fsdp"),
            P("fsdp", None),
            P("fsdp"),
        ),
        check_vma=False,
    )
```

```python
import functools
import math

import jax
import jax.numpy as jnp
from jax import lax
from jax.experimental import pallas as pl
from jax.experimental.pallas import tpu as pltpu
from jax.sharding import PartitionSpec as P

HEAD_DIM = 64
BF = jnp.bfloat16
F32 = jnp.float32
epsilon = 1e-06
VMEM_LIMIT = 58 * 1024 * 1024

ITEM = 256
SCALE = 0.35
TEXT_AT = 208


def cdiv(a, b):
    return -(-a // b)


def dot_nn(a, b):
    return lax.dot_general(a, b, (((1,), (0,)), ((), ())), preferred_element_type=F32)


def dot_nt(a, b):
    return lax.dot_general(a, b, (((1,), (1,)), ((), ())), preferred_element_type=F32)


def dot_tn(a, b):
    return lax.dot_general(a, b, (((0,), (0,)), ((), ())), preferred_element_type=F32)


def gelu_parts(upper):
    half = 0.5 * (1.0 + lax.erf(upper * math.sqrt(0.5)))
    slope = half + upper * (jnp.exp(-0.5 * upper * upper) * (1.0 / math.sqrt(2.0 * math.pi)))
    return upper * half, slope


def normalize(hidden):
    center = hidden - jnp.mean(hidden, axis=-1, keepdims=True)
    spread = jnp.mean(center * center, axis=-1, keepdims=True)
    scale = lax.rsqrt(spread + epsilon)
    return center * scale, scale


def start_rows(pieces, target, me, sems):
    block = target.shape[0] // 8
    copies = []
    for index, (slot, first, ref) in enumerate(pieces):
        row = pl.multiple_of((me ^ slot) * block + first, 16)
        copy = pltpu.make_async_copy(ref, target.at[pl.ds(row, ref.shape[0])], sems.at[index])
        copy.start()
        copies.append(copy)
    return copies


def mixed_in(tok, mask, vec, rows):
    keep = mask[rows, :]
    return keep * vec[0:1, :] + (1.0 - keep) * tok[rows, :].astype(F32)


def gate_kernel(count, *refs):
    del count, refs


def gate(arrays, after):
    count = len(arrays)
    return pl.pallas_call(
        functools.partial(gate_kernel, count),
        out_shape=[jax.ShapeDtypeStruct(a.shape, a.dtype) for a in arrays],
        in_specs=[pl.BlockSpec(memory_space=pl.ANY)] * (count + len(after)),
        out_specs=[pl.BlockSpec(memory_space=pl.ANY)] * count,
        input_output_aliases={i: i for i in range(count)},
        cost_estimate=pl.CostEstimate(flops=1000, bytes_accessed=1000, transcendentals=0),
    )(*arrays, *after)


def tick(token, after):
    return gate([token], after)[0]


def prep_kernel(text_rows, info, tokens, out_grad, w_out, down, up, text_up, *outs):
    tok, grad, grad_v, grad_t, sums, out_copy, down_copy, up_mine, up_other, strip0, te1, te2, te3, token = outs
    token[...] = jnp.zeros(token.shape, F32)
    items, row_count, width = tokens.shape
    patches = row_count - text_rows
    tail = ITEM - TEXT_AT - text_rows
    zeros = lambda n: jnp.zeros((n, width), F32)
    totals = [zeros(1), zeros(1)]
    texts = []
    for i in range(items):
        for source, target in ((tokens, tok), (out_grad, grad)):
            whole = source[i].astype(F32)
            patch, text = whole[:patches], whole[patches:]
            full = jnp.concatenate([patch, zeros(TEXT_AT - patches), text, zeros(tail)], axis=0)
            target[pl.ds(i * ITEM, ITEM), :] = full.astype(BF)
            if target is grad:
                grad_v[pl.ds(i * TEXT_AT, TEXT_AT), :] = full[:TEXT_AT].astype(BF)
                texts.append(text)
                totals[0] = totals[0] + jnp.sum(patch, axis=0, keepdims=True)
                totals[1] = totals[1] + jnp.sum(text, axis=0, keepdims=True)
    slots = jnp.concatenate(texts, axis=0).astype(BF)
    grad_t[...] = slots
    sums[0:1, :] = totals[0]
    sums[1:2, :] = totals[1]
    out_copy[...] = w_out[...]
    down_copy[...] = down[...]
    chip = info[0] // 2
    side = chip % 2
    block = up.shape[0]
    pair = 2 * down.shape[0]
    strip = lambda ref, c: ref[:, pl.ds(pl.multiple_of(c * pair, 128), pair)]
    for k in range(2):
        up_mine[:, k * pair : (k + 1) * pair] = strip(up, side + 2 * k)
        up_other[:, k * pair : (k + 1) * pair] = strip(up, 1 - side + 2 * k)
    strip0[...] = strip(text_up, chip)
    for k, target in ((1, te1), (2, te2), (3, te3)):
        target[pl.ds(0, block), :] = strip(text_up, chip ^ k)
        target[pl.ds(block, slots.shape[0]), :] = slots


def norm_kernel(info, tok, mask, even, odd, *refs):
    n1, vec, up_bias, shards = refs[-4:]
    me = info[0]
    total, width = tok.shape
    block = width // 8
    for slot in range(8):
        shards[me ^ slot] = (even, odd)[slot % 2][slot // 2]
    wide = jnp.concatenate([shards[b] for b in range(8)], axis=1)
    lane = lax.broadcasted_iota(jnp.int32, (1024, width), 0)
    to = lax.broadcasted_iota(jnp.int32, (1024, width), 1)
    spread = ((lane // 128) * block + lane % 128 == to) & (lane % 128 < block)
    vec[...] = dot_nn(wide, jnp.where(spread, 1.0, 0.0).astype(BF))
    hid = up_bias.shape[1] // 4
    for q in range(4):
        b = (q // 2) * 4 + q % 2 + ((me // 2) % 2) * 2
        for r in range(hid // 128):
            at = q * hid + r * 128
            up_bias[0:1, at : at + 128] = shards[b, 10 + r : 11 + r, :].astype(F32)

    @pl.loop(0, total // 64)
    def _(step):
        rows = pl.ds(pl.multiple_of(step * 64, 64), 64)
        normal, _unused = normalize(mixed_in(tok, mask, vec, rows))
        n1[rows, :] = (normal * vec[1:2, :] + vec[2:3, :]).astype(BF)


def qkv_kernel(slots, info, n1, vec, *refs):
    count = len(slots)
    pieces = refs[:count]
    qkv, weight, bias, sems = refs[-4:]
    width = n1.shape[1]
    copies = start_rows([(s, f, r) for (s, f), r in zip(slots, pieces)], weight, info[0], sems)
    bias[0:1, 0:width] = vec[3:4, :]
    bias[0:1, width : 2 * width] = jnp.zeros((1, width), F32)
    bias[0:1, 2 * width : 3 * width] = vec[4:5, :]
    for copy in copies:
        copy.wait()

    @pl.loop(0, 3 * width // 256)
    def _(step):
        cols = pl.ds(pl.multiple_of(step * 256, 256), 256)
        factor = jnp.where(step < width // 256, 0.125, 1.0).astype(F32)
        out = dot_nn(n1[...], weight[:, cols])
        qkv[:, cols] = ((out + bias[0:1, cols]) * factor).astype(BF)


def attn_kernel(info, qkv, *refs):
    probs, ctx = refs[-2:]
    total, width = ctx.shape
    items = total // ITEM
    pairs = width // 128
    patches = info[3]

    @pl.loop(0, items * pairs)
    def _(step):
        item, pair = step // pairs, step % pairs
        rows = pl.ds(pl.multiple_of(item * ITEM, ITEM), ITEM)
        lane = lambda part: pl.ds(pl.multiple_of(part * width + pair * 128, 128), 128)
        q2, k2, v2 = qkv[rows, lane(0)], qkv[rows, lane(1)], qkv[rows, lane(2)]
        low = lax.broadcasted_iota(jnp.int32, (ITEM, 128), 1) < HEAD_DIM
        zero = jnp.zeros_like(q2)
        both = jnp.concatenate([jnp.where(low, q2, zero), jnp.where(low, zero, q2)], axis=0)
        scores = dot_nt(both, k2)
        col = lax.broadcasted_iota(jnp.int32, (1, ITEM), 1)
        valid = (col < patches) | ((col >= TEXT_AT) & (col < TEXT_AT + info[1 + item]))
        scores = jnp.where(valid, scores, -1000000000.0)
        expo = jnp.exp(scores - jnp.max(scores, axis=-1, keepdims=True))
        prob = (expo * (1.0 / jnp.sum(expo, axis=-1, keepdims=True))).astype(BF)
        probs[step] = prob
        wide = jnp.concatenate([prob[:ITEM], prob[ITEM:]], axis=1)
        values = jnp.concatenate([jnp.where(low, v2, zero), jnp.where(low, zero, v2)], axis=0)
        ctx[rows, pl.ds(pl.multiple_of(pair * 128, 128), 128)] = dot_nn(wide, values).astype(BF)


def out_kernel(text_rows, info, tok, mask, vec, ctx, out_w, *refs):
    h1, n2t, *n2v = refs[-2 - tok.shape[0] // ITEM :]
    items = tok.shape[0] // ITEM
    texts = []
    for i in range(items):
        for at, size in ((0, TEXT_AT), (TEXT_AT, ITEM - TEXT_AT)):
            rows = pl.ds(i * ITEM + at, size)
            attended = dot_nn(ctx[rows, :], out_w[...]) + vec[5:6, :]
            hidden = mixed_in(tok, mask, vec, rows) + attended
            h1[rows, :] = hidden
            normal, _unused = normalize(hidden)
            second = normal * vec[6:7, :] + vec[7:8, :]
            if at == 0:
                n2v[i][...] = second.astype(BF)
            else:
                texts.append(second[:text_rows])
    n2t[...] = jnp.concatenate(texts, axis=0).astype(BF)


def pack_kernel(info, strip0, te1, te2, te3, grad_t, pack):
    block, hid = strip0.shape[0], strip0.shape[1] // 2
    rows = grad_t.shape[0]
    other = pl.ds(pl.multiple_of((1 - info[0] % 2) * hid, 128), hid)
    for k, ref in enumerate((strip0, te1, te2, te3)):
        at = (k // 2) * block
        pack[at : at + block, (k % 2) * hid : (k % 2 + 1) * hid] = ref[pl.ds(0, block), other]
        there = pl.ds(2 * block + k * rows, rows)
        pack[there, :] = grad_t[...] if k == 0 else ref[pl.ds(block, rows), :]


def up_rows(me, pieces, target, sems):
    block = target.shape[0] // 8
    copies = []
    for index, (base, ref) in enumerate(pieces):
        for k in range(2):
            row = pl.multiple_of((me ^ (base + 2 * k)) * block, 16)
            sem = sems.at[2 * index + k]
            copies.append(pltpu.make_async_copy(ref.at[k], target.at[pl.ds(row, block)], sem))
    for copy in copies:
        copy.start()
    return copies


def place_of(me):
    return (me // 4) * 2 + me % 2


def vision_kernel(pair, items, info, grad, up_bias, *refs):
    parts, refs = refs[:items], refs[items:]
    ups, downs = refs[:4], refs[4:6]
    branch, gn2, act, low, up_w, down_w, rows_in, sems = refs[-8:]
    me = info[0]
    block = downs[0].shape[1]
    copies = up_rows(me, list(zip((0, 4, 1, 5), ups)), up_w, sems)
    place = place_of(me)
    for j in range(4):
        row = pl.multiple_of((place ^ j) * block, 16)
        copy = pltpu.make_async_copy(downs[j % 2].at[j // 2], down_w.at[pl.ds(row, block)], sems.at[8 + j])
        copy.start()
        copies.append(copy)
    for copy in copies:
        copy.wait()
    mine = grad.at[(me // 2) % 2 ^ 1] if pair else grad
    for i, part in enumerate(parts):
        rows_in[pl.ds(i * TEXT_AT, TEXT_AT), :] = part[...]
    chunk = 512
    for step in range(down_w.shape[0] // chunk):
        cols = slice(step * chunk, (step + 1) * chunk)
        upper = dot_nn(rows_in[...], up_w[:, cols]) + up_bias[0:1, cols]
        active, slope = gelu_parts(upper)
        active = active.astype(BF)
        act[:, cols] = active
        back = (dot_nt(mine[...], down_w[cols, :]) * slope).astype(BF)
        low[:, cols] = back
        if step == 0:
            sum_branch = dot_nn(active, down_w[cols, :])
            sum_gn2 = dot_nt(back, up_w[:, cols])
        else:
            sum_branch = sum_branch + dot_nn(active, down_w[cols, :])
            sum_gn2 = sum_gn2 + dot_nt(back, up_w[:, cols])
    branch[...] = sum_branch.astype(branch.dtype)
    gn2[...] = sum_gn2.astype(gn2.dtype)


def vision_grad_kernel(items, info, *refs):
    ins = refs[:items], refs[items : 2 * items]
    grads, refs = refs[2 * items], refs[2 * items + 1 :]
    acts, lows = refs[:2], refs[2:4]
    up_keep, up_send, down_keep, down_send, bias_sums = refs[-11:-6]
    left_t, act_t, right, low, turn0, turn1 = refs[-6:]
    me = info[0]
    rows, width = items * ins[0][0].shape[0], ins[0][0].shape[1]
    block = width // 8
    half = down_keep.shape[1]
    place, core = place_of(me), me % 2
    for k in range(2):
        at = pl.ds(k * rows, rows)
        right[at, :] = grads[(me // 2) % 2 ^ k]
        low[at, :] = lows[k][...]
        turned = jnp.concatenate([ref[...] for ref in ins[k]], axis=0).T
        turn = (turn0, turn1)[k]
        for b in range(8):
            spot = pl.multiple_of((me ^ b) * block, 16)
            turn[pl.ds(spot, block), :] = turned[b * block : (b + 1) * block]
        left_t[:, at] = turn[...]
        act_t[:, at] = acts[k][...].T
    chunk = 512
    for step in range(4 * half // chunk):
        cols = slice(step * chunk, (step + 1) * chunk)
        grad_up = dot_nn(left_t[...], low[:, cols])
        bias_sums[0:1, cols] = jnp.sum(low[:, cols].astype(F32), axis=0, keepdims=True)
        grad_up = grad_up.astype(BF)
        for b in range(4):
            up_keep[b, :, cols] = grad_up[2 * b * block : (2 * b + 1) * block]
            up_send[b, :, cols] = grad_up[(2 * b + 1) * block : (2 * b + 2) * block]
    for q in range(4):
        grad_down = dot_nn(act_t[q * half : (q + 1) * half, :], right[...]).astype(BF)
        side = (q // 2) ^ (place // 2)

        @pl.when(core == q % 2)
        def _():
            down_keep[side] = grad_down

        @pl.when(core != q % 2)
        def _():
            down_send[side] = grad_down


def text_kernel(info, down, up_bias, strip0, te1, te2, te3, far, even, odd, *refs):
    grad0, refs = refs[0], refs[1:]
    branch_keep, branch_send, gn2_keep, gn2_send, up_keep, up_send, grad_down, bias_sums = refs[-12:-4]
    up_w, left, right, left_t = refs[-4:]
    me = info[0]
    width = down.shape[1]
    hid = down.shape[0]
    block = width // 8
    rows = even.shape[1]
    mine = pl.ds(pl.multiple_of((me % 2) * hid, 128), hid)
    spot = lambda slot: pl.ds(pl.multiple_of((me ^ slot) * block, 16), block)
    up_w[spot(0), :] = strip0[:, mine]
    for s, te in ((2, te1), (4, te2), (6, te3)):
        up_w[spot(s), :] = te[pl.ds(0, block), mine]
        right[pl.ds(s * rows, rows), :] = te[pl.ds(block, rows), :]
    up_w[spot(1), :] = far[pl.ds(0, block), pl.ds(0, hid)]
    up_w[spot(3), :] = far[pl.ds(0, block), pl.ds(hid, hid)]
    up_w[spot(5), :] = far[pl.ds(block, block), pl.ds(0, hid)]
    up_w[spot(7), :] = far[pl.ds(block, block), pl.ds(hid, hid)]
    right[pl.ds(0, rows), :] = grad0[...]
    for k in range(4):
        right[pl.ds((2 * k + 1) * rows, rows), :] = far[pl.ds(2 * block + k * rows, rows), :]
    for slot in range(8):
        left[pl.ds(slot * rows, rows), :] = (even, odd)[slot % 2][slot // 2]
    turned = left[...].T
    for b in range(8):
        left_t[spot(b), :] = turned[b * block : (b + 1) * block]
    upper = dot_nn(left[...], up_w[...]) + up_bias[...]
    active, slope = gelu_parts(upper)
    act = active.astype(BF)
    low = (dot_nt(right[...], down[...]) * slope).astype(BF)
    bias_sums[...] = jnp.sum(low.astype(F32), axis=0, keepdims=True)
    gn2 = dot_nt(low, up_w[...]).astype(BF)
    branch = dot_nn(act, down[...]).astype(BF)
    for s in range(4):
        gn2_keep[s] = gn2[2 * s * rows : (2 * s + 1) * rows]
        gn2_send[s] = gn2[(2 * s + 1) * rows : (2 * s + 2) * rows]
        branch_keep[s] = branch[2 * s * rows : (2 * s + 1) * rows]
        branch_send[s] = branch[(2 * s + 1) * rows : (2 * s + 2) * rows]
    grad_down[...] = dot_tn(act, right[...]).astype(BF)
    grad_up = dot_nn(left_t[...], low).astype(BF)
    for b in range(4):
        up_keep[b] = grad_up[2 * b * block : (2 * b + 1) * block]
        up_send[b] = grad_up[(2 * b + 1) * block : (2 * b + 2) * block]


def attn_bwd_kernel(text_rows, info, gn2v, gn2x, t0, t1, t2, t3, grad, h1, vec, qkv, probs, weight, *refs):
    gh1, low, stacked, sums, gn2, gctx = refs[-6:]
    total, width = h1.shape
    items = total // ITEM
    text = (
        t0[0].astype(F32) + t1[...].astype(F32) + t2[...].astype(F32) + t3[...].astype(F32)
    )
    for i in range(items):
        part = pl.ds(i * TEXT_AT, TEXT_AT)
        gn2[pl.ds(i * ITEM, TEXT_AT), :] = gn2v[part, :] + gn2x[part, :].astype(F32)
        gn2[pl.ds(i * ITEM + TEXT_AT, text_rows), :] = text[i * text_rows : (i + 1) * text_rows]
        pad = ITEM - TEXT_AT - text_rows
        gn2[pl.ds(i * ITEM + TEXT_AT + text_rows, pad), :] = jnp.zeros((pad, width), F32)
    sums[...] = jnp.zeros_like(sums)

    @pl.loop(0, total // 64)
    def _(step):
        rows = pl.ds(pl.multiple_of(step * 64, 64), 64)
        normal, scale = normalize(h1[rows, :])
        above = gn2[rows, :]
        inner = above * vec[6:7, :]
        back = scale * (
            inner
            - jnp.mean(inner, axis=-1, keepdims=True)
            - normal * jnp.mean(inner * normal, axis=-1, keepdims=True)
        )
        out = grad[rows, :].astype(F32)
        hidden = out + back
        gh1[rows, :] = hidden
        low[rows, :] = hidden.astype(BF)
        sums[0:1, :] += jnp.sum(above * normal, axis=0, keepdims=True)
        sums[1:2, :] += jnp.sum(above, axis=0, keepdims=True)
        sums[2:3, :] += jnp.sum(hidden.astype(BF).astype(F32), axis=0, keepdims=True)

    gctx[...] = dot_nt(low[...], weight[...]).astype(BF)
    pairs = width // 128

    @pl.loop(0, items * pairs)
    def _(step):
        item, pair = step // pairs, step % pairs
        rows = pl.ds(pl.multiple_of(item * ITEM, ITEM), ITEM)
        lane = lambda part: pl.ds(pl.multiple_of(part * width + pair * 128, 128), 128)
        q2, k2, v2 = qkv[rows, lane(0)], qkv[rows, lane(1)], qkv[rows, lane(2)]
        g2 = gctx[rows, pl.ds(pl.multiple_of(pair * 128, 128), 128)]
        lower = lax.broadcasted_iota(jnp.int32, (ITEM, 128), 1) < HEAD_DIM
        zero = jnp.zeros_like(q2)
        split = lambda a: jnp.concatenate([jnp.where(lower, a, zero), jnp.where(lower, zero, a)], axis=0)
        both_g = split(g2)
        prob_b = probs[step]
        prob = prob_b.astype(F32)
        gprob = dot_nt(both_g, v2)
        weighted = prob * gprob
        gscore = (weighted - prob * jnp.sum(weighted, axis=-1, keepdims=True)).astype(BF)
        stacked[rows, lane(2)] = dot_tn(prob_b, both_g).astype(BF)
        stacked[rows, lane(1)] = dot_tn(gscore, split(q2)).astype(BF)
        wide = jnp.concatenate([gscore[:ITEM], gscore[ITEM:]], axis=1)
        gquery = dot_nn(wide, split(k2)).astype(BF).astype(F32) * 0.125
        stacked[rows, lane(0)] = gquery.astype(BF)

    for part in (0, 2):
        cols = stacked[:, part * width : (part + 1) * width].astype(F32)
        sums[3 + part // 2 : 4 + part // 2, :] = jnp.sum(cols, axis=0, keepdims=True)


def attn_grad_kernel(last, info, left, *refs):
    me = info[0]
    width = left.shape[1]
    block = width // 8
    keep, send, left_t, other_t, right, sem = refs[-6:]
    others, stacked = (refs[:2], refs[2]) if last else ((), refs[0])
    first = 2 * width if last else 0
    copy = pltpu.make_async_copy(stacked.at[:, pl.ds(first, right.shape[1])], right, sem.at[0])
    copy.start()
    for source, target in ((left, left_t), (others[0], other_t)) if last else ((left, left_t),):
        turned = source[...].T
        for b in range(8):
            place = pl.multiple_of((me ^ b) * block, 16)
            target[pl.ds(place, block), :] = turned[b * block : (b + 1) * block]
    for part in (1, 0) if last else (0, 1):
        cols = slice(part * width, (part + 1) * width)
        if last and part == 1:
            value = dot_nn(other_t[...], others[1][...]).astype(BF)
        else:
            if part == 0:
                copy.wait()
            value = dot_nn(left_t[...], right[:, cols]).astype(BF)
        for b in range(4):
            keep[b, :, cols] = value[2 * b * block : (2 * b + 1) * block]
            send[b, :, cols] = value[(2 * b + 1) * block : (2 * b + 2) * block]


def last_kernel(slots, info, stacked, gh1, tok, mask, vec, *refs):
    count = len(slots)
    pieces = refs[:count]
    gtok, sums, weight, sems = refs[-4:]
    copies = start_rows([(s, f, r) for (s, f), r in zip(slots, pieces)], weight, info[0], sems)
    sums[...] = jnp.zeros_like(sums)
    for copy in copies:
        copy.wait()

    @pl.loop(0, tok.shape[0] // 128)
    def _(step):
        rows = pl.ds(pl.multiple_of(step * 128, 128), 128)
        above = dot_nt(stacked[rows, :], weight[...])
        normal, scale = normalize(mixed_in(tok, mask, vec, rows))
        inner = above * vec[1:2, :]
        back = scale * (
            inner
            - jnp.mean(inner, axis=-1, keepdims=True)
            - normal * jnp.mean(inner * normal, axis=-1, keepdims=True)
        )
        hidden = gh1[rows, :] + back
        keep = mask[rows, :]
        gtok[rows, :] = hidden * (1.0 - keep)
        sums[0:1, :] += jnp.sum(hidden * keep, axis=0, keepdims=True)
        sums[1:2, :] += jnp.sum(above * normal, axis=0, keepdims=True)
        sums[2:3, :] += jnp.sum(above, axis=0, keepdims=True)


def call(kernel, outs, scratch, args, pieces=(), us=1):
    in_specs = [pl.BlockSpec(memory_space=pltpu.SMEM)]
    in_specs += [pl.BlockSpec(memory_space=pltpu.VMEM)] * (len(args) - 1)
    in_specs += [pl.BlockSpec(memory_space=pl.ANY)] * len(pieces)
    return pl.pallas_call(
        kernel,
        out_shape=[jax.ShapeDtypeStruct(s, d) for s, d in outs],
        in_specs=in_specs,
        out_specs=[pl.BlockSpec(memory_space=pltpu.VMEM)] * len(outs),
        scratch_shapes=scratch,
        compiler_params=pltpu.CompilerParams(vmem_limit_bytes=VMEM_LIMIT),
        cost_estimate=pl.CostEstimate(flops=int(us * SCALE * 1.1e9), bytes_accessed=int(us * SCALE * 1e6), transcendentals=0),
    )(*args, *pieces)


def swap(array, mask):
    return lax.ppermute(array, "fsdp", [(i, i ^ mask) for i in range(8)])


def along_rep(array, pairs):
    return lax.ppermute(array, "rep", pairs)


def add(*terms):
    out = terms[0].astype(F32)
    for term in terms[1:]:
        out = out + term.astype(F32)
    return out.astype(BF)


def planned(
    tokens,
    out_grad,
    masked,
    lengths,
    mask_vec,
    norm1_gain,
    norm1_shift,
    w_qkv,
    query_bias,
    value_bias,
    w_out,
    out_bias,
    norm2_gain,
    norm2_shift,
    vision_up,
    vision_up_bias,
    vision_down,
    vision_down_bias,
    text_up,
    text_up_bias,
    text_down,
    text_down_bias,
):
    items, row_count, width = tokens.shape
    text_rows = masked.shape[1]
    patches = row_count - text_rows
    block = width // 8
    half = block // 2
    hid = vision_down.shape[0]
    pair = 2 * hid
    hidden = 8 * hid
    total = items * ITEM
    vision_rows = items * TEXT_AT
    slot_rows = items * text_rows
    te_rows = block + slot_rows
    me = lax.axis_index("fsdp").astype(jnp.int32)
    rep = lax.axis_index("rep").astype(jnp.int32)
    core, chip, side = me % 2, me // 2, (me // 2) % 2
    sem = lambda n: pltpu.SemaphoreType.DMA((n,))
    quad = lambda r, c: ((4, r, c), BF)

    names = (
        mask_vec,
        norm1_gain,
        norm1_shift,
        query_bias,
        value_bias,
        out_bias,
        norm2_gain,
        norm2_shift,
        vision_down_bias,
        text_down_bias,
    )
    own_vec = jnp.pad(jnp.stack(names), ((0, 0), (0, 128 - block)))
    own_vec = jnp.concatenate([own_vec, vision_up_bias.reshape(-1, 128)], axis=0)
    own_vec = jnp.pad(own_vec, ((0, 16 - own_vec.shape[0]), (0, 0)))[None]
    vx, vy, vxy = swap(own_vec, 2), swap(own_vec, 4), swap(own_vec, 6)
    qx, qy = swap(w_qkv, 2), swap(w_qkv, 4)
    mask = jnp.concatenate(
        [
            jnp.zeros((items, TEXT_AT), F32),
            masked.astype(F32),
            jnp.zeros((items, ITEM - TEXT_AT - text_rows), F32),
        ],
        axis=1,
    ).reshape(total, 1)
    info = jnp.concatenate([me[None], lengths, jnp.full((1,), patches, jnp.int32)])
    tok, grad, grad_v, grad_t, grad_sums, own_out, own_down, up_mine, up_other, strip0, te1, te2, te3, t = call(
        functools.partial(prep_kernel, text_rows),
        [
            ((total, width), BF),
            ((total, width), BF),
            ((vision_rows, width), BF),
            ((slot_rows, width), BF),
            ((2, width), F32),
            ((block, width), BF),
            ((hid, width), BF),
            ((block, 2 * pair), BF),
            ((block, 2 * pair), BF),
            ((block, pair), BF),
            ((te_rows, width), BF),
            ((te_rows, width), BF),
            ((te_rows, width), BF),
            ((8, 128), F32),
        ],
        [],
        [info, tokens, out_grad, w_out, vision_down, vision_up, text_up],
        us=5,
    )
    vec_four = gate([jnp.concatenate([own_vec, vx, vy, vxy], axis=0)], [t])[0]
    vec_arrays = [vec_four, swap(vec_four, 1)]
    part1, part2 = gate([qx[:half], qy[half:]], [tok, vec_arrays[1]])

    far1, far2 = swap(part1, 4), swap(part2, 2)
    near = [swap(a, 1) for a in (w_qkv, qx, qy)]
    n1, vec, up_bias = call(
        norm_kernel,
        [((total, width), BF), ((16, width), F32), ((1, 4 * hid), F32)],
        [pltpu.VMEM((8, 16, 128), BF)],
        [info, tok, mask, *vec_arrays],
        [part1],
        us=5,
    )
    far1, far2, up_other, own_down, own_out = gate([far1, far2, up_other, own_down, own_out], [n1, *near])
    out_all = lax.all_gather(own_out, "fsdp", tiled=True)
    pairs = [[0, 2], [1, 3], [4, 6], [5, 7]]
    grad_pair = lax.all_gather(grad_v, "fsdp", axis_index_groups=pairs)
    attn = [(0, 0, w_qkv), (2, 0, qx), (4, 0, qy), (6, 0, far1), (6, half, far2)]
    attn += [(1, 0, near[0]), (3, 0, near[1]), (5, 0, near[2]), (7, 0, swap(far1, 1)), (7, half, swap(far2, 1))]
    attn_slots = tuple((p[0], p[1]) for p in attn)
    attn_arrays = [p[2] for p in attn]

    up_x, down_y = swap(up_other, 2), swap(own_down, 4)
    (qkv,) = call(
        functools.partial(qkv_kernel, attn_slots),
        [((total, 3 * width), BF)],
        [pltpu.VMEM((width, 3 * width), BF), pltpu.VMEM((1, 3 * width), F32), sem(len(attn))],
        [info, n1, vec],
        attn_arrays,
        us=8,
    )
    t = tick(t, [qkv, up_x])

    up_x, te1, te2, te3 = gate([up_x, te1, te2, te3], [t])
    up_two = jnp.stack([up_mine, up_x])
    up_y, up_c = swap(up_two, 4), swap(up_two, 1)
    te1, te3 = swap(te1, 2), swap(te3, 6)
    probs, ctx = call(
        attn_kernel,
        [((items * width // 128, 2 * ITEM, ITEM), BF), ((total, width), BF)],
        [],
        [info, qkv],
        [t],
        us=10,
    )
    t = tick(t, [ctx, up_y, up_c, te1, te3, down_y])

    up_y, te1, te2, te3, down_y = gate([up_y, te1, te2, te3, down_y], [t])
    te2 = swap(te2, 4)
    down_two = jnp.stack([own_down, down_y])
    up_yc, down_c = swap(up_y, 1), swap(down_two, 1)
    h1, n2t, *n2v = call(
        functools.partial(out_kernel, text_rows),
        [((total, width), F32), ((slot_rows, width), BF)] + [((TEXT_AT, width), BF)] * items,
        [],
        [info, tok, mask, vec, ctx, out_all],
        [t],
        us=5,
    )
    t = tick(t, [n2t, te2, up_yc, down_c, grad_pair])

    te1, te2, te3, n2t, *n2v = gate([te1, te2, te3, n2t, *n2v], [t])
    (pack,) = call(
        pack_kernel,
        [((2 * block + 4 * slot_rows, width), BF)],
        [],
        [info, strip0, te1, te2, te3, grad_t],
    )
    text_in = [swap(n2t, 2), swap(n2t, 4), swap(n2t, 6)]
    n2x = [swap(n2v[0], 2)]
    far = swap(pack, 1)
    weights = [up_two, up_y, up_c, up_yc, down_two, down_c]

    def vision(rows_in, grads, kind, after):
        return call(
            functools.partial(vision_kernel, kind == BF, items),
            [
                ((vision_rows, width), kind),
                ((vision_rows, width), kind),
                ((vision_rows, 4 * hid), BF),
                ((vision_rows, 4 * hid), BF),
            ],
            [
                pltpu.VMEM((width, 4 * hid), BF),
                pltpu.VMEM((4 * hid, width), BF),
                pltpu.VMEM((vision_rows, width), BF),
                sem(12),
            ],
            [info, grads, up_bias, *rows_in],
            [*weights, *after],
            us=9,
        )

    branch_own, gn2_own, act_own, low_own = vision(n2v, grad_v, F32, [pack])
    t = tick(t, [gn2_own, *text_in, n2x[0], far])

    far, *text_in = gate([far, *text_in], [t])
    text_four = jnp.stack([n2t, *text_in])
    text_odd = swap(text_four, 1)
    n2x += [swap(a, 2) for a in gate(n2v[1:], [t])]
    branch_keep, branch_send, gn2_keep, gn2_send, tu_keep, tu_send, td, text_bias_sum = call(
        text_kernel,
        [
            quad(slot_rows, width),
            quad(slot_rows, width),
            quad(slot_rows, width),
            quad(slot_rows, width),
            quad(block, hid),
            quad(block, hid),
            ((hid, width), BF),
            ((1, hid), F32),
        ],
        [
            pltpu.VMEM((width, hid), BF),
            pltpu.VMEM((8 * slot_rows, width), BF),
            pltpu.VMEM((8 * slot_rows, width), BF),
            pltpu.VMEM((width, 8 * slot_rows), BF),
        ],
        [
            info,
            text_down,
            text_up_bias.astype(F32).reshape(1, hid),
            strip0,
            te1,
            te2,
            te3,
            far,
            text_four,
            text_odd,
            grad_t,
        ],
        us=6,
    )
    t = tick(t, [gn2_keep, *n2x])
    tu_keep, tu_send, td = lax.psum((tu_keep, tu_send, td), "rep")

    gn2_send, *n2x = gate([gn2_send, *n2x], [t])
    gn2_sum = add(gn2_keep, swap(gn2_send, 1))
    gn2_text = [gn2_sum] + [swap(gn2_sum[s], 2 * s) for s in (1, 2, 3)]
    branch_x, gn2_x, act_x, low_x = vision(n2x, grad_pair, BF, [gn2_sum])
    t = tick(t, [gn2_x, *gn2_text[1:]])

    (gn2_x,) = gate([gn2_x], [t])
    gn2_back = swap(gn2_x, 2)
    vu_keep, vu_send, vd_keep, vd_send, vu_bias_sum = call(
        functools.partial(vision_grad_kernel, items),
        [
            quad(block, 4 * hid),
            quad(block, 4 * hid),
            ((2, hid, width), BF),
            ((2, hid, width), BF),
            ((1, 4 * hid), F32),
        ],
        [
            pltpu.VMEM((width, 2 * vision_rows), BF),
            pltpu.VMEM((4 * hid, 2 * vision_rows), BF),
            pltpu.VMEM((2 * vision_rows, width), BF),
            pltpu.VMEM((2 * vision_rows, 4 * hid), BF),
            pltpu.VMEM((width, vision_rows), BF),
            pltpu.VMEM((width, vision_rows), BF),
        ],
        [info, *n2v, *n2x, grad_pair, act_own, act_x, low_own, low_x],
        [t],
        us=12,
    )
    t = tick(t, [vu_bias_sum, gn2_back])

    vu_send, vd_send, branch_x, branch_send, gn2_back = gate([vu_send, vd_send, branch_x, branch_send, gn2_back], [t])
    vu_got, vd_got = swap(vu_send, 1), swap(vd_send, 1)
    vd_near, vd_far = add(vd_keep[0], vd_got[0]), add(vd_keep[1], vd_got[1])
    vu_far = [add(vu_keep[k], vu_got[k]) for k in (2, 3)]
    vd_y, vu_y1 = swap(vd_far, 4), swap(vu_far[1], 4)
    branch_back = swap(branch_x, 2)
    branch_got = swap(branch_send, 1)
    gh1, low_attn, stacked, sums_two = call(
        functools.partial(attn_bwd_kernel, text_rows),
        [((total, width), F32), ((total, width), BF), ((total, 3 * width), BF), ((8, width), F32)],
        [pltpu.VMEM((total, width), F32), pltpu.VMEM((total, width), BF)],
        [info, gn2_own, gn2_back, *gn2_text, grad, h1, vec, qkv, probs, out_all],
        [vd_far, *vu_far],
        us=18,
    )
    t = tick(t, [stacked, vd_y, vu_y1, branch_back, branch_got])

    vd_y, vu_y1, vu_far0, branch_got = gate([vd_y, vu_y1, vu_far[0], branch_got], [t])
    vd_sum = add(vd_near, vd_y)
    vu_x = swap(add(vu_keep[1], vu_got[1], vu_y1), 2)
    vu_y0 = swap(vu_far0, 4)

    def attn_grads(last, after):
        return call(
            functools.partial(attn_grad_kernel, last),
            [quad(block, 2 * width), quad(block, 2 * width)],
            [
                pltpu.VMEM((width, total), BF),
                pltpu.VMEM((width, total), BF),
                pltpu.VMEM((total, (1 if last else 2) * width), BF),
                sem(1),
            ],
            [info, n1, ctx, low_attn] if last else [info, n1],
            [stacked, *after],
            us=5,
        )

    a_keep, a_send = attn_grads(False, [t])
    t = tick(t, [a_keep, vu_x, vu_y0])
    a_send, vu_x, vu_y0 = gate([a_send, vu_x, vu_y0], [t])
    a_got = swap(a_send, 1)
    branch_sum = add(branch_keep, branch_got)
    vu_both = jnp.stack([add(vu_keep[0], vu_got[0], vu_y0), vu_x])
    vu, vd = lax.psum((vu_both, vd_sum), "rep", axis_index_groups=[[1, 0, 2, 3]])
    b_keep, b_send = attn_grads(True, [t])
    t = tick(t, [b_keep, a_got])
    a_got, b_send, branch_sum = gate([a_got, b_send, branch_sum], [t])
    b_got = swap(b_send, 1)

    def begin(keep, got, one):
        i = one // 2
        return add(jnp.stack([keep[i], keep[3]]), jnp.stack([got[i], got[3]]))

    a_first, b_first = begin(a_keep, a_got, 2), begin(b_keep, b_got, 4)
    a_there, b_there = swap(a_first, 2), swap(b_first, 4)
    gtok, sums_one = call(
        functools.partial(last_kernel, attn_slots),
        [((total, width), F32), ((8, width), F32)],
        [pltpu.VMEM((width, 3 * width), BF), sem(len(attn))],
        [info, stacked, gh1, tok, mask, vec],
        attn_arrays + [a_first, b_first, vu_both, vd_sum],
        us=12,
    )
    t = tick(t, [sums_one, a_there, b_there])

    a_there, b_there = gate([a_there, b_there], [t])
    a_next, b_next = add(a_keep[2], a_got[2], a_there[1]), add(b_keep[1], b_got[1], b_there[1])
    a_beyond, b_beyond = swap(a_next, 4), swap(b_next, 2)
    (sums_one,) = gate([sums_one], [tick(t, [a_next, b_next])])
    vu_sum = vu_bias_sum.reshape(2, 1, pair)
    vu_sum = jnp.where(
        side == 0,
        jnp.concatenate([vu_sum, jnp.zeros_like(vu_sum)], axis=1),
        jnp.concatenate([jnp.zeros_like(vu_sum), vu_sum], axis=1),
    )
    count, rows = len(names), hid // block
    vec_rows = count + 2 * rows
    vu_sum = vu_sum.reshape(8, rows, block).transpose(1, 0, 2).reshape(-1, width)
    flat = jnp.concatenate(
        [sums_one[0:3], sums_two[3:5], sums_two[2:3], sums_two[0:2], grad_sums, vu_sum], axis=0
    )
    for m in (1, 2, 4):
        flat = flat + swap(flat, m)
    own_sums = lax.dynamic_slice_in_dim(flat, me * block, block, axis=1)
    own_sums = jnp.concatenate([own_sums, text_bias_sum.reshape(-1, block)], axis=0)
    ga = add(a_keep[0], a_got[0], a_there[0], a_beyond)
    gb = add(b_keep[0], b_got[0], b_there[0], b_beyond)

    inner = (rep == 1) | (rep == 2)

    def rep_sum(array):
        part = add(array, along_rep(array, [(0, 1), (3, 2)]))
        whole = add(part, along_rep(part, [(1, 2), (2, 1)]))
        return jnp.where(inner, whole, along_rep(whole, [(1, 0), (2, 3)]))

    plane_sums = [ga, gb]
    own_sums = own_sums.reshape(-1)
    own_sums = jnp.pad(own_sums, (0, 8 * 2 * width - own_sums.shape[0])).reshape(8, 2 * width)
    ga, gb = rep_sum(jnp.concatenate([ga, own_sums.astype(BF)], axis=0)), rep_sum(gb)
    last_sums = [ga, gb]
    tu_keep, tu_send, td, branch_sum, branch_back = gate([tu_keep, tu_send, td, branch_sum, branch_back], plane_sums)
    branch_t = [branch_sum] + [swap(branch_sum[s], 2 * s) for s in (1, 2, 3)]
    tu_got = swap(tu_send, 1)
    tu_wide = jnp.where(
        core == 0,
        jnp.concatenate([tu_keep, tu_got], axis=-1),
        jnp.concatenate([tu_got, tu_keep], axis=-1),
    )
    tu_all = [tu_wide[0]] + [swap(tu_wide[s], 2 * s) for s in (1, 2, 3)]
    tu_x = [jnp.where(side == 0, tu_all[k], tu_all[k ^ 1]) for k in range(4)]
    tu_y = [jnp.where(me // 4 == 0, tu_x[k], tu_x[k ^ 2]) for k in range(4)]
    grad_text_up = jnp.concatenate(tu_y, axis=1).astype(F32)
    grad_text_down = td.astype(F32)

    ga = ga.astype(F32)
    mine = ga[block:].reshape(-1)[: vec_rows * block].reshape(vec_rows, block)
    ga = ga[:block]
    vec_grad = [mine[i] for i in range(count)]
    vu_bias_grad = mine[count : count + rows].reshape(-1)
    tu_bias_grad = mine[count + rows : count + 2 * rows].reshape(-1)

    vu, vd = gate([vu, vd], last_sums)
    gb = gb.astype(F32)
    grad_w_qkv = jnp.concatenate([ga, gb[:, :width]], axis=1)
    grad_w_out = gb[:, width:]
    vu_s = [jnp.where(side == 0, vu[k], vu[1 - k]) for k in range(2)]
    grad_vision_up = jnp.concatenate(
        [vu_s[0][:, :pair], vu_s[1][:, :pair], vu_s[0][:, pair:], vu_s[1][:, pair:]], axis=1
    ).astype(F32)
    grad_vision_down = vd.astype(F32)
    h1 = h1.reshape(items, ITEM, width)
    branch_v = (branch_own + branch_back.astype(F32)).reshape(items, TEXT_AT, width)[:, :patches]
    mixed_v = h1[:, :patches] + branch_v + vec[8][None, None]
    branch_t = branch_t[0][0].astype(F32) + sum(b.astype(F32) for b in branch_t[1:])
    branch_t = branch_t.reshape(items, text_rows, width)
    mixed_t = h1[:, TEXT_AT : TEXT_AT + text_rows] + branch_t + vec[9][None, None]
    mixed = jnp.concatenate([mixed_v.astype(BF), mixed_t.astype(BF)], axis=1)
    gtok = gtok.reshape(items, ITEM, width)
    grad_tokens = jnp.concatenate(
        [gtok[:, :patches], gtok[:, TEXT_AT : TEXT_AT + text_rows]], axis=1
    )
    return (
        mixed,
        grad_tokens,
        vec_grad[0],
        vec_grad[1],
        vec_grad[2],
        grad_w_qkv,
        vec_grad[3],
        vec_grad[4],
        grad_w_out,
        vec_grad[5],
        vec_grad[6],
        vec_grad[7],
        grad_vision_up,
        vu_bias_grad,
        grad_vision_down,
        vec_grad[8],
        grad_text_up,
        tu_bias_grad,
        grad_text_down,
        vec_grad[9],
    )


def layer_norm(hidden, gain, shift):
    center = hidden - jnp.mean(hidden, axis=-1, keepdims=True)
    spread = jnp.mean(center * center, axis=-1, keepdims=True)
    return center * lax.rsqrt(spread + epsilon) * gain + shift


def exact_gelu(values):
    return jax.nn.gelu(values, approximate=False)


def expert_forward(rows_in, up_matrix, up_shift, down_matrix, down_shift):
    upper = jnp.dot(rows_in, up_matrix, preferred_element_type=jnp.float32) + up_shift.astype(
        jnp.float32
    )
    active, gelu_pull = jax.vjp(exact_gelu, upper)
    active_b = active.astype(jnp.bfloat16)
    result = jnp.dot(active_b, down_matrix, preferred_element_type=jnp.float32) + down_shift.astype(
        jnp.float32
    )
    return (result, active_b, gelu_pull)


def expert_backward(rows_in, active_b, gelu_pull, up_matrix, down_matrix, grad_b):
    grad_down = jnp.einsum("rf,rd->fd", active_b, grad_b, preferred_element_type=jnp.float32)
    grad_down_shift = jnp.sum(grad_b.astype(jnp.float32), axis=0)
    grad_active = jnp.einsum("rd,fd->rf", grad_b, down_matrix, preferred_element_type=jnp.float32)
    (grad_upper,) = gelu_pull(grad_active)
    upper_b = grad_upper.astype(jnp.bfloat16)
    grad_up = jnp.einsum("rd,rf->df", rows_in, upper_b, preferred_element_type=jnp.float32)
    grad_up_shift = jnp.sum(upper_b.astype(jnp.float32), axis=0)
    grad_rows = jnp.einsum("rf,df->rd", upper_b, up_matrix, preferred_element_type=jnp.float32)
    return (grad_up, grad_up_shift, grad_down, grad_down_shift, grad_rows)


def general(
    tokens,
    out_grad,
    masked,
    lengths,
    mask_vec,
    norm1_gain,
    norm1_shift,
    w_qkv,
    query_bias,
    value_bias,
    w_out,
    out_bias,
    norm2_gain,
    norm2_shift,
    vision_up,
    vision_up_bias,
    vision_down,
    vision_down_bias,
    text_up,
    text_up_bias,
    text_down,
    text_down_bias,
):
    item_count, row_count, model_width = tokens.shape
    slot_count = masked.shape[1]
    patches = row_count - slot_count
    head_count = model_width // HEAD_DIM
    split_shape = (item_count, row_count, head_count, HEAD_DIM)

    def fetch_attention():
        return (
            lax.all_gather(mask_vec, "fsdp", axis=0, tiled=True),
            lax.all_gather(norm1_gain, "fsdp", axis=0, tiled=True),
            lax.all_gather(norm1_shift, "fsdp", axis=0, tiled=True),
            lax.all_gather(w_qkv, "fsdp", axis=0, tiled=True),
            lax.all_gather(query_bias, "fsdp", axis=0, tiled=True),
            lax.all_gather(value_bias, "fsdp", axis=0, tiled=True),
            lax.all_gather(w_out, "fsdp", axis=0, tiled=True),
            lax.all_gather(out_bias, "fsdp", axis=0, tiled=True),
        )

    def fetch_feedforward():
        return (
            lax.all_gather(norm2_gain, "fsdp", axis=0, tiled=True),
            lax.all_gather(norm2_shift, "fsdp", axis=0, tiled=True),
            lax.all_gather(vision_up, "fsdp", axis=0, tiled=True),
            lax.all_gather(vision_up_bias, "fsdp", axis=0, tiled=True),
            lax.all_gather(vision_down, "fsdp", axis=0, tiled=True),
            lax.all_gather(vision_down_bias, "fsdp", axis=0, tiled=True),
            lax.all_gather(text_up, "fsdp", axis=0, tiled=True),
            lax.all_gather(text_up_bias, "fsdp", axis=0, tiled=True),
            lax.all_gather(text_down, "fsdp", axis=0, tiled=True),
            lax.all_gather(text_down_bias, "fsdp", axis=0, tiled=True),
        )

    attn_full = fetch_attention()
    full_mask, gain_one, shift_one, qkv_matrix, query_shift, value_shift, out_matrix, out_shift = (
        attn_full
    )
    mask_rows = jnp.concatenate(
        [jnp.zeros((item_count, patches), jnp.float32), masked.astype(jnp.float32)], axis=1
    )[:, :, None]
    hidden0 = mask_rows * full_mask.astype(jnp.float32) + (1.0 - mask_rows) * tokens.astype(
        jnp.float32
    )
    normed1, first_pull = jax.vjp(
        layer_norm, hidden0, gain_one.astype(jnp.float32), shift_one.astype(jnp.float32)
    )
    first_in = normed1.astype(jnp.bfloat16).reshape(item_count * row_count, model_width)
    projected = jnp.dot(first_in, qkv_matrix, preferred_element_type=jnp.float32)
    query_b = (
        ((projected[:, :model_width] + query_shift.astype(jnp.float32)) * 0.125)
        .astype(jnp.bfloat16)
        .reshape(split_shape)
    )
    key_b = projected[:, model_width : 2 * model_width].astype(jnp.bfloat16).reshape(split_shape)
    value_b = (
        (projected[:, 2 * model_width :] + value_shift.astype(jnp.float32))
        .astype(jnp.bfloat16)
        .reshape(split_shape)
    )
    key_index = jnp.arange(row_count, dtype=jnp.int32)
    valid_keys = (key_index[None, :] < patches + lengths[:, None])[:, None, None, :]

    def scores_of():
        raw_scores = jnp.einsum(
            "iqhd,ikhd->ihqk", query_b, key_b, preferred_element_type=jnp.float32
        )
        return jnp.where(valid_keys, raw_scores, -1000000000.0)

    scores = scores_of()
    top_score = jnp.max(scores, axis=-1, keepdims=True)
    expo = jnp.exp(scores - top_score)
    totals = jnp.sum(expo, axis=-1, keepdims=True)
    probs = expo / totals
    log_total = top_score + jnp.log(totals)
    context = jnp.einsum(
        "ihqk,ikhd->iqhd", probs.astype(jnp.bfloat16), value_b, preferred_element_type=jnp.float32
    )
    context_b = context.reshape(item_count * row_count, model_width).astype(jnp.bfloat16)
    attended = jnp.dot(
        context_b, out_matrix, preferred_element_type=jnp.float32
    ) + out_shift.astype(jnp.float32)
    hidden1 = hidden0 + attended.reshape(item_count, row_count, model_width)
    ffn_full = fetch_feedforward()
    (
        gain_two,
        shift_two,
        vision_upm,
        vision_upb,
        vision_downm,
        vision_downb,
        text_upm,
        text_upb,
        text_downm,
        text_downb,
    ) = ffn_full
    normed2, second_pull = jax.vjp(
        layer_norm, hidden1, gain_two.astype(jnp.float32), shift_two.astype(jnp.float32)
    )
    second_in = normed2.astype(jnp.bfloat16)
    patch_in = second_in[:, :patches].reshape(-1, model_width)
    text_in = second_in[:, patches:].reshape(-1, model_width)
    vision_out, vision_act, vision_pull = expert_forward(
        patch_in, vision_upm, vision_upb, vision_downm, vision_downb
    )
    text_out, text_act, text_pull = expert_forward(
        text_in, text_upm, text_upb, text_downm, text_downb
    )
    mixed = hidden1 + jnp.concatenate(
        [
            vision_out.reshape(item_count, patches, model_width),
            text_out.reshape(item_count, slot_count, model_width),
        ],
        axis=1,
    )
    cotangent = out_grad.astype(jnp.float32)
    branch_b = cotangent.astype(jnp.bfloat16)
    ffn_back = fetch_feedforward()
    vision_grads = expert_backward(
        patch_in,
        vision_act,
        vision_pull,
        ffn_back[2],
        ffn_back[4],
        branch_b[:, :patches].reshape(-1, model_width),
    )
    text_grads = expert_backward(
        text_in,
        text_act,
        text_pull,
        ffn_back[6],
        ffn_back[8],
        branch_b[:, patches:].reshape(-1, model_width),
    )
    grad_normed2 = jnp.concatenate(
        [
            vision_grads[4].reshape(item_count, patches, model_width),
            text_grads[4].reshape(item_count, slot_count, model_width),
        ],
        axis=1,
    )
    grad_hidden1_norm, grad_gain_two, grad_shift_two = second_pull(grad_normed2)
    grad_hidden1 = cotangent + grad_hidden1_norm
    attn_back = fetch_attention()
    grad_attn_b = grad_hidden1.reshape(-1, model_width).astype(jnp.bfloat16)
    grad_out_matrix = jnp.einsum(
        "rd,re->de", context_b, grad_attn_b, preferred_element_type=jnp.float32
    )
    grad_out_shift = jnp.sum(grad_attn_b.astype(jnp.float32), axis=0)
    grad_context = jnp.einsum(
        "re,de->rd", grad_attn_b, attn_back[6], preferred_element_type=jnp.float32
    )
    grad_context_b = grad_context.astype(jnp.bfloat16).reshape(split_shape)
    again_probs = jnp.exp(scores_of() - log_total)
    grad_probs = jnp.einsum(
        "iqhd,ikhd->ihqk", grad_context_b, value_b, preferred_element_type=jnp.float32
    )
    grad_value = jnp.einsum(
        "ihqk,iqhd->ikhd",
        again_probs.astype(jnp.bfloat16),
        grad_context_b,
        preferred_element_type=jnp.float32,
    )
    row_inner = jnp.sum(again_probs * grad_probs, axis=-1, keepdims=True)
    grad_scores_b = (again_probs * (grad_probs - row_inner)).astype(jnp.bfloat16)
    grad_query = jnp.einsum(
        "ihqk,ikhd->iqhd", grad_scores_b, key_b, preferred_element_type=jnp.float32
    )
    grad_key = jnp.einsum(
        "ihqk,iqhd->ikhd", grad_scores_b, query_b, preferred_element_type=jnp.float32
    )
    grad_query_b = grad_query.astype(jnp.bfloat16) * jnp.bfloat16(0.125)
    stacked = jnp.concatenate(
        [
            grad_query_b.reshape(-1, model_width),
            grad_key.astype(jnp.bfloat16).reshape(-1, model_width),
            grad_value.astype(jnp.bfloat16).reshape(-1, model_width),
        ],
        axis=1,
    )
    grad_qkv = jnp.einsum("rd,re->de", first_in, stacked, preferred_element_type=jnp.float32)
    grad_query_shift = jnp.sum(stacked[:, :model_width].astype(jnp.float32), axis=0)
    grad_value_shift = jnp.sum(stacked[:, 2 * model_width :].astype(jnp.float32), axis=0)
    grad_normed1 = jnp.einsum(
        "re,de->rd", stacked, attn_back[3], preferred_element_type=jnp.float32
    )
    grad_hidden0_norm, grad_gain_one, grad_shift_one = first_pull(
        grad_normed1.reshape(item_count, row_count, model_width)
    )
    grad_hidden0 = grad_hidden1 + grad_hidden0_norm
    grad_tokens = grad_hidden0 * (1.0 - mask_rows)
    grad_mask = jnp.sum(grad_hidden0 * mask_rows, axis=(0, 1))
    ffn_share = (
        lax.psum_scatter(grad_gain_two, "fsdp", scatter_dimension=0, tiled=True),
        lax.psum_scatter(grad_shift_two, "fsdp", scatter_dimension=0, tiled=True),
        lax.psum_scatter(vision_grads[0], "fsdp", scatter_dimension=0, tiled=True),
        lax.psum_scatter(vision_grads[1], "fsdp", scatter_dimension=0, tiled=True),
        lax.psum_scatter(vision_grads[2], "fsdp", scatter_dimension=0, tiled=True),
        lax.psum_scatter(vision_grads[3], "fsdp", scatter_dimension=0, tiled=True),
        lax.psum_scatter(text_grads[0], "fsdp", scatter_dimension=0, tiled=True),
        lax.psum_scatter(text_grads[1], "fsdp", scatter_dimension=0, tiled=True),
        lax.psum_scatter(text_grads[2], "fsdp", scatter_dimension=0, tiled=True),
        lax.psum_scatter(text_grads[3], "fsdp", scatter_dimension=0, tiled=True),
    )
    attn_share = (
        lax.psum_scatter(grad_mask, "fsdp", scatter_dimension=0, tiled=True),
        lax.psum_scatter(grad_gain_one, "fsdp", scatter_dimension=0, tiled=True),
        lax.psum_scatter(grad_shift_one, "fsdp", scatter_dimension=0, tiled=True),
        lax.psum_scatter(grad_qkv, "fsdp", scatter_dimension=0, tiled=True),
        lax.psum_scatter(grad_query_shift, "fsdp", scatter_dimension=0, tiled=True),
        lax.psum_scatter(grad_value_shift, "fsdp", scatter_dimension=0, tiled=True),
        lax.psum_scatter(grad_out_matrix, "fsdp", scatter_dimension=0, tiled=True),
        lax.psum_scatter(grad_out_shift, "fsdp", scatter_dimension=0, tiled=True),
    )
    quarter = (
        lax.psum_scatter(
            attn_share[0].astype(jnp.bfloat16), "rep", scatter_dimension=0, tiled=True
        ).astype(jnp.float32),
        lax.psum_scatter(
            attn_share[1].astype(jnp.bfloat16), "rep", scatter_dimension=0, tiled=True
        ).astype(jnp.float32),
        lax.psum_scatter(
            attn_share[2].astype(jnp.bfloat16), "rep", scatter_dimension=0, tiled=True
        ).astype(jnp.float32),
        lax.psum_scatter(
            attn_share[3].astype(jnp.bfloat16), "rep", scatter_dimension=0, tiled=True
        ).astype(jnp.float32),
        lax.psum_scatter(
            attn_share[4].astype(jnp.bfloat16), "rep", scatter_dimension=0, tiled=True
        ).astype(jnp.float32),
        lax.psum_scatter(
            attn_share[5].astype(jnp.bfloat16), "rep", scatter_dimension=0, tiled=True
        ).astype(jnp.float32),
        lax.psum_scatter(
            attn_share[6].astype(jnp.bfloat16), "rep", scatter_dimension=0, tiled=True
        ).astype(jnp.float32),
        lax.psum_scatter(
            attn_share[7].astype(jnp.bfloat16), "rep", scatter_dimension=0, tiled=True
        ).astype(jnp.float32),
        lax.psum_scatter(
            ffn_share[0].astype(jnp.bfloat16), "rep", scatter_dimension=0, tiled=True
        ).astype(jnp.float32),
        lax.psum_scatter(
            ffn_share[1].astype(jnp.bfloat16), "rep", scatter_dimension=0, tiled=True
        ).astype(jnp.float32),
        lax.psum_scatter(
            ffn_share[2].astype(jnp.bfloat16), "rep", scatter_dimension=0, tiled=True
        ).astype(jnp.float32),
        lax.psum_scatter(
            ffn_share[3].astype(jnp.bfloat16), "rep", scatter_dimension=0, tiled=True
        ).astype(jnp.float32),
        lax.psum_scatter(
            ffn_share[4].astype(jnp.bfloat16), "rep", scatter_dimension=0, tiled=True
        ).astype(jnp.float32),
        lax.psum_scatter(
            ffn_share[5].astype(jnp.bfloat16), "rep", scatter_dimension=0, tiled=True
        ).astype(jnp.float32),
        lax.psum_scatter(
            ffn_share[6].astype(jnp.bfloat16), "rep", scatter_dimension=0, tiled=True
        ).astype(jnp.float32),
        lax.psum_scatter(
            ffn_share[7].astype(jnp.bfloat16), "rep", scatter_dimension=0, tiled=True
        ).astype(jnp.float32),
        lax.psum_scatter(
            ffn_share[8].astype(jnp.bfloat16), "rep", scatter_dimension=0, tiled=True
        ).astype(jnp.float32),
        lax.psum_scatter(
            ffn_share[9].astype(jnp.bfloat16), "rep", scatter_dimension=0, tiled=True
        ).astype(jnp.float32),
    )
    summed = (
        lax.all_gather(quarter[0].astype(jnp.bfloat16), "rep", axis=0, tiled=True).astype(
            jnp.float32
        ),
        lax.all_gather(quarter[1].astype(jnp.bfloat16), "rep", axis=0, tiled=True).astype(
            jnp.float32
        ),
        lax.all_gather(quarter[2].astype(jnp.bfloat16), "rep", axis=0, tiled=True).astype(
            jnp.float32
        ),
        lax.all_gather(quarter[3].astype(jnp.bfloat16), "rep", axis=0, tiled=True).astype(
            jnp.float32
        ),
        lax.all_gather(quarter[4].astype(jnp.bfloat16), "rep", axis=0, tiled=True).astype(
            jnp.float32
        ),
        lax.all_gather(quarter[5].astype(jnp.bfloat16), "rep", axis=0, tiled=True).astype(
            jnp.float32
        ),
        lax.all_gather(quarter[6].astype(jnp.bfloat16), "rep", axis=0, tiled=True).astype(
            jnp.float32
        ),
        lax.all_gather(quarter[7].astype(jnp.bfloat16), "rep", axis=0, tiled=True).astype(
            jnp.float32
        ),
        lax.all_gather(quarter[8].astype(jnp.bfloat16), "rep", axis=0, tiled=True).astype(
            jnp.float32
        ),
        lax.all_gather(quarter[9].astype(jnp.bfloat16), "rep", axis=0, tiled=True).astype(
            jnp.float32
        ),
        lax.all_gather(quarter[10].astype(jnp.bfloat16), "rep", axis=0, tiled=True).astype(
            jnp.float32
        ),
        lax.all_gather(quarter[11].astype(jnp.bfloat16), "rep", axis=0, tiled=True).astype(
            jnp.float32
        ),
        lax.all_gather(quarter[12].astype(jnp.bfloat16), "rep", axis=0, tiled=True).astype(
            jnp.float32
        ),
        lax.all_gather(quarter[13].astype(jnp.bfloat16), "rep", axis=0, tiled=True).astype(
            jnp.float32
        ),
        lax.all_gather(quarter[14].astype(jnp.bfloat16), "rep", axis=0, tiled=True).astype(
            jnp.float32
        ),
        lax.all_gather(quarter[15].astype(jnp.bfloat16), "rep", axis=0, tiled=True).astype(
            jnp.float32
        ),
        lax.all_gather(quarter[16].astype(jnp.bfloat16), "rep", axis=0, tiled=True).astype(
            jnp.float32
        ),
        lax.all_gather(quarter[17].astype(jnp.bfloat16), "rep", axis=0, tiled=True).astype(
            jnp.float32
        ),
    )
    return (
        mixed.astype(jnp.bfloat16),
        grad_tokens,
        summed[0],
        summed[1],
        summed[2],
        summed[3],
        summed[4],
        summed[5],
        summed[6],
        summed[7],
        summed[8],
        summed[9],
        summed[10],
        summed[11],
        summed[12],
        summed[13],
        summed[14],
        summed[15],
        summed[16],
        summed[17],
    )


def solution(mesh):
    if mesh.shape["fsdp"] == 8 and mesh.shape["rep"] == 4:
        body = planned
    else:
        body = general
    return jax.shard_map(
        body,
        mesh=mesh,
        in_specs=(
            P(("fsdp", "rep"), None, None),
            P(("fsdp", "rep"), None, None),
            P(("fsdp", "rep"), None),
            P(("fsdp", "rep")),
            P("fsdp"),
            P("fsdp"),
            P("fsdp"),
            P("fsdp", None),
            P("fsdp"),
            P("fsdp"),
            P("fsdp", None),
            P("fsdp"),
            P("fsdp"),
            P("fsdp"),
            P("fsdp", None),
            P("fsdp"),
            P("fsdp", None),
            P("fsdp"),
            P("fsdp", None),
            P("fsdp"),
            P("fsdp", None),
            P("fsdp"),
        ),
        out_specs=(
            P(("fsdp", "rep"), None, None),
            P(("fsdp", "rep"), None, None),
            P("fsdp"),
            P("fsdp"),
            P("fsdp"),
            P("fsdp", None),
            P("fsdp"),
            P("fsdp"),
            P("fsdp", None),
            P("fsdp"),
            P("fsdp"),
            P("fsdp"),
            P("fsdp", None),
            P("fsdp"),
            P("fsdp", None),
            P("fsdp"),
            P("fsdp", None),
            P("fsdp"),
            P("fsdp", None),
            P("fsdp"),
        ),
        check_vma=False,
    )
```
